128 devices in a mesh: leaf: 32 (over x, y, core), rep: 4 (over z).
Axes of the slice: x: 4, y: 4, z: 4, core: 2. Of those that a mesh axis runs over, the one named last changes fastest.
Arguments:
- fine_coeffs: float32 [8000, 32768], P(None, ('leaf', 'rep')), may hold values from -6 to 6
- set_counts: int32 [128], P(('leaf', 'rep')), may hold values from 64 to 256, as said below
- route_first: int32 [32768], P(('leaf', 'rep')), may hold values from 0 to 255, as said below
- route_top: int32 [4096], P(('leaf', 'rep')), may hold values from 0 to 63, as said below
- level_gain: float32 [3, 7000], replicated, may hold values from 0.1 to 1
Outputs:
- smoothed: float32 [8000, 32768], P(None, ('leaf', 'rep'))
- coarse: float32 [1000, 1024], P(None, ('leaf', 'rep'))
The draws below stay inside these ranges and needn't reach their ends.
Inputs may be any that keep to these rules, and one draw needn't show every extreme that they name: A device's live finest sets are its first set_counts entries; some device has all 256 live. For a live set, route_first // 2 is the device owning its parent and route_first % 2 the slot that owner keeps for this device; live sets of one device have distinct values. Entries of sets that are not live lie in the same range and mean nothing. Some device fills all 2 slots of some owner. route_top // 2 is the leaf index of the parent's owner, which has the same rep index as the set; route_top % 2 is the slot that owner keeps for this device; values of one device are distinct. Some device fills all 2 slots of some owner.
All inputs are finite; a program needn't handle non-finite values.
Results may differ from the reference program's by a relative error of at most 0.0001.
Values sent between devices are 32-bit elements; how exact they have to be, the bound alone decides.
A program may use at most 192 MiB of HBM per device.

```python
import math
import jax
import jax.numpy as jnp
import numpy as np
from jax import lax

POLY_ORDER = 10
LEVELS = 3
SETS_DEV = 256
SLOTS_FIRST = 2
SETS_MID = 32
SLOTS_TOP = 2
FINE_SETS = 32768
N_LEAF = 32
N_REP = 4


def first_tree(key):
    key = jax.random.fold_in(key, 101)
    key_counts, key_full, key_scores, key_start = jax.random.split(key, 4)
    devices = N_LEAF * N_REP
    counts = jax.random.randint(key_counts, (devices,), SETS_DEV // 4, SETS_DEV + 1)
    full_device = jax.random.randint(key_full, (), 0, devices)
    counts = counts.at[full_device].set(SETS_DEV)
    groups = SETS_DEV // SLOTS_FIRST
    start_owner = jax.random.randint(key_start, (devices,), 0, devices)
    start_owner = start_owner.at[full_device].set((devices - groups) % devices)
    slot_index = lax.broadcasted_iota(jnp.int32, (devices, SETS_DEV), 1)
    scores = jax.random.randint(key_scores, (devices, SETS_DEV), 0, 1 << 20)
    keyed = jnp.where(slot_index < counts[:, None], scores, (1 << 21) + slot_index)
    ordering = jnp.argsort(keyed, axis=1, stable=True)
    ranking = jnp.argsort(ordering, axis=1, stable=True).astype(jnp.int32)
    owners = (start_owner[:, None] + ranking // SLOTS_FIRST) % devices
    codes = owners * SLOTS_FIRST + ranking % SLOTS_FIRST
    return (counts.astype(jnp.int32), codes.reshape(-1).astype(jnp.int32))


def draw_set_counts(key, part):
    counts, codes = first_tree(key)
    return counts


def draw_route_first(key, part):
    counts, codes = first_tree(key)
    return codes


def draw_route_top(key, part):
    key = jax.random.fold_in(key, 202)
    key_pick, key_scores, key_start = jax.random.split(key, 3)
    devices = N_LEAF * N_REP
    groups = SETS_MID // SLOTS_TOP
    pinned = jax.random.randint(key_pick, (), 0, devices)
    start_owner = jax.random.randint(key_start, (devices,), 0, N_LEAF)
    start_owner = start_owner.at[pinned].set((N_LEAF - groups) % N_LEAF)
    scores = jax.random.randint(key_scores, (devices, SETS_MID), 0, 1 << 20)
    ordering = jnp.argsort(scores, axis=1, stable=True)
    ranking = jnp.argsort(ordering, axis=1, stable=True).astype(jnp.int32)
    owners = (start_owner[:, None] + ranking // SLOTS_TOP) % N_LEAF
    codes = owners * SLOTS_TOP + ranking % SLOTS_TOP
    return codes.reshape(-1).astype(jnp.int32)


def block_levels(key, dims, cuts, least, top_value):
    factor_of, own = 1.0, jax.random.fold_in(key, 6)
    for dim, parts in cuts:
        heights = jnp.exp(jax.random.uniform(jax.random.fold_in(own, dim), (parts,), jnp.float32, least / len(cuts), top_value / len(cuts)))
        factor_of = factor_of * jnp.repeat(heights, dims[dim] // parts).reshape([-1 if axis == dim else 1 for axis in range(len(dims))])
    return factor_of


def noise(own_key, extent, width, reach, cuts=(), dtype=jnp.bfloat16):
    values = width * jax.random.normal(own_key, extent, jnp.float32)
    if cuts:
        values = values * block_levels(own_key, extent, cuts, -0.22, 0.18)
    return jnp.clip(values, -reach, reach).astype(dtype)


def setup_inputs(seed: int = 0) -> dict:
    streams_of = jax.random.split(jax.random.key(seed), 6)
    fine_coeffs = noise(streams_of[0], (8 * POLY_ORDER ** 3, FINE_SETS), 1.0, 6.0, ((1, 128),), jnp.float32)
    set_counts = draw_set_counts(jax.random.fold_in(streams_of[5], 71), 0)
    route_first = draw_route_first(jax.random.fold_in(streams_of[5], 71), 0)
    route_top = draw_route_top(jax.random.fold_in(streams_of[5], 71), 0)
    level_gain = jnp.clip(jnp.exp(jax.random.uniform(streams_of[4], (LEVELS, 7 * POLY_ORDER ** 3), jnp.float32, math.log(0.1), math.log(1.0))), 0.1, 1.0)
    return dict(fine_coeffs=fine_coeffs, set_counts=set_counts, route_first=route_first, route_top=route_top, level_gain=level_gain)


FULL_PRECISION = lax.Precision.HIGHEST

def legendre_pair(count, position):
    before, current = (1.0, position)
    for degree in range(1, count):
        before, current = (current, ((2 * degree + 1) * position * current - degree * before) / (degree + 1))
    derivative = count * (position * current - before) / (position * position - 1.0)
    return (current, derivative)

def gauss_points(count):
    nodes = []
    weights = []
    for node_index in range(count):
        estimate = math.cos(math.pi * (node_index + 0.75) / (count + 0.5))
        for newton_step in range(100):
            current, derivative = legendre_pair(count, estimate)
            estimate = estimate - current / derivative
        current, derivative = legendre_pair(count, estimate)
        nodes.append(estimate)
        weights.append(2.0 / ((1.0 - estimate * estimate) * derivative * derivative))
    return (np.array(nodes), np.array(weights))

def legendre_rows(degree_count, points):
    values = [points * 0.0 + 1.0, points.copy()]
    for degree in range(1, degree_count - 1):
        values.append(((2 * degree + 1) * points * values[degree] - degree * values[degree - 1]) / (degree + 1))
    return np.stack([np.sqrt(2.0 * degree + 1.0) * values[degree] for degree in range(degree_count)])

def two_scale(poly_order):
    points, weights = gauss_points(2 * poly_order)
    lower_half = (points + 1.0) / 4.0
    half_weights = weights / 4.0
    child_rows = legendre_rows(poly_order, 4.0 * lower_half - 1.0)
    parent_low = legendre_rows(poly_order, 2.0 * lower_half - 1.0)
    parent_high = legendre_rows(poly_order, 2.0 * (lower_half + 0.5) - 1.0)
    filter_left = math.sqrt(2.0) * (parent_low * half_weights) @ child_rows.T
    filter_right = math.sqrt(2.0) * (parent_high * half_weights) @ child_rows.T
    basis_rows = list(np.concatenate([filter_left, filter_right], axis=1))
    units = np.eye(2 * poly_order)
    for step_index in range(poly_order):
        residuals = []
        for vector in units:
            for sweep in range(2):
                for previous in basis_rows:
                    vector = vector - np.dot(previous, vector) * previous
            residuals.append(vector)
        lengths = np.array([np.sqrt(np.dot(vector, vector)) for vector in residuals])
        chosen = int(np.argmax(lengths))
        basis_rows.append(residuals[chosen] / lengths[chosen])
    filters = np.array(basis_rows).reshape(2, poly_order, 2, poly_order)
    return jnp.asarray(filters, jnp.float32)

def compress(coeffs, filters):
    poly_order = filters.shape[1]
    blocks = coeffs.reshape(2, 2, 2, poly_order, poly_order, poly_order, -1)
    along_x = jnp.einsum('pqai,abcijks->pbcqjks', filters, blocks, precision=FULL_PRECISION)
    along_y = jnp.einsum('rtbj,pbcqjks->prcqtks', filters, along_x, precision=FULL_PRECISION)
    along_z = jnp.einsum('uwck,prcqtks->pruqtws', filters, along_y, precision=FULL_PRECISION)
    return along_z.reshape(8 * poly_order ** 3, -1)

def reconstruct(coeffs, filters):
    poly_order = filters.shape[1]
    blocks = coeffs.reshape(2, 2, 2, poly_order, poly_order, poly_order, -1)
    along_x = jnp.einsum('pqai,pbcqjks->abcijks', filters, blocks, precision=FULL_PRECISION)
    along_y = jnp.einsum('pqbj,apciqks->abcijks', filters, along_x, precision=FULL_PRECISION)
    along_z = jnp.einsum('pqck,abpijqs->abcijks', filters, along_y, precision=FULL_PRECISION)
    return along_z.reshape(8 * poly_order ** 3, -1)

def to_sets(members, cube_size):
    set_total = members.shape[1] // 8
    return members.reshape(cube_size, set_total, 8).transpose(2, 0, 1).reshape(8 * cube_size, set_total)

def to_members(sets_rows, cube_size):
    set_total = sets_rows.shape[1]
    return sets_rows.reshape(8, cube_size, set_total).transpose(1, 2, 0).reshape(cube_size, 8 * set_total)

def reference(fine_coeffs, set_counts, route_first, route_top, level_gain):
    filters = two_scale(POLY_ORDER)
    cube_size = POLY_ORDER ** 3
    devices = N_LEAF * N_REP
    column = lax.iota(jnp.int32, fine_coeffs.shape[1])
    sender = column // SETS_DEV
    living = column % SETS_DEV < set_counts[sender]
    packed = compress(fine_coeffs, filters)
    parents = packed[:cube_size]
    details = packed[cube_size:] * level_gain[0][:, None]
    member_width = devices * SLOTS_FIRST
    total_first = devices * member_width
    position_first = route_first // SLOTS_FIRST * member_width + sender * SLOTS_FIRST + route_first % SLOTS_FIRST
    target = jnp.where(living, position_first, total_first).astype(jnp.int32)
    members = jnp.zeros((cube_size, total_first + 1), jnp.float32).at[:, target].set(parents)[:, :total_first]
    middle = to_sets(members, cube_size)
    packed_mid = compress(middle, filters)
    parents_mid = packed_mid[:cube_size]
    details_mid = packed_mid[cube_size:] * level_gain[1][:, None]
    mid_column = lax.iota(jnp.int32, middle.shape[1])
    mid_sender = mid_column // SETS_MID
    sender_leaf = mid_sender // N_REP
    sender_rep = mid_sender % N_REP
    width_top = N_LEAF * SLOTS_TOP
    owner_top = route_top // SLOTS_TOP * N_REP + sender_rep
    position_top = (owner_top * width_top + sender_leaf * SLOTS_TOP + route_top % SLOTS_TOP).astype(jnp.int32)
    top_members = jnp.zeros((cube_size, devices * width_top), jnp.float32).at[:, position_top].set(parents_mid)
    packed_top = compress(to_sets(top_members, cube_size), filters)
    coarse = packed_top[:cube_size]
    scaled_top = jnp.concatenate([coarse, packed_top[cube_size:] * level_gain[2][:, None]], 0)
    top_back = to_members(reconstruct(scaled_top, filters), cube_size)
    parents_mid_new = top_back[:, position_top]
    rebuilt_mid = reconstruct(jnp.concatenate([parents_mid_new, details_mid], 0), filters)
    mid_back = to_members(rebuilt_mid, cube_size)
    parents_fine = jnp.where(living, mid_back[:, position_first.astype(jnp.int32)], 0.0)
    smoothed = reconstruct(jnp.concatenate([parents_fine, details], 0), filters)
    smoothed = jnp.where(living, smoothed, 0.0)
    return (smoothed, coarse)
```

```python
import functools
import math

import jax
import jax.numpy as jnp
import ml_dtypes
import numpy as np
from jax import lax
from jax.experimental import pallas as pl
from jax.experimental.pallas import tpu as pltpu
from jax.sharding import PartitionSpec as P

POLY_ORDER = 10
F32 = jnp.float32
BF16 = jnp.bfloat16
MESH = pl.DeviceIdType.MESH


def legendre_pair(count, position):
    before, current = (1.0, position)
    for degree in range(1, count):
        before, current = (
            current,
            ((2 * degree + 1) * position * current - degree * before) / (degree + 1),
        )
    derivative = count * (position * current - before) / (position * position - 1.0)
    return (current, derivative)


def gauss_points(count):
    nodes = []
    weights = []
    for node_index in range(count):
        estimate = math.cos(math.pi * (node_index + 0.75) / (count + 0.5))
        for newton_step in range(100):
            current, derivative = legendre_pair(count, estimate)
            estimate = estimate - current / derivative
        current, derivative = legendre_pair(count, estimate)
        nodes.append(estimate)
        weights.append(2.0 / ((1.0 - estimate * estimate) * derivative * derivative))
    return (np.array(nodes), np.array(weights))


def legendre_rows(degree_count, points):
    values = [points * 0.0 + 1.0, points.copy()]
    for degree in range(1, degree_count - 1):
        values.append(
            ((2 * degree + 1) * points * values[degree] - degree * values[degree - 1])
            / (degree + 1)
        )
    return np.stack(
        [np.sqrt(2.0 * degree + 1.0) * values[degree] for degree in range(degree_count)]
    )


@functools.cache
def two_scale(poly_order):
    points, weights = gauss_points(2 * poly_order)
    lower_half = (points + 1.0) / 4.0
    half_weights = weights / 4.0
    child_rows = legendre_rows(poly_order, 4.0 * lower_half - 1.0)
    parent_low = legendre_rows(poly_order, 2.0 * lower_half - 1.0)
    parent_high = legendre_rows(poly_order, 2.0 * (lower_half + 0.5) - 1.0)
    filter_left = math.sqrt(2.0) * (parent_low * half_weights) @ child_rows.T
    filter_right = math.sqrt(2.0) * (parent_high * half_weights) @ child_rows.T
    basis_rows = list(np.concatenate([filter_left, filter_right], axis=1))
    units = np.eye(2 * poly_order)
    for step_index in range(poly_order):
        residuals = []
        for vector in units:
            for sweep in range(2):
                for previous in basis_rows:
                    vector = vector - np.dot(previous, vector) * previous
            residuals.append(vector)
        lengths = np.array([np.sqrt(np.dot(vector, vector)) for vector in residuals])
        chosen = int(np.argmax(lengths))
        basis_rows.append(residuals[chosen] / lengths[chosen])
    filters = np.array(basis_rows).reshape(2, poly_order, 2, poly_order)
    return filters.astype(np.float32).astype(np.float64)


def halves(matrix):
    high = matrix.astype(ml_dtypes.bfloat16)
    low = (matrix - high.astype(np.float64)).astype(ml_dtypes.bfloat16)
    return high, low


def left3(matrix):
    high, low = halves(matrix)
    return np.concatenate([high, low, high], axis=-1)


def right3(matrix):
    high, low = halves(matrix)
    return np.concatenate([high, low, high], axis=-2)


@functools.cache
def tables():
    H = two_scale(POLY_ORDER)
    out = {}
    yz = np.einsum("rtbj,uwck->rutwbcjk", H, H)
    yz = yz.reshape(4, 100, 4, 100)
    par = np.zeros((2, 104, 4, 2, 100))
    for i2 in range(2):
        par[i2, :100, :, i2, :] = yz[0]
    par = par.reshape(208, 800)
    out["par"] = left3(par)
    out["parT"] = left3(par.T.copy())
    full = np.zeros((2, 4, 104, 4, 104))
    full[0, :, :100, :, :100] = yz
    full[1, :, :100, :, 4:] = yz
    full = full.reshape(2, 416, 416)
    out["yz"] = left3(full)
    out["yzT"] = left3(full.transpose(0, 2, 1))
    hx = H.reshape(20, 20)
    kx = np.kron(hx, np.eye(8))
    out["x"] = left3(kx)
    out["xT"] = left3(kx.T.copy())
    out["x0"] = left3(kx[:80])
    out["x0T"] = left3(kx[:80].T.copy())
    mid = np.zeros((4, 104, 2, 2, 104))
    mid[:, :100, :, :, :100] = yz.reshape(4, 100, 2, 2, 100).transpose(0, 1, 3, 2, 4)
    mid = mid.reshape(416, 416)
    out["mid"] = left3(mid)
    out["midT"] = left3(mid.T.copy())
    rx = np.zeros((2, 3, 4, 32, 2, 32, 10))
    for tile in range(3):
        for quarter in range(4 if tile < 2 else 2):
            i = 4 * tile + quarter
            for s in range(32):
                rx[:, tile, quarter, s, :, s, :] = H[:, :, :, i].transpose(2, 0, 1)
    rx = rx.reshape(2, 384, 640)
    out["rx"] = np.stack(halves(rx), 0)
    ex = np.zeros((128, 2, 32, 10))
    for p in range(2):
        for m in range(10):
            ex[p * 10 + m, p, :, m] = 1.0
    out["ex"] = ex.reshape(128, 640).astype(ml_dtypes.bfloat16)
    up = np.zeros((2, 2, 104, 128))
    up[:, :, :100, :100] = yz[0].reshape(100, 2, 2, 100).transpose(1, 2, 3, 0)
    out["up"] = left3(up.reshape(2, 208, 128))
    top = np.zeros((4, 128, 4, 128))
    top[:, :100, :, :100] = yz.transpose(2, 3, 0, 1)
    top = top.reshape(512, 512)
    out["top"] = right3(top)
    out["topT"] = right3(top.T.copy())
    one = np.zeros((2, 16, 2, 16))
    one[:, :10, :, :10] = H
    kt = np.kron(np.eye(8), one.reshape(32, 32))
    out["tx"] = left3(kt)
    out["txT"] = left3(kt.T.copy())
    return out


def split(x):
    high = x.astype(BF16)
    low = (x - high.astype(F32)).astype(BF16)
    return high, low


def dot(a, b):
    return lax.dot_general(a, b, (((1,), (0,)), ((), ())), preferred_element_type=F32)


def dot_t(a, b):
    return lax.dot_general(a, b, (((1,), (1,)), ((), ())), preferred_element_type=F32)


def left_dot(m3, x):
    high, low = split(x)
    return dot(m3, jnp.concatenate([high, high, low], 0))


def right_dot(x, m3):
    high, low = split(x)
    return dot(jnp.concatenate([high, high, low], 1), m3)


def one_hot_dot(x, hot):
    high, low = split(x)
    return dot(high, hot) + dot(low, hot)


def quarter_of(shape):
    return lax.broadcasted_iota(jnp.int32, shape, len(shape) - 1) // 32


def place(pieces, rows):
    mark = quarter_of((rows, 128))
    out = None
    for n, (tile, now) in enumerate(pieces):
        turn = ((n - now) * 32) % 128
        moved = pltpu.roll(tile, turn, 1) if turn else tile
        out = moved if out is None else jnp.where(mark == n, moved, out)
    return out


def vmem(mib):
    return pltpu.CompilerParams(vmem_limit_bytes=mib * 1024 * 1024)


def whole(shape):
    return pl.BlockSpec(shape, lambda *_: (0,) * len(shape))


SMEM = pl.BlockSpec(memory_space=pltpu.SMEM)


def parents_kernel(rep_ref, x_ref, par_ref, x0_ref, tgt_ref, b0, b1, b2, b3, acc, pm):
    step = pl.program_id(0)
    u = left_dot(par_ref[...], x_ref[...].reshape(800, 256))
    u = u.reshape(2, 13, 8, 256)
    acc[:, 2 * step] = u[0]
    acc[:, 2 * step + 1] = u[1]

    @pl.when(step == 9)
    def _():
        for t in range(13):
            v = left_dot(x0_ref[...], acc[t].reshape(160, 256))
            pm[:, 8 * t : 8 * t + 8, :] = v.reshape(10, 8, 256)
        lane = lax.broadcasted_iota(jnp.int32, (256, 256), 1)
        owner_rep = (lane // 64 + rep_ref[0]) % 4
        code = 2 * ((lane % 32) * 4 + owner_rep) + (lane // 32) % 2
        hot = (tgt_ref[...] == code).astype(F32).astype(BF16)
        y = one_hot_dot(pm[...].reshape(1040, 256), hot).reshape(10, 104, 256)
        for o, out in enumerate((b0, b1, b2, b3)):
            tile = y[:, :, (o // 2) * 128 : (o // 2) * 128 + 128]
            base = (o % 2) * 2
            for s in range(2):
                for q in range(2):
                    out[:, (2 * s + q) * 128 : (2 * s + q + 1) * 128] = place(
                        [(tile[4 * q + n], base + s) for n in range(4)], 104
                    )
            out[:, 512:640] = place(
                [(tile[8], base), (tile[9], base), (tile[8], base + 1), (tile[9], base + 1)], 104
            )


def parents_call(x5, rep, target):
    T = tables()
    block = jax.ShapeDtypeStruct((104, 640), F32)
    return pl.pallas_call(
        parents_kernel,
        grid=(10,),
        in_specs=[
            SMEM,
            pl.BlockSpec((1, 4, 1, 200, 256), lambda s: (s // 5, 0, s % 5, 0, 0)),
            whole((208, 2400)),
            whole((80, 480)),
            whole((256, 1)),
        ],
        out_specs=[whole((104, 640))] * 4,
        out_shape=[block] * 4,
        scratch_shapes=[pltpu.VMEM((13, 20, 8, 256), F32), pltpu.VMEM((10, 104, 256), F32)],
        compiler_params=vmem(32),
        cost_estimate=pl.CostEstimate(flops=2 * 10**9, bytes_accessed=10**7, transcendentals=0),
        name="parents",
    )(rep, x5, T["par"], T["x0"], target)


def details_kernel(x_ref, yz_ref, x1_ref, xt_ref, yzt_ref, g_ref, o_ref, acc):
    step = pl.program_id(0)

    @pl.when(step < 10)
    def _():
        for i2 in range(2):
            w = x_ref[0, :, 0, 96 * i2 : 96 * i2 + 104, :].reshape(416, 256)
            u = left_dot(yz_ref[i2], w)
            acc[:, 2 * step + i2] = u.reshape(52, 8, 256)

    @pl.when((step >= 10) & (step < 23))
    def _():
        for n in range(4):
            t = (step - 10) * 4 + n
            v = left_dot(x1_ref[...], acc[t].reshape(160, 256))
            row = lax.broadcasted_iota(jnp.int32, (384, 256), 0) % 128
            gain = dot(g_ref[...], (row == t).astype(F32).astype(BF16))
            w = left_dot(xt_ref[...], v * gain)
            acc[t] = w.reshape(20, 8, 256)

    @pl.when(step >= 23)
    def _():
        pair = step - 23
        z = []
        for i2 in range(2):
            w = acc[:, 2 * pair + i2].reshape(416, 256)
            z.append(left_dot(yzt_ref[i2], w).reshape(4, 104, 256))
        o_ref[0, :, 0, 0:96, :] = z[0][:, 0:96]
        o_ref[0, :, 0, 96:104, :] = z[0][:, 96:104] + z[1][:, 0:8]
        o_ref[0, :, 0, 104:200, :] = z[1][:, 8:104]


def details_call(x5, gain3):
    T = tables()

    def x_map(s):
        n = jnp.minimum(s, 9)
        return (n // 5, 0, n % 5, 0, 0)

    def o_map(s):
        n = jnp.maximum(s - 23, 0)
        return (n // 5, 0, n % 5, 0, 0)

    return pl.pallas_call(
        details_kernel,
        grid=(33,),
        in_specs=[
            pl.BlockSpec((1, 4, 1, 200, 256), x_map),
            whole((2, 416, 1248)),
            whole((160, 480)),
            whole((160, 480)),
            whole((2, 416, 1248)),
            whole((160, 384)),
        ],
        out_specs=pl.BlockSpec((1, 4, 1, 200, 256), o_map),
        out_shape=jax.ShapeDtypeStruct((2, 4, 5, 200, 256), F32),
        scratch_shapes=[pltpu.VMEM((52, 20, 8, 256), F32)],
        compiler_params=vmem(40),
        cost_estimate=pl.CostEstimate(
            flops=15 * 10**9, bytes_accessed=2 * 10**7, transcendentals=0
        ),
        name="details",
    )(x5, T["yz"], T["x"], T["xT"], T["yzT"], gain3)


def middle_kernel(
    rep_ref, b0, b1, b2, b3, rx_ref, mid_ref, midt_ref, g_ref, ex_ref,
    p_ref, d0, d1, d2, d3, got, back,
):
    rep = rep_ref[0]
    for o, b in enumerate((b0, b1, b2, b3)):
        got[(rep + 4 - o) % 4] = b[...]
    high_rx, low_rx = rx_ref[0].reshape(768, 640), rx_ref[1].reshape(768, 640)
    rows = []
    for s in range(2):
        for by in range(2):
            parts = []
            for bx in range(2):
                r = 2 * bx + by
                last = got[r, :, 512:640]
                parts += [
                    got[r, :, 256 * s : 256 * s + 256],
                    pltpu.roll(last, 64, 1) if s else last,
                ]
            rows.append(jnp.concatenate(parts, 1))
    x = jnp.concatenate(rows, 0)
    high, low = split(x)
    u = dot(high, high_rx) + dot(low, high_rx) + dot(high, low_rx)
    v = left_dot(mid_ref[...], u)
    p_ref[...] = jnp.transpose(v[0:128, 0:384])[0:320].reshape(8, 40, 128)
    gh, gl = split(g_ref[...])
    gm, gl = gl, (g_ref[...] - gh.astype(F32) - gl.astype(F32)).astype(BF16)
    gain = dot(gh, ex_ref[...]) + dot(gm, ex_ref[...]) + dot(gl, ex_ref[...])
    w = left_dot(midt_ref[...], v * gain)
    high, low = split(w)
    z = dot_t(high, high_rx) + dot_t(low, high_rx) + dot_t(high, low_rx)
    for by in range(2):
        for bx in range(2):
            r = 2 * bx + by
            for s in range(2):
                base = (2 * s + by) * 104
                back[r, :, 256 * s : 256 * s + 256] = z[
                    base : base + 104, 384 * bx : 384 * bx + 256
                ]
            last = [
                z[(2 * s + by) * 104 : (2 * s + by) * 104 + 104, 384 * bx + 256 : 384 * bx + 384]
                for s in range(2)
            ]
            back[r, :, 512:640] = last[0] + pltpu.roll(last[1], 64, 1)
    for o, d in enumerate((d0, d1, d2, d3)):
        d[...] = back[(rep + o) % 4]


def middle_call(blocks, rep, gain):
    T = tables()
    block = jax.ShapeDtypeStruct((104, 640), F32)
    return pl.pallas_call(
        middle_kernel,
        in_specs=[SMEM] + [pl.BlockSpec(memory_space=pltpu.VMEM)] * 9,
        out_specs=[pl.BlockSpec(memory_space=pltpu.VMEM)] * 5,
        out_shape=[jax.ShapeDtypeStruct((8, 40, 128), F32)] + [block] * 4,
        scratch_shapes=[pltpu.VMEM((4, 104, 640), F32), pltpu.VMEM((4, 104, 640), F32)],
        compiler_params=vmem(32),
        name="middle",
    )(rep, *blocks, T["rx"], T["mid"], T["midT"], gain, T["ex"])


def gather_kernel(slab_ref, out_ref, own_sem, send, recv, fsend, frecv):
    leaf = lax.axis_index("leaf")
    rep = lax.axis_index("rep")
    core = leaf % 2
    me = leaf // 2
    sibling = leaf + 1 - 2 * core
    barrier = pltpu.get_barrier_semaphore()

    def greet(k, carry):
        other = 2 * ((me + k) % 16) + core
        pl.semaphore_signal(barrier, inc=1, device_id=(other, rep), device_id_type=MESH)
        return carry

    lax.fori_loop(1, 16, greet, 0)
    pl.semaphore_signal(barrier, inc=1, device_id=(sibling, rep), device_id_type=MESH)
    own = pltpu.make_async_copy(slab_ref.at[me // 2], out_ref.at[leaf], own_sem)
    own.start()
    pl.semaphore_wait(barrier, 16)

    def out_copy(k):
        to = (me + k) % 16
        return pltpu.make_async_remote_copy(
            src_ref=slab_ref.at[to // 2],
            dst_ref=out_ref.at[leaf],
            send_sem=send.at[k],
            recv_sem=recv.at[k],
            device_id=(2 * to + core, rep),
            device_id_type=MESH,
        )

    def in_copy(k):
        slot = 2 * ((me + 16 - k) % 16) + core
        return pltpu.make_async_remote_copy(
            src_ref=slab_ref.at[0],
            dst_ref=out_ref.at[slot],
            send_sem=send.at[k],
            recv_sem=recv.at[k],
            device_id=(leaf, rep),
            device_id_type=MESH,
        )

    def pass_copy(k, which):
        slot = 2 * ((me + 16 - k) % 16) + which
        return pltpu.make_async_remote_copy(
            src_ref=out_ref.at[slot],
            dst_ref=out_ref.at[slot],
            send_sem=fsend.at[k],
            recv_sem=frecv.at[k],
            device_id=(sibling, rep),
            device_id_type=MESH,
        )

    def begin(k, carry):
        out_copy(k).start()
        return carry

    lax.fori_loop(1, 16, begin, 0)
    own.wait()
    pass_copy(0, core).start()

    def relay(k, carry):
        in_copy(k).wait_recv()
        pass_copy(k, core).start()
        return carry

    lax.fori_loop(1, 16, relay, 0)

    def finish(k, carry):
        pass_copy(k, 1 - core).wait_recv()
        pass_copy(k, core).wait_send()
        return carry

    lax.fori_loop(0, 16, finish, 0)

    def sent(k, carry):
        out_copy(k).wait_send()
        return carry

    lax.fori_loop(1, 16, sent, 0)


def gather_call(slabs):
    return pl.pallas_call(
        gather_kernel,
        in_specs=[pl.BlockSpec(memory_space=pltpu.VMEM)],
        out_specs=pl.BlockSpec(memory_space=pltpu.VMEM),
        out_shape=jax.ShapeDtypeStruct((32, 40, 128), F32),
        scratch_shapes=[
            pltpu.SemaphoreType.DMA,
            pltpu.SemaphoreType.DMA((16,)),
            pltpu.SemaphoreType.DMA((16,)),
            pltpu.SemaphoreType.DMA((16,)),
            pltpu.SemaphoreType.DMA((16,)),
        ],
        compiler_params=pltpu.CompilerParams(collective_id=1, has_side_effects=True),
        name="to_top",
    )(slabs)


def top_kernel(
    route_ref, turn_ref, g_ref, top_ref, tx_ref, txt_ref, topt_ref, gain_ref,
    p_ref, c_ref, kids,
):
    kids[...] = jnp.zeros_like(kids)

    def scatter(l, carry):
        for t in range(4):
            code = route_ref[t, l]
            kids[(code // 2) * 8 + t * 2 + code % 2, 0:10, :] = g_ref[l, 10 * t : 10 * t + 10, :]
        return carry

    lax.fori_loop(0, 32, scatter, 0)
    for g in range(4):
        sets = kids[64 * g : 64 * g + 64].reshape(8, 2, 4, 16, 128)
        y = jnp.concatenate([sets[:, :, b].reshape(256, 128) for b in range(4)], 1)
        z = right_dot(y, top_ref[...])
        v = left_dot(tx_ref[...], z)
        c_ref[8 * g : 8 * g + 8] = v.reshape(8, 2, 16, 512)[:, 0, :, 0:128]
        v = (v.reshape(8, 32, 512) * gain_ref[...][None]).reshape(256, 512)
        z = left_dot(txt_ref[...], v)
        y = right_dot(z, topt_ref[...])
        for l in range(8):
            for b in range(4):
                for bx in range(2):
                    kids[64 * g + 8 * l + 4 * bx + b] = y[
                        32 * l + 16 * bx : 32 * l + 16 * bx + 16, 128 * b : 128 * b + 128
                    ]

    def pick(n, carry):
        for t in range(4):
            code = route_ref[t, 4 * n + turn_ref[0]]
            p_ref[n, 10 * t : 10 * t + 10, :] = kids[(code // 2) * 8 + t * 2 + code % 2, 0:10, :]
        return carry

    lax.fori_loop(0, 8, pick, 0)


def top_call(routes, turn, got, gain):
    T = tables()
    return pl.pallas_call(
        top_kernel,
        in_specs=[SMEM, SMEM] + [pl.BlockSpec(memory_space=pltpu.VMEM)] * 6,
        out_specs=[pl.BlockSpec(memory_space=pltpu.VMEM)] * 2,
        out_shape=[
            jax.ShapeDtypeStruct((8, 40, 128), F32),
            jax.ShapeDtypeStruct((32, 16, 128), F32),
        ],
        scratch_shapes=[pltpu.VMEM((256, 16, 128), F32)],
        compiler_params=vmem(32),
        name="top",
    )(routes, turn, got, T["top"], T["tx"], T["txT"], T["topT"], gain)


def spread_kernel(slab_ref, top_ref, out_ref, coarse_ref, own_sem, send, recv, csend, crecv):
    leaf = lax.axis_index("leaf")
    rep = lax.axis_index("rep")
    turn = leaf % 4
    group = leaf // 4
    me = group * 4 + rep
    barrier = pltpu.get_barrier_semaphore()

    def greet(k, carry):
        to = (me + k) % 32
        pl.semaphore_signal(
            barrier, inc=1, device_id=(4 * (to // 4) + turn, to % 4), device_id_type=MESH
        )
        return carry

    lax.fori_loop(1, 32, greet, 0)
    own = pltpu.make_async_copy(slab_ref.at[group], out_ref.at[me], own_sem.at[0])
    own.start()
    own_top = pltpu.make_async_copy(top_ref.at[leaf], coarse_ref.at[group], own_sem.at[1])
    own_top.start()
    pl.semaphore_wait(barrier, 31)

    def out_copy(k):
        to = (me + k) % 32
        return pltpu.make_async_remote_copy(
            src_ref=slab_ref.at[to // 4],
            dst_ref=out_ref.at[me],
            send_sem=send.at[k],
            recv_sem=recv.at[k],
            device_id=(4 * (to // 4) + turn, to % 4),
            device_id_type=MESH,
        )

    def in_copy(k):
        return pltpu.make_async_remote_copy(
            src_ref=slab_ref.at[0],
            dst_ref=out_ref.at[(me + 32 - k) % 32],
            send_sem=send.at[k],
            recv_sem=recv.at[k],
            device_id=(leaf, rep),
            device_id_type=MESH,
        )

    def out_top(k):
        to = 4 * ((group + k) % 8) + turn
        return pltpu.make_async_remote_copy(
            src_ref=top_ref.at[to],
            dst_ref=coarse_ref.at[group],
            send_sem=csend.at[k],
            recv_sem=crecv.at[k],
            device_id=(to, rep),
            device_id_type=MESH,
        )

    def in_top(k):
        return pltpu.make_async_remote_copy(
            src_ref=top_ref.at[0],
            dst_ref=coarse_ref.at[(group + 8 - k) % 8],
            send_sem=csend.at[k],
            recv_sem=crecv.at[k],
            device_id=(leaf, rep),
            device_id_type=MESH,
        )

    def begin(k, carry):
        out_copy(k).start()
        return carry

    def begin_top(k, carry):
        out_top(k).start()
        return carry

    lax.fori_loop(1, 32, begin, 0)
    lax.fori_loop(1, 8, begin_top, 0)

    def finish(k, carry):
        in_copy(k).wait_recv()
        out_copy(k).wait_send()
        return carry

    def finish_top(k, carry):
        in_top(k).wait_recv()
        out_top(k).wait_send()
        return carry

    lax.fori_loop(1, 32, finish, 0)
    lax.fori_loop(1, 8, finish_top, 0)
    own.wait()
    own_top.wait()


def spread_call(slabs, tops):
    return pl.pallas_call(
        spread_kernel,
        in_specs=[pl.BlockSpec(memory_space=pltpu.VMEM)] * 2,
        out_specs=[pl.BlockSpec(memory_space=pltpu.VMEM)] * 2,
        out_shape=[
            jax.ShapeDtypeStruct((32, 40, 128), F32),
            jax.ShapeDtypeStruct((8, 16, 128), F32),
        ],
        scratch_shapes=[
            pltpu.SemaphoreType.DMA((2,)),
            pltpu.SemaphoreType.DMA((32,)),
            pltpu.SemaphoreType.DMA((32,)),
            pltpu.SemaphoreType.DMA((8,)),
            pltpu.SemaphoreType.DMA((8,)),
        ],
        compiler_params=pltpu.CompilerParams(collective_id=2, has_side_effects=True),
        name="from_top",
    )(slabs, tops)


def final_kernel(
    rep_ref, slab_ref, d0, d1, d2, d3, up_ref, rx_ref, tgt_ref, x0t_ref, part_ref, z_ref, live_ref,
    o_ref, got, ypos, pnew, wide,
):
    step = pl.program_id(0)

    @pl.when(step == 0)
    def _():
        rep = rep_ref[0]
        by, bx = rep % 2, rep // 2
        for o, d in enumerate((d0, d1, d2, d3)):
            got[(rep + 4 - o) % 4] = d[...]
        mine = slab_ref[...].reshape(8, 4, 40, 128)
        cols = []
        for r in range(4):
            rows = mine[:, r].reshape(320, 128)
            rows = jnp.concatenate([rows, jnp.zeros((64, 128), F32)], 0)
            cols.append(jnp.transpose(rows))
        tall = left_dot(up_ref[by], jnp.concatenate(cols, 1))
        stack = jnp.concatenate(
            [tall[104 * s : 104 * s + 104, 384 * r : 384 * r + 384] for r in range(4) for s in range(2)],
            0,
        )
        high, low = split(stack)
        hi_rx = rx_ref[0, bx][:, 0:384]
        lo_rx = rx_ref[1, bx][:, 0:384]
        f = dot_t(high, hi_rx) + dot_t(low, hi_rx) + dot_t(high, lo_rx)
        for r in range(4):
            for s in range(2):
                base = (2 * r + s) * 104
                got[r, :, 256 * s : 256 * s + 256] += f[base : base + 104, 0:256]
            got[r, :, 512:640] += f[2 * r * 104 : 2 * r * 104 + 104, 256:384] + pltpu.roll(
                f[(2 * r + 1) * 104 : (2 * r + 2) * 104, 256:384], 64, 1
            )
        for i in range(10):
            for pair in range(2):
                pieces = []
                for r in (2 * pair, 2 * pair + 1):
                    for s in range(2):
                        if i < 8:
                            tile = 2 * s + i // 4
                            now = i % 4
                        else:
                            tile = 4
                            now = 2 * s + i - 8
                        pieces.append((got[r, :, 128 * tile : 128 * tile + 128], now))
                ypos[i, :, 128 * pair : 128 * pair + 128] = place(pieces, 104)
        row = lax.broadcasted_iota(jnp.int32, (256, 256), 0)
        code = 2 * ((row % 32) * 4 + row // 64) + (row // 32) % 2
        hot = (tgt_ref[...] == code).astype(F32).astype(BF16)
        pnew[...] = one_hot_dot(ypos[...].reshape(1040, 256), hot).reshape(10, 104, 256)
        for t in range(13):
            w = pnew[:, 8 * t : 8 * t + 8, :].reshape(80, 256)
            wide[:, 8 * t : 8 * t + 8, :] = left_dot(x0t_ref[...], w).reshape(20, 8, 256)

    w = wide[pl.ds(2 * step, 2)].reshape(208, 256)
    out = left_dot(part_ref[...], w).reshape(4, 200, 256) + z_ref[0, :, 0]
    o_ref[0, :, 0] = jnp.where(live_ref[...][None] > 0, out, 0.0)


def final_call(rep, slabs, blocks, target, z5, live):
    T = tables()
    wide = pl.BlockSpec((1, 4, 1, 200, 256), lambda s: (s // 5, 0, s % 5, 0, 0))
    return pl.pallas_call(
        final_kernel,
        grid=(10,),
        in_specs=[SMEM, whole((32, 40, 128))]
        + [whole((104, 640))] * 4
        + [
            whole((2, 208, 384)),
            whole((2, 2, 384, 640)),
            whole((1, 256)),
            whole((160, 240)),
            whole((800, 624)),
            wide,
            whole((1, 256)),
        ],
        out_specs=wide,
        out_shape=jax.ShapeDtypeStruct((2, 4, 5, 200, 256), F32),
        scratch_shapes=[
            pltpu.VMEM((4, 104, 640), F32),
            pltpu.VMEM((10, 104, 256), F32),
            pltpu.VMEM((10, 104, 256), F32),
            pltpu.VMEM((20, 104, 256), F32),
        ],
        compiler_params=vmem(40),
        name="final",
    )(rep, slabs, *blocks, T["up"], T["rx"], target, T["x0T"], T["parT"], z5, live)


def gain_cube(row):
    cube = jnp.concatenate([jnp.zeros((1000,), F32), row]).reshape(2, 4, 10, 100)
    return jnp.pad(cube, ((0, 0), (0, 0), (0, 0), (0, 4)))


def finest_gain(row):
    cube = gain_cube(row).reshape(2, 4, 10, 13, 8).transpose(0, 2, 4, 1, 3).reshape(160, 52)
    cube = jnp.pad(cube, ((0, 0), (0, 76)))
    high = lax.reduce_precision(cube, 8, 7)
    rest = cube - high
    mid = lax.reduce_precision(rest, 8, 7)
    return jnp.concatenate([high, mid, rest - mid], 1).astype(BF16)


def middle_gain(row):
    cube = gain_cube(row).transpose(1, 3, 0, 2).reshape(416, 20)
    return jnp.pad(cube, ((0, 0), (0, 108)))


def top_gain(row):
    cube = jnp.concatenate([jnp.ones((1000,), F32), row]).reshape(2, 4, 10, 100)
    cube = jnp.pad(cube, ((0, 0), (0, 0), (0, 6), (0, 28)))
    return cube.transpose(0, 2, 1, 3).reshape(32, 512)


def swap(blocks):
    out = [blocks[0]]
    for o in range(1, 4):
        out.append(lax.ppermute(blocks[o], "rep", [(r, (r + o) % 4) for r in range(4)]))
    return out


def shards(fine_coeffs, set_counts, route_first, route_top, level_gain):
    leaf = lax.axis_index("leaf")
    rep = lax.axis_index("rep").reshape(1).astype(jnp.int32)
    living = lax.iota(jnp.int32, 256) < set_counts[0]
    target = jnp.where(living, route_first, -1)
    live = living.astype(F32).reshape(1, 256)
    routes = lax.all_gather(route_top, "leaf")
    routes = lax.dynamic_slice_in_dim(routes, (leaf // 4) * 4, 4, 0)
    turn = (leaf % 4).reshape(1).astype(jnp.int32)
    x5 = fine_coeffs.reshape(2, 4, 5, 200, 256)
    blocks = parents_call(x5, rep, target.reshape(256, 1))
    blocks = swap(blocks)
    z5 = details_call(x5, finest_gain(level_gain[0]))
    mids = middle_call(blocks, rep, middle_gain(level_gain[1]))
    back = swap(mids[1:])
    got = gather_call(mids[0])
    slabs, tops = top_call(routes, turn, got, top_gain(level_gain[2]))
    new, coarse = spread_call(slabs, tops)
    out = final_call(rep, new, back, target.reshape(1, 256), z5, live)
    coarse = coarse[:, :10, :100].reshape(8, 1000).T
    return (out.reshape(8000, 256), coarse)


def solution(mesh):
    placed = (
        P(None, ("leaf", "rep")),
        P(("leaf", "rep")),
        P(("leaf", "rep")),
        P(("leaf", "rep")),
        P(),
    )
    return jax.shard_map(
        shards,
        mesh=mesh,
        in_specs=placed,
        out_specs=(P(None, ("leaf", "rep")), P(None, ("leaf", "rep"))),
        check_vma=False,
    )
```

```python
import functools
import math

import jax
import jax.numpy as jnp
import ml_dtypes
import numpy as np
from jax import lax
from jax.experimental import pallas as pl
from jax.experimental.pallas import tpu as pltpu
from jax.sharding import PartitionSpec as P

POLY_ORDER = 10
F32 = jnp.float32
BF16 = jnp.bfloat16
MESH = pl.DeviceIdType.MESH


def legendre_pair(count, position):
    before, current = (1.0, position)
    for degree in range(1, count):
        before, current = (
            current,
            ((2 * degree + 1) * position * current - degree * before) / (degree + 1),
        )
    derivative = count * (position * current - before) / (position * position - 1.0)
    return (current, derivative)


def gauss_points(count):
    nodes = []
    weights = []
    for node_index in range(count):
        estimate = math.cos(math.pi * (node_index + 0.75) / (count + 0.5))
        for newton_step in range(100):
            current, derivative = legendre_pair(count, estimate)
            estimate = estimate - current / derivative
        current, derivative = legendre_pair(count, estimate)
        nodes.append(estimate)
        weights.append(2.0 / ((1.0 - estimate * estimate) * derivative * derivative))
    return (np.array(nodes), np.array(weights))


def legendre_rows(degree_count, points):
    values = [points * 0.0 + 1.0, points.copy()]
    for degree in range(1, degree_count - 1):
        values.append(
            ((2 * degree + 1) * points * values[degree] - degree * values[degree - 1])
            / (degree + 1)
        )
    return np.stack(
        [np.sqrt(2.0 * degree + 1.0) * values[degree] for degree in range(degree_count)]
    )


@functools.cache
def two_scale(poly_order):
    points, weights = gauss_points(2 * poly_order)
    lower_half = (points + 1.0) / 4.0
    half_weights = weights / 4.0
    child_rows = legendre_rows(poly_order, 4.0 * lower_half - 1.0)
    parent_low = legendre_rows(poly_order, 2.0 * lower_half - 1.0)
    parent_high = legendre_rows(poly_order, 2.0 * (lower_half + 0.5) - 1.0)
    filter_left = math.sqrt(2.0) * (parent_low * half_weights) @ child_rows.T
    filter_right = math.sqrt(2.0) * (parent_high * half_weights) @ child_rows.T
    basis_rows = list(np.concatenate([filter_left, filter_right], axis=1))
    units = np.eye(2 * poly_order)
    for step_index in range(poly_order):
        residuals = []
        for vector in units:
            for sweep in range(2):
                for previous in basis_rows:
                    vector = vector - np.dot(previous, vector) * previous
            residuals.append(vector)
        lengths = np.array([np.sqrt(np.dot(vector, vector)) for vector in residuals])
        chosen = int(np.argmax(lengths))
        basis_rows.append(residuals[chosen] / lengths[chosen])
    filters = np.array(basis_rows).reshape(2, poly_order, 2, poly_order)
    return filters.astype(np.float32).astype(np.float64)


def halves(matrix):
    high = matrix.astype(ml_dtypes.bfloat16)
    low = (matrix - high.astype(np.float64)).astype(ml_dtypes.bfloat16)
    return high, low


def left3(matrix):
    high, low = halves(matrix)
    return np.concatenate([high, low, high], axis=-1)


def right3(matrix):
    high, low = halves(matrix)
    return np.concatenate([high, low, high], axis=-2)


@functools.cache
def tables():
    H = two_scale(POLY_ORDER)
    out = {}
    yz = np.einsum("rtbj,uwck->rutwbcjk", H, H)
    yz = yz.reshape(4, 100, 4, 100)
    par = np.zeros((2, 104, 4, 2, 100))
    for i2 in range(2):
        par[i2, :100, :, i2, :] = yz[0]
    par = par.reshape(208, 800)
    out["par"] = left3(par)
    out["parT"] = left3(par.T.copy())
    full = np.zeros((2, 4, 104, 4, 104))
    full[0, :, :100, :, :100] = yz
    full[1, :, :100, :, 4:] = yz
    full = full.reshape(2, 416, 416)
    out["yz"] = left3(full)
    out["yzT"] = left3(full.transpose(0, 2, 1))
    hx = H.reshape(20, 20)
    kx = np.kron(hx, np.eye(8))
    out["x"] = left3(kx)
    out["xT"] = left3(kx.T.copy())
    out["x0"] = left3(kx[:80])
    out["x0T"] = left3(kx[:80].T.copy())
    mid = np.zeros((4, 104, 2, 2, 104))
    mid[:, :100, :, :, :100] = yz.reshape(4, 100, 2, 2, 100).transpose(0, 1, 3, 2, 4)
    mid = mid.reshape(416, 416)
    out["mid"] = left3(mid)
    out["midT"] = left3(mid.T.copy())
    rx = np.zeros((2, 3, 4, 32, 2, 32, 10))
    for tile in range(3):
        for quarter in range(4 if tile < 2 else 2):
            i = 4 * tile + quarter
            for s in range(32):
                rx[:, tile, quarter, s, :, s, :] = H[:, :, :, i].transpose(2, 0, 1)
    rx = rx.reshape(2, 384, 640)
    out["rx"] = np.stack(halves(rx), 0)
    ex = np.zeros((128, 2, 32, 10))
    for p in range(2):
        for m in range(10):
            ex[p * 10 + m, p, :, m] = 1.0
    out["ex"] = ex.reshape(128, 640).astype(ml_dtypes.bfloat16)
    up = np.zeros((2, 2, 104, 128))
    up[:, :, :100, :100] = yz[0].reshape(100, 2, 2, 100).transpose(1, 2, 3, 0)
    out["up"] = left3(up.reshape(2, 208, 128))
    top = np.zeros((4, 128, 4, 128))
    top[:, :100, :, :100] = yz.transpose(2, 3, 0, 1)
    top = top.reshape(512, 512)
    out["top"] = right3(top)
    out["topT"] = right3(top.T.copy())
    one = np.zeros((2, 16, 2, 16))
    one[:, :10, :, :10] = H
    kt = np.kron(np.eye(8), one.reshape(32, 32))
    out["tx"] = left3(kt)
    out["txT"] = left3(kt.T.copy())
    return out


def split(x):
    high = x.astype(BF16)
    low = (x - high.astype(F32)).astype(BF16)
    return high, low


def dot(a, b):
    return lax.dot_general(a, b, (((1,), (0,)), ((), ())), preferred_element_type=F32)


def dot_t(a, b):
    return lax.dot_general(a, b, (((1,), (1,)), ((), ())), preferred_element_type=F32)


def left_dot(m3, x):
    high, low = split(x)
    return dot(m3, jnp.concatenate([high, high, low], 0))


def right_dot(x, m3):
    high, low = split(x)
    return dot(jnp.concatenate([high, high, low], 1), m3)


def one_hot_dot(x, hot):
    high, low = split(x)
    return dot(high, hot) + dot(low, hot)


def quarter_of(shape):
    return lax.broadcasted_iota(jnp.int32, shape, len(shape) - 1) // 32


def place(pieces, rows):
    mark = quarter_of((rows, 128))
    out = None
    for n, (tile, now) in enumerate(pieces):
        turn = ((n - now) * 32) % 128
        moved = pltpu.roll(tile, turn, 1) if turn else tile
        out = moved if out is None else jnp.where(mark == n, moved, out)
    return out


def vmem(mib):
    return pltpu.CompilerParams(vmem_limit_bytes=mib * 1024 * 1024)


def whole(shape):
    return pl.BlockSpec(shape, lambda *_: (0,) * len(shape))


SMEM = pl.BlockSpec(memory_space=pltpu.SMEM)


def window(ref, pair):
    return ref.at[pair // 5, :, pair % 5]


def parents_kernel(rep_ref, x_ref, par_ref, x0_ref, tgt_ref, b0, b1, b2, b3, xb, acc, pm, sem):
    loads = [pltpu.make_async_copy(window(x_ref, n), xb.at[n], sem.at[n]) for n in range(10)]
    for load in loads[:3]:
        load.start()
    lane = lax.broadcasted_iota(jnp.int32, (256, 256), 1)
    owner_rep = (lane // 64 + rep_ref[0]) % 4
    code = 2 * ((lane % 32) * 4 + owner_rep) + (lane // 32) % 2
    hot = (tgt_ref[...] == code).astype(F32).astype(BF16)
    for n in range(10):
        loads[n].wait()
        if n < 7:
            loads[n + 3].start()
        u = left_dot(par_ref[...], xb[n].reshape(800, 256)).reshape(2, 13, 8, 256)
        acc[:, 2 * n] = u[0]
        acc[:, 2 * n + 1] = u[1]
    for t in range(13):
        v = left_dot(x0_ref[...], acc[t].reshape(160, 256))
        pm[:, 8 * t : 8 * t + 8, :] = v.reshape(10, 8, 256)
    y = one_hot_dot(pm[...].reshape(1040, 256), hot).reshape(10, 104, 256)
    for o, out in enumerate((b0, b1, b2, b3)):
        tile = y[:, :, (o // 2) * 128 : (o // 2) * 128 + 128]
        base = (o % 2) * 2
        for s in range(2):
            for q in range(2):
                out[:, (2 * s + q) * 128 : (2 * s + q + 1) * 128] = place(
                    [(tile[4 * q + n], base + s) for n in range(4)], 104
                )
        out[:, 512:640] = place(
            [(tile[8], base), (tile[9], base), (tile[8], base + 1), (tile[9], base + 1)], 104
        )


VMEM = pl.BlockSpec(memory_space=pltpu.VMEM)
ANY = pl.BlockSpec(memory_space=pl.ANY)
BLOCK = jax.ShapeDtypeStruct((104, 640), F32)


def parents_call(x5, rep, target):
    T = tables()
    return pl.pallas_call(
        parents_kernel,
        in_specs=[SMEM, ANY, VMEM, VMEM, VMEM],
        out_specs=[VMEM] * 4,
        out_shape=[BLOCK] * 4,
        scratch_shapes=[
            pltpu.VMEM((10, 4, 200, 256), F32),
            pltpu.VMEM((13, 20, 8, 256), F32),
            pltpu.VMEM((10, 104, 256), F32),
            pltpu.SemaphoreType.DMA((10,)),
        ],
        compiler_params=vmem(60),
        cost_estimate=pl.CostEstimate(flops=2 * 10**9, bytes_accessed=10**7, transcendentals=0),
        name="parents",
    )(rep, x5, T["par"], T["x0"], target)


def details_kernel(x_ref, yz_ref, x1_ref, xt_ref, g_ref, o_ref, xb, acc, acc2, sem, osem):
    loads = [pltpu.make_async_copy(window(x_ref, n), xb.at[n], sem.at[n]) for n in range(10)]
    for load in loads[:3]:
        load.start()
    for n in range(10):
        loads[n].wait()
        if n < 7:
            loads[n + 3].start()
        for i2 in range(2):
            w = xb[n, :, 96 * i2 : 96 * i2 + 104, :].reshape(416, 256)
            acc[:, 2 * n + i2] = left_dot(yz_ref[i2], w).reshape(52, 8, 256)

    def store(p):
        part = pl.ds(13 * p, 13)
        return pltpu.make_async_copy(acc2.at[part], o_ref.at[part], osem.at[p])

    def quarter(p, carry):
        for n in range(13):
            t = 13 * p + n
            v = left_dot(x1_ref[...], acc[t].reshape(160, 256))
            v = v * jnp.broadcast_to(g_ref[p][:, n : n + 1], (160, 256))
            acc2[t] = left_dot(xt_ref[...], v).reshape(20, 8, 256)
        store(p).start()
        return carry

    lax.fori_loop(0, 4, quarter, 0)
    for p in range(4):
        store(p).wait()


def details_call(x5, gain):
    T = tables()
    return pl.pallas_call(
        details_kernel,
        in_specs=[ANY, VMEM, VMEM, VMEM, VMEM],
        out_specs=ANY,
        out_shape=jax.ShapeDtypeStruct((52, 20, 8, 256), F32),
        scratch_shapes=[
            pltpu.VMEM((10, 4, 200, 256), F32),
            pltpu.VMEM((52, 20, 8, 256), F32),
            pltpu.VMEM((52, 20, 8, 256), F32),
            pltpu.SemaphoreType.DMA((10,)),
            pltpu.SemaphoreType.DMA((4,)),
        ],
        compiler_params=vmem(60),
        cost_estimate=pl.CostEstimate(
            flops=15 * 10**9, bytes_accessed=2 * 10**7, transcendentals=0
        ),
        name="details",
    )(x5, T["yz"], T["x"], T["xT"], gain)


def middle_kernel(
    rep_ref, b0, b1, b2, b3, rx_ref, mid_ref, midt_ref, g_ref, ex_ref,
    p_ref, d0, d1, d2, d3, got, back,
):
    rep = rep_ref[0]
    for o, b in enumerate((b0, b1, b2, b3)):
        got[(rep + 4 - o) % 4] = b[...]
    high_rx, low_rx = rx_ref[0].reshape(768, 640), rx_ref[1].reshape(768, 640)
    rows = []
    for s in range(2):
        for by in range(2):
            parts = []
            for bx in range(2):
                r = 2 * bx + by
                last = got[r, :, 512:640]
                parts += [
                    got[r, :, 256 * s : 256 * s + 256],
                    pltpu.roll(last, 64, 1) if s else last,
                ]
            rows.append(jnp.concatenate(parts, 1))
    x = jnp.concatenate(rows, 0)
    high, low = split(x)
    u = dot(high, high_rx) + dot(low, high_rx) + dot(high, low_rx)
    v = left_dot(mid_ref[...], u)
    p_ref[...] = jnp.transpose(v[0:128, 0:384])[0:320].reshape(8, 40, 128)
    gh, gl = split(g_ref[...])
    gm, gl = gl, (g_ref[...] - gh.astype(F32) - gl.astype(F32)).astype(BF16)
    gain = dot(gh, ex_ref[...]) + dot(gm, ex_ref[...]) + dot(gl, ex_ref[...])
    w = left_dot(midt_ref[...], v * gain)
    high, low = split(w)
    z = dot_t(high, high_rx) + dot_t(low, high_rx) + dot_t(high, low_rx)
    for by in range(2):
        for bx in range(2):
            r = 2 * bx + by
            for s in range(2):
                base = (2 * s + by) * 104
                back[r, :, 256 * s : 256 * s + 256] = z[
                    base : base + 104, 384 * bx : 384 * bx + 256
                ]
            last = [
                z[(2 * s + by) * 104 : (2 * s + by) * 104 + 104, 384 * bx + 256 : 384 * bx + 384]
                for s in range(2)
            ]
            back[r, :, 512:640] = last[0] + pltpu.roll(last[1], 64, 1)
    for o, d in enumerate((d0, d1, d2, d3)):
        d[...] = back[(rep + o) % 4]


def middle_call(blocks, rep, gain):
    T = tables()
    block = jax.ShapeDtypeStruct((104, 640), F32)
    return pl.pallas_call(
        middle_kernel,
        in_specs=[SMEM] + [pl.BlockSpec(memory_space=pltpu.VMEM)] * 9,
        out_specs=[pl.BlockSpec(memory_space=pltpu.VMEM)] * 5,
        out_shape=[jax.ShapeDtypeStruct((8, 40, 128), F32)] + [block] * 4,
        scratch_shapes=[pltpu.VMEM((4, 104, 640), F32), pltpu.VMEM((4, 104, 640), F32)],
        compiler_params=vmem(60),
        name="middle",
    )(rep, *blocks, T["rx"], T["mid"], T["midT"], gain, T["ex"])


def gather_kernel(slab_ref, way_ref, out_ref, ways_ref, own_sem, send, recv, fsend, frecv, wsend, wrecv):
    leaf = lax.axis_index("leaf")
    rep = lax.axis_index("rep")
    core = leaf % 2
    me = leaf // 2
    sibling = leaf + 1 - 2 * core
    barrier = pltpu.get_barrier_semaphore()

    def greet(k, carry):
        other = 2 * ((me + k) % 16) + core
        pl.semaphore_signal(barrier, inc=1, device_id=(other, rep), device_id_type=MESH)
        return carry

    lax.fori_loop(1, 16, greet, 0)
    pl.semaphore_signal(barrier, inc=1, device_id=(sibling, rep), device_id_type=MESH)
    first, turn = 4 * (leaf // 4), leaf % 4
    across = first + (sibling + 2) % 4
    pl.semaphore_signal(barrier, inc=1, device_id=(across, rep), device_id_type=MESH)
    own = pltpu.make_async_copy(slab_ref.at[me // 2], out_ref.at[leaf], own_sem.at[0])
    own.start()
    own_way = pltpu.make_async_copy(way_ref, ways_ref.at[turn], own_sem.at[1])
    own_way.start()
    pl.semaphore_wait(barrier, 17)

    def way_copy(k, slot):
        return pltpu.make_async_remote_copy(
            src_ref=way_ref,
            dst_ref=ways_ref.at[slot],
            send_sem=wsend.at[k],
            recv_sem=wrecv.at[k],
            device_id=(first + (turn + k) % 4, rep),
            device_id_type=MESH,
        )

    for k in range(1, 4):
        way_copy(k, turn).start()

    def out_copy(k):
        to = (me + k) % 16
        return pltpu.make_async_remote_copy(
            src_ref=slab_ref.at[to // 2],
            dst_ref=out_ref.at[leaf],
            send_sem=send.at[k],
            recv_sem=recv.at[k],
            device_id=(2 * to + core, rep),
            device_id_type=MESH,
        )

    def in_copy(k):
        slot = 2 * ((me + 16 - k) % 16) + core
        return pltpu.make_async_remote_copy(
            src_ref=slab_ref.at[0],
            dst_ref=out_ref.at[slot],
            send_sem=send.at[k],
            recv_sem=recv.at[k],
            device_id=(leaf, rep),
            device_id_type=MESH,
        )

    def pass_copy(k, which):
        slot = 2 * ((me + 16 - k) % 16) + which
        return pltpu.make_async_remote_copy(
            src_ref=out_ref.at[slot],
            dst_ref=out_ref.at[slot],
            send_sem=fsend.at[k],
            recv_sem=frecv.at[k],
            device_id=(sibling, rep),
            device_id_type=MESH,
        )

    def begin(k, carry):
        out_copy(k).start()
        return carry

    lax.fori_loop(1, 16, begin, 0)
    own.wait()
    pass_copy(0, core).start()

    def relay(k, carry):
        in_copy(k).wait_recv()
        pass_copy(k, core).start()
        return carry

    lax.fori_loop(1, 16, relay, 0)

    def finish(k, carry):
        pass_copy(k, 1 - core).wait_recv()
        pass_copy(k, core).wait_send()
        return carry

    lax.fori_loop(0, 16, finish, 0)

    def sent(k, carry):
        out_copy(k).wait_send()
        return carry

    lax.fori_loop(1, 16, sent, 0)
    for k in range(1, 4):
        way_copy(k, (turn + 4 - k) % 4).wait_recv()
        way_copy(k, turn).wait_send()
    own_way.wait()


def gather_call(slabs, way):
    return pl.pallas_call(
        gather_kernel,
        in_specs=[ANY, ANY],
        out_specs=[ANY, ANY],
        out_shape=[
            jax.ShapeDtypeStruct((32, 40, 128), F32),
            jax.ShapeDtypeStruct((4, 8, 128), jnp.int32),
        ],
        scratch_shapes=[
            pltpu.SemaphoreType.DMA((2,)),
            pltpu.SemaphoreType.DMA((16,)),
            pltpu.SemaphoreType.DMA((16,)),
            pltpu.SemaphoreType.DMA((16,)),
            pltpu.SemaphoreType.DMA((16,)),
            pltpu.SemaphoreType.DMA((4,)),
            pltpu.SemaphoreType.DMA((4,)),
        ],
        compiler_params=pltpu.CompilerParams(
            collective_id=1, has_side_effects=True, vmem_limit_bytes=60 * 1024 * 1024
        ),
        name="to_top",
    )(slabs, way)


def top_kernel(
    route_ref, turn_ref, g_ref, top_ref, tx_ref, txt_ref, topt_ref, gain_ref,
    p_ref, c_ref, kids,
):
    kids[...] = jnp.zeros_like(kids)

    def scatter(l, carry):
        for t in range(4):
            code = route_ref[t, 0, l]
            kids[(code // 2) * 8 + t * 2 + code % 2, 0:10, :] = g_ref[l, 10 * t : 10 * t + 10, :]
        return carry

    lax.fori_loop(0, 32, scatter, 0)
    for g in range(4):
        sets = kids[64 * g : 64 * g + 64].reshape(8, 2, 4, 16, 128)
        y = jnp.concatenate([sets[:, :, b].reshape(256, 128) for b in range(4)], 1)
        z = right_dot(y, top_ref[...])
        v = left_dot(tx_ref[...], z)
        c_ref[8 * g : 8 * g + 8] = v.reshape(8, 2, 16, 512)[:, 0, :, 0:128]
        v = (v.reshape(8, 32, 512) * gain_ref[...][None]).reshape(256, 512)
        z = left_dot(txt_ref[...], v)
        y = right_dot(z, topt_ref[...])
        for l in range(8):
            for b in range(4):
                for bx in range(2):
                    kids[64 * g + 8 * l + 4 * bx + b] = y[
                        32 * l + 16 * bx : 32 * l + 16 * bx + 16, 128 * b : 128 * b + 128
                    ]

    def pick(n, carry):
        for t in range(4):
            code = route_ref[t, 0, 4 * n + turn_ref[0]]
            p_ref[n, 10 * t : 10 * t + 10, :] = kids[(code // 2) * 8 + t * 2 + code % 2, 0:10, :]
        return carry

    lax.fori_loop(0, 8, pick, 0)


def top_call(routes, turn, got, gain):
    T = tables()
    return pl.pallas_call(
        top_kernel,
        in_specs=[SMEM, SMEM] + [pl.BlockSpec(memory_space=pltpu.VMEM)] * 6,
        out_specs=[pl.BlockSpec(memory_space=pltpu.VMEM)] * 2,
        out_shape=[
            jax.ShapeDtypeStruct((8, 40, 128), F32),
            jax.ShapeDtypeStruct((32, 16, 128), F32),
        ],
        scratch_shapes=[pltpu.VMEM((256, 16, 128), F32)],
        compiler_params=vmem(60),
        name="top",
    )(routes, turn, got, T["top"], T["tx"], T["txT"], T["topT"], gain)


def spread_kernel(slab_ref, top_ref, out_ref, coarse_ref, own_sem, send, recv, csend, crecv):
    leaf = lax.axis_index("leaf")
    rep = lax.axis_index("rep")
    turn = leaf % 4
    group = leaf // 4
    me = group * 4 + rep
    barrier = pltpu.get_barrier_semaphore()

    def greet(k, carry):
        to = (me + k) % 32
        pl.semaphore_signal(
            barrier, inc=1, device_id=(4 * (to // 4) + turn, to % 4), device_id_type=MESH
        )
        return carry

    lax.fori_loop(1, 32, greet, 0)
    own = pltpu.make_async_copy(slab_ref.at[group], out_ref.at[me], own_sem.at[0])
    own.start()
    own_top = pltpu.make_async_copy(top_ref.at[leaf], coarse_ref.at[group], own_sem.at[1])
    own_top.start()
    pl.semaphore_wait(barrier, 31)

    def out_copy(k):
        to = (me + k) % 32
        return pltpu.make_async_remote_copy(
            src_ref=slab_ref.at[to // 4],
            dst_ref=out_ref.at[me],
            send_sem=send.at[k],
            recv_sem=recv.at[k],
            device_id=(4 * (to // 4) + turn, to % 4),
            device_id_type=MESH,
        )

    def in_copy(k):
        return pltpu.make_async_remote_copy(
            src_ref=slab_ref.at[0],
            dst_ref=out_ref.at[(me + 32 - k) % 32],
            send_sem=send.at[k],
            recv_sem=recv.at[k],
            device_id=(leaf, rep),
            device_id_type=MESH,
        )

    def out_top(k):
        to = 4 * ((group + k) % 8) + turn
        return pltpu.make_async_remote_copy(
            src_ref=top_ref.at[to],
            dst_ref=coarse_ref.at[group],
            send_sem=csend.at[k],
            recv_sem=crecv.at[k],
            device_id=(to, rep),
            device_id_type=MESH,
        )

    def in_top(k):
        return pltpu.make_async_remote_copy(
            src_ref=top_ref.at[0],
            dst_ref=coarse_ref.at[(group + 8 - k) % 8],
            send_sem=csend.at[k],
            recv_sem=crecv.at[k],
            device_id=(leaf, rep),
            device_id_type=MESH,
        )

    def begin(k, carry):
        out_copy(k).start()
        return carry

    def begin_top(k, carry):
        out_top(k).start()
        return carry

    lax.fori_loop(1, 32, begin, 0)
    lax.fori_loop(1, 8, begin_top, 0)

    def finish(k, carry):
        in_copy(k).wait_recv()
        out_copy(k).wait_send()
        return carry

    def finish_top(k, carry):
        in_top(k).wait_recv()
        out_top(k).wait_send()
        return carry

    lax.fori_loop(1, 32, finish, 0)
    lax.fori_loop(1, 8, finish_top, 0)
    own.wait()
    own_top.wait()


def spread_call(slabs, tops):
    return pl.pallas_call(
        spread_kernel,
        in_specs=[ANY] * 2,
        out_specs=[ANY] * 2,
        out_shape=[
            jax.ShapeDtypeStruct((32, 40, 128), F32),
            jax.ShapeDtypeStruct((8, 16, 128), F32),
        ],
        scratch_shapes=[
            pltpu.SemaphoreType.DMA((2,)),
            pltpu.SemaphoreType.DMA((32,)),
            pltpu.SemaphoreType.DMA((32,)),
            pltpu.SemaphoreType.DMA((8,)),
            pltpu.SemaphoreType.DMA((8,)),
        ],
        compiler_params=pltpu.CompilerParams(
            collective_id=2, has_side_effects=True, vmem_limit_bytes=60 * 1024 * 1024
        ),
        name="from_top",
    )(slabs, tops)


def final_kernel(
    rep_ref, slab_ref, d0, d1, d2, d3, up_ref, rx_ref, tgt_ref, x0t_ref, yzt_ref, z_ref, live_ref,
    o_ref, got, ypos, pnew, big, ob, sem, osem,
):
    loads = [
        pltpu.make_async_copy(
            z_ref.at[pl.ds(13 * p, 13)], big.at[pl.ds(13 * p, 13)], sem.at[p]
        )
        for p in range(4)
    ]
    for load in loads:
        load.start()
    rep = rep_ref[0]
    by, bx = rep % 2, rep // 2
    for o, d in enumerate((d0, d1, d2, d3)):
        got[(rep + 4 - o) % 4] = d[...]
    mine = slab_ref[...].reshape(8, 4, 40, 128)
    cols = []
    for r in range(4):
        rows = mine[:, r].reshape(320, 128)
        rows = jnp.concatenate([rows, jnp.zeros((64, 128), F32)], 0)
        cols.append(jnp.transpose(rows))
    tall = left_dot(up_ref[by], jnp.concatenate(cols, 1))
    stack = jnp.concatenate(
        [tall[104 * s : 104 * s + 104, 384 * r : 384 * r + 384] for r in range(4) for s in range(2)],
        0,
    )
    high, low = split(stack)
    hi_rx = rx_ref[0, bx][:, 0:384]
    lo_rx = rx_ref[1, bx][:, 0:384]
    f = dot_t(high, hi_rx) + dot_t(low, hi_rx) + dot_t(high, lo_rx)
    for r in range(4):
        for s in range(2):
            base = (2 * r + s) * 104
            got[r, :, 256 * s : 256 * s + 256] += f[base : base + 104, 0:256]
        got[r, :, 512:640] += f[2 * r * 104 : 2 * r * 104 + 104, 256:384] + pltpu.roll(
            f[(2 * r + 1) * 104 : (2 * r + 2) * 104, 256:384], 64, 1
        )
    for i in range(10):
        for pair in range(2):
            pieces = []
            for r in (2 * pair, 2 * pair + 1):
                for s in range(2):
                    if i < 8:
                        tile = 2 * s + i // 4
                        now = i % 4
                    else:
                        tile = 4
                        now = 2 * s + i - 8
                    pieces.append((got[r, :, 128 * tile : 128 * tile + 128], now))
            ypos[i, :, 128 * pair : 128 * pair + 128] = place(pieces, 104)
    row = lax.broadcasted_iota(jnp.int32, (256, 256), 0)
    code = 2 * ((row % 32) * 4 + row // 64) + (row // 32) % 2
    hot = (tgt_ref[...] == code).astype(F32).astype(BF16)
    pnew[...] = one_hot_dot(ypos[...].reshape(1040, 256), hot).reshape(10, 104, 256)
    loads[0].wait()
    for t in range(13):
        w = pnew[:, 8 * t : 8 * t + 8, :].reshape(80, 256)
        big[t] += left_dot(x0t_ref[...], w).reshape(20, 8, 256)
    for load in loads[1:]:
        load.wait()
    live = jnp.broadcast_to(live_ref[...][None] > 0, (4, 104, 256))
    stores = []
    for n in range(10):
        z = []
        for i2 in range(2):
            w = big[:, 2 * n + i2].reshape(416, 256)
            z.append(jnp.where(live, left_dot(yzt_ref[i2], w).reshape(4, 104, 256), 0.0))
        ob[n, :, 0:96, :] = z[0][:, 0:96]
        ob[n, :, 96:104, :] = z[0][:, 96:104] + z[1][:, 0:8]
        ob[n, :, 104:200, :] = z[1][:, 8:104]
        store = pltpu.make_async_copy(ob.at[n], window(o_ref, n), osem.at[n])
        store.start()
        stores.append(store)
    for store in stores:
        store.wait()


def final_call(rep, slabs, blocks, target, z, live):
    T = tables()
    return pl.pallas_call(
        final_kernel,
        in_specs=[SMEM] + [VMEM] * 10 + [ANY, VMEM],
        out_specs=ANY,
        out_shape=jax.ShapeDtypeStruct((2, 4, 5, 200, 256), F32),
        scratch_shapes=[
            pltpu.VMEM((4, 104, 640), F32),
            pltpu.VMEM((10, 104, 256), F32),
            pltpu.VMEM((10, 104, 256), F32),
            pltpu.VMEM((52, 20, 8, 256), F32),
            pltpu.VMEM((10, 4, 200, 256), F32),
            pltpu.SemaphoreType.DMA((4,)),
            pltpu.SemaphoreType.DMA((10,)),
        ],
        compiler_params=vmem(60),
        name="final",
    )(rep, slabs, *blocks, T["up"], T["rx"], target, T["x0T"], T["yzT"], z, live)


def gain_cube(row):
    cube = jnp.concatenate([jnp.zeros((1000,), F32), row]).reshape(2, 4, 10, 100)
    return jnp.pad(cube, ((0, 0), (0, 0), (0, 0), (0, 4)))


def finest_gain(row):
    cube = gain_cube(row).reshape(2, 4, 10, 13, 8).transpose(1, 0, 2, 4, 3).reshape(4, 160, 13)
    return jnp.pad(cube, ((0, 0), (0, 0), (0, 115)))


def middle_gain(row):
    cube = gain_cube(row).transpose(1, 3, 0, 2).reshape(416, 20)
    return jnp.pad(cube, ((0, 0), (0, 108)))


def top_gain(row):
    cube = jnp.concatenate([jnp.ones((1000,), F32), row]).reshape(2, 4, 10, 100)
    cube = jnp.pad(cube, ((0, 0), (0, 0), (0, 6), (0, 28)))
    return cube.transpose(0, 2, 1, 3).reshape(32, 512)


def swap(blocks):
    out = [blocks[0]]
    for o in range(1, 4):
        out.append(lax.ppermute(blocks[o], "rep", [(r, (r + o) % 4) for r in range(4)]))
    return out


def shards(fine_coeffs, set_counts, route_first, route_top, level_gain):
    leaf = lax.axis_index("leaf")
    rep = lax.axis_index("rep").reshape(1).astype(jnp.int32)
    living = lax.iota(jnp.int32, 256) < set_counts[0]
    target = jnp.where(living, route_first, -1)
    live = living.astype(F32).reshape(1, 256)
    way = jnp.pad(route_top.reshape(1, 32), ((0, 7), (0, 96)))
    turn = (leaf % 4).reshape(1).astype(jnp.int32)
    x5 = fine_coeffs.reshape(2, 4, 5, 200, 256)
    blocks = parents_call(x5, rep, target.reshape(256, 1))
    blocks = swap(blocks)
    z = details_call(x5, finest_gain(level_gain[0]))
    z, *blocks = lax.optimization_barrier((z, *blocks))
    mids = middle_call(blocks, rep, middle_gain(level_gain[1]))
    back = swap(mids[1:])
    got, routes = gather_call(mids[0], way)
    slabs, tops = top_call(routes, turn, got, top_gain(level_gain[2]))
    new, coarse = spread_call(slabs, tops)
    out = final_call(rep, new, back, target.reshape(1, 256), z, live)
    coarse = coarse[:, :10, :100].reshape(8, 1000).T
    return (out.reshape(8000, 256), coarse)


def solution(mesh):
    placed = (
        P(None, ("leaf", "rep")),
        P(("leaf", "rep")),
        P(("leaf", "rep")),
        P(("leaf", "rep")),
        P(),
    )
    return jax.shard_map(
        shards,
        mesh=mesh,
        in_specs=placed,
        out_specs=(P(None, ("leaf", "rep")), P(None, ("leaf", "rep"))),
        check_vma=False,
    )
```

```python
import functools
import math

import jax
import jax.numpy as jnp
import ml_dtypes
import numpy as np
from jax import lax
from jax.experimental import pallas as pl
from jax.experimental.pallas import tpu as pltpu
from jax.sharding import PartitionSpec as P

POLY_ORDER = 10
F32 = jnp.float32
BF16 = jnp.bfloat16
MESH = pl.DeviceIdType.MESH


def legendre_pair(count, position):
    before, current = (1.0, position)
    for degree in range(1, count):
        before, current = (
            current,
            ((2 * degree + 1) * position * current - degree * before) / (degree + 1),
        )
    derivative = count * (position * current - before) / (position * position - 1.0)
    return (current, derivative)


def gauss_points(count):
    nodes = []
    weights = []
    for node_index in range(count):
        estimate = math.cos(math.pi * (node_index + 0.75) / (count + 0.5))
        for newton_step in range(100):
            current, derivative = legendre_pair(count, estimate)
            estimate = estimate - current / derivative
        current, derivative = legendre_pair(count, estimate)
        nodes.append(estimate)
        weights.append(2.0 / ((1.0 - estimate * estimate) * derivative * derivative))
    return (np.array(nodes), np.array(weights))


def legendre_rows(degree_count, points):
    values = [points * 0.0 + 1.0, points.copy()]
    for degree in range(1, degree_count - 1):
        values.append(
            ((2 * degree + 1) * points * values[degree] - degree * values[degree - 1])
            / (degree + 1)
        )
    return np.stack(
        [np.sqrt(2.0 * degree + 1.0) * values[degree] for degree in range(degree_count)]
    )


@functools.cache
def two_scale(poly_order):
    points, weights = gauss_points(2 * poly_order)
    lower_half = (points + 1.0) / 4.0
    half_weights = weights / 4.0
    child_rows = legendre_rows(poly_order, 4.0 * lower_half - 1.0)
    parent_low = legendre_rows(poly_order, 2.0 * lower_half - 1.0)
    parent_high = legendre_rows(poly_order, 2.0 * (lower_half + 0.5) - 1.0)
    filter_left = math.sqrt(2.0) * (parent_low * half_weights) @ child_rows.T
    filter_right = math.sqrt(2.0) * (parent_high * half_weights) @ child_rows.T
    basis_rows = list(np.concatenate([filter_left, filter_right], axis=1))
    units = np.eye(2 * poly_order)
    for step_index in range(poly_order):
        residuals = []
        for vector in units:
            for sweep in range(2):
                for previous in basis_rows:
                    vector = vector - np.dot(previous, vector) * previous
            residuals.append(vector)
        lengths = np.array([np.sqrt(np.dot(vector, vector)) for vector in residuals])
        chosen = int(np.argmax(lengths))
        basis_rows.append(residuals[chosen] / lengths[chosen])
    filters = np.array(basis_rows).reshape(2, poly_order, 2, poly_order)
    return filters.astype(np.float32).astype(np.float64)


def halves(matrix):
    high = matrix.astype(ml_dtypes.bfloat16)
    low = (matrix - high.astype(np.float64)).astype(ml_dtypes.bfloat16)
    return high, low


def left3(matrix):
    high, low = halves(matrix)
    return np.concatenate([high, low, high], axis=-1)


def right3(matrix):
    high, low = halves(matrix)
    return np.concatenate([high, low, high], axis=-2)


@functools.cache
def tables():
    H = two_scale(POLY_ORDER)
    out = {}
    yz = np.einsum("rtbj,uwck->rutwbcjk", H, H)
    yz = yz.reshape(4, 100, 4, 100)
    par = np.zeros((2, 104, 4, 2, 100))
    for i2 in range(2):
        par[i2, :100, :, i2, :] = yz[0]
    par = par.reshape(208, 800)
    out["par"] = left3(par)
    out["parT"] = left3(par.T.copy())
    full = np.zeros((2, 4, 104, 4, 104))
    full[0, :, :100, :, :100] = yz
    full[1, :, :100, :, 4:] = yz
    full = full.reshape(2, 416, 416)
    out["yz"] = left3(full)
    out["yzT"] = left3(full.transpose(0, 2, 1))
    hx = H.reshape(20, 20)
    kx = np.kron(hx, np.eye(8))
    out["x"] = left3(kx)
    out["xT"] = left3(kx.T.copy())
    out["x0"] = left3(kx[:80])
    out["x0T"] = left3(kx[:80].T.copy())
    mid = np.zeros((4, 104, 2, 2, 104))
    mid[:, :100, :, :, :100] = yz.reshape(4, 100, 2, 2, 100).transpose(0, 1, 3, 2, 4)
    mid = mid.reshape(416, 416)
    out["mid"] = left3(mid)
    out["midT"] = left3(mid.T.copy())
    rx = np.zeros((2, 3, 4, 32, 2, 32, 10))
    for tile in range(3):
        for quarter in range(4 if tile < 2 else 2):
            i = 4 * tile + quarter
            for s in range(32):
                rx[:, tile, quarter, s, :, s, :] = H[:, :, :, i].transpose(2, 0, 1)
    rx = rx.reshape(2, 384, 640)
    out["rx"] = np.stack(halves(rx), 0)
    ex = np.zeros((128, 2, 32, 10))
    for p in range(2):
        for m in range(10):
            ex[p * 10 + m, p, :, m] = 1.0
    out["ex"] = ex.reshape(128, 640).astype(ml_dtypes.bfloat16)
    up = np.zeros((2, 2, 104, 128))
    up[:, :, :100, :100] = yz[0].reshape(100, 2, 2, 100).transpose(1, 2, 3, 0)
    out["up"] = left3(up.reshape(2, 208, 128))
    top = np.zeros((4, 128, 4, 128))
    top[:, :100, :, :100] = yz.transpose(2, 3, 0, 1)
    top = top.reshape(512, 512)
    out["top"] = right3(top)
    out["topT"] = right3(top.T.copy())
    one = np.zeros((2, 16, 2, 16))
    one[:, :10, :, :10] = H
    kt = np.kron(np.eye(8), one.reshape(32, 32))
    out["tx"] = left3(kt)
    out["txT"] = left3(kt.T.copy())
    return out


def split(x):
    high = x.astype(BF16)
    low = (x - high.astype(F32)).astype(BF16)
    return high, low


def dot(a, b):
    return lax.dot_general(a, b, (((1,), (0,)), ((), ())), preferred_element_type=F32)


def dot_t(a, b):
    return lax.dot_general(a, b, (((1,), (1,)), ((), ())), preferred_element_type=F32)


def left_dot(m3, x):
    high, low = split(x)
    return dot(m3, jnp.concatenate([high, high, low], 0))


def right_dot(x, m3):
    high, low = split(x)
    return dot(jnp.concatenate([high, high, low], 1), m3)


def one_hot_dot(x, hot):
    high, low = split(x)
    return dot(high, hot) + dot(low, hot)


def quarter_of(shape):
    return lax.broadcasted_iota(jnp.int32, shape, len(shape) - 1) // 32


def place(pieces, rows):
    mark = quarter_of((rows, 128))
    out = None
    for n, (tile, now) in enumerate(pieces):
        turn = ((n - now) * 32) % 128
        moved = pltpu.roll(tile, turn, 1) if turn else tile
        out = moved if out is None else jnp.where(mark == n, moved, out)
    return out


def vmem(mib):
    return pltpu.CompilerParams(vmem_limit_bytes=mib * 1024 * 1024)


def whole(shape):
    return pl.BlockSpec(shape, lambda *_: (0,) * len(shape))


SMEM = pl.BlockSpec(memory_space=pltpu.SMEM)


def window(ref, pair):
    return ref.at[pair // 5, :, pair % 5]


def parents_kernel(rep_ref, x_ref, par_ref, x0_ref, tgt_ref, b0, b1, b2, b3, xb, acc, pm, sem):
    loads = [pltpu.make_async_copy(window(x_ref, n), xb.at[n], sem.at[n]) for n in range(10)]
    for load in loads[:3]:
        load.start()
    lane = lax.broadcasted_iota(jnp.int32, (256, 256), 1)
    owner_rep = (lane // 64 + rep_ref[0]) % 4
    code = 2 * ((lane % 32) * 4 + owner_rep) + (lane // 32) % 2
    hot = (tgt_ref[...] == code).astype(F32).astype(BF16)
    for n in range(10):
        loads[n].wait()
        if n < 7:
            loads[n + 3].start()
        u = left_dot(par_ref[...], xb[n].reshape(800, 256)).reshape(2, 13, 8, 256)
        acc[:, 2 * n] = u[0]
        acc[:, 2 * n + 1] = u[1]
    for t in range(13):
        v = left_dot(x0_ref[...], acc[t].reshape(160, 256))
        pm[:, 8 * t : 8 * t + 8, :] = v.reshape(10, 8, 256)
    y = one_hot_dot(pm[...].reshape(1040, 256), hot).reshape(10, 104, 256)
    for o, out in enumerate((b0, b1, b2, b3)):
        tile = y[:, :, (o // 2) * 128 : (o // 2) * 128 + 128]
        base = (o % 2) * 2
        for s in range(2):
            for q in range(2):
                out[:, (2 * s + q) * 128 : (2 * s + q + 1) * 128] = place(
                    [(tile[4 * q + n], base + s) for n in range(4)], 104
                )
        out[:, 512:640] = place(
            [(tile[8], base), (tile[9], base), (tile[8], base + 1), (tile[9], base + 1)], 104
        )


VMEM = pl.BlockSpec(memory_space=pltpu.VMEM)
ANY = pl.BlockSpec(memory_space=pl.ANY)
BLOCK = jax.ShapeDtypeStruct((104, 640), F32)


def parents_call(x5, rep, target):
    T = tables()
    return pl.pallas_call(
        parents_kernel,
        in_specs=[SMEM, ANY, VMEM, VMEM, VMEM],
        out_specs=[VMEM] * 4,
        out_shape=[BLOCK] * 4,
        scratch_shapes=[
            pltpu.VMEM((10, 4, 200, 256), F32),
            pltpu.VMEM((13, 20, 8, 256), F32),
            pltpu.VMEM((10, 104, 256), F32),
            pltpu.SemaphoreType.DMA((10,)),
        ],
        compiler_params=vmem(60),
        cost_estimate=pl.CostEstimate(flops=2 * 10**9, bytes_accessed=10**7, transcendentals=0),
        name="parents",
    )(rep, x5, T["par"], T["x0"], target)


def details_kernel(x_ref, yz_ref, x1_ref, xt_ref, g_ref, o_ref, xb, acc, acc2, sem, osem):
    loads = [pltpu.make_async_copy(window(x_ref, n), xb.at[n], sem.at[n]) for n in range(10)]
    for load in loads[:3]:
        load.start()
    for n in range(10):
        loads[n].wait()
        if n < 7:
            loads[n + 3].start()
        for i2 in range(2):
            w = xb[n, :, 96 * i2 : 96 * i2 + 104, :].reshape(416, 256)
            acc[:, 2 * n + i2] = left_dot(yz_ref[i2], w).reshape(52, 8, 256)

    def store(p):
        part = pl.ds(13 * p, 13)
        return pltpu.make_async_copy(acc2.at[part], o_ref.at[part], osem.at[p])

    def quarter(p, carry):
        for n in range(13):
            t = 13 * p + n
            v = left_dot(x1_ref[...], acc[t].reshape(160, 256))
            v = v * jnp.broadcast_to(g_ref[p][:, n : n + 1], (160, 256))
            acc2[t] = left_dot(xt_ref[...], v).reshape(20, 8, 256)
        store(p).start()
        return carry

    lax.fori_loop(0, 4, quarter, 0)
    for p in range(4):
        store(p).wait()


def details_call(x5, gain):
    T = tables()
    return pl.pallas_call(
        details_kernel,
        in_specs=[ANY, VMEM, VMEM, VMEM, VMEM],
        out_specs=ANY,
        out_shape=jax.ShapeDtypeStruct((52, 20, 8, 256), F32),
        scratch_shapes=[
            pltpu.VMEM((10, 4, 200, 256), F32),
            pltpu.VMEM((52, 20, 8, 256), F32),
            pltpu.VMEM((52, 20, 8, 256), F32),
            pltpu.SemaphoreType.DMA((10,)),
            pltpu.SemaphoreType.DMA((4,)),
        ],
        compiler_params=vmem(60),
        cost_estimate=pl.CostEstimate(
            flops=15 * 10**9, bytes_accessed=2 * 10**7, transcendentals=0
        ),
        name="details",
    )(x5, T["yz"], T["x"], T["xT"], gain)


def core_kernel(
    b0, b1, b2, b3, way_ref, g1_ref, g2_ref, rx_hbm, mid_hbm, midt_hbm, ex_hbm, top_hbm, tx_hbm,
    txt_hbm, topt_hbm,
    out_ref, coarse_ref, back_ref,
    rx_ref, mid_ref, midt_ref, ex_ref, top_ref, tx_ref, txt_ref, topt_ref,
    got, back, slab, g_ref, ways, inv, kids, tops, news, ways_s, inv_s,
    csem, bsem, own_sem, send, recv, fsend, frecv, wsend, wrecv, zsend, zrecv,
    psend, precv, tsend, trecv,
):
    leaf = lax.axis_index("leaf")
    rep = lax.axis_index("rep")
    core = leaf % 2
    half = leaf // 2
    sibling = leaf + 1 - 2 * core
    turn = leaf % 4
    group = leaf // 4
    first = 4 * group
    across = first + (sibling + 2) % 4
    spot = group * 4 + rep
    barrier = pltpu.get_barrier_semaphore()

    def greet_core(k, carry):
        other = 2 * ((half + k) % 16) + core
        pl.semaphore_signal(barrier, inc=1, device_id=(other, rep), device_id_type=MESH)
        return carry

    def greet_turn(k, carry):
        to = (spot + k) % 32
        pl.semaphore_signal(
            barrier, inc=1, device_id=(4 * (to // 4) + turn, to % 4), device_id_type=MESH
        )
        return carry

    lax.fori_loop(1, 16, greet_core, 0)
    pl.semaphore_signal(barrier, inc=1, device_id=(sibling, rep), device_id_type=MESH)
    pl.semaphore_signal(barrier, inc=1, device_id=(across, rep), device_id_type=MESH)
    lax.fori_loop(1, 32, greet_turn, 0)

    ins = [
        pltpu.make_async_copy(b, got.at[(rep + 4 - o) % 4], bsem.at[o])
        for o, b in enumerate((b0, b1, b2, b3))
    ]
    consts = [
        pltpu.make_async_copy(src, dst, csem.at[n])
        for n, (src, dst) in enumerate(
            (
                (rx_hbm, rx_ref), (mid_hbm, mid_ref), (midt_hbm, midt_ref), (ex_hbm, ex_ref),
                (top_hbm, top_ref), (tx_hbm, tx_ref), (txt_hbm, txt_ref), (topt_hbm, topt_ref),
            )
        )
    ]
    for load in ins:
        load.start()
    for load in consts:
        load.start()

    for load in ins:
        load.wait()
    consts[0].wait()
    high_rx, low_rx = rx_ref[0].reshape(768, 640), rx_ref[1].reshape(768, 640)
    rows = []
    for s in range(2):
        for by in range(2):
            parts = []
            for bx in range(2):
                r = 2 * bx + by
                last = got[r, :, 512:640]
                parts += [
                    got[r, :, 256 * s : 256 * s + 256],
                    pltpu.roll(last, 64, 1) if s else last,
                ]
            rows.append(jnp.concatenate(parts, 1))
    x = jnp.concatenate(rows, 0)
    high, low = split(x)
    u = dot(high, high_rx) + dot(low, high_rx) + dot(high, low_rx)
    high, low = split(u)
    u3 = jnp.concatenate([high, high, low], 0)
    consts[1].wait()
    v0 = dot(mid_ref[0:128], u3)
    slab[...] = jnp.transpose(v0[:, 0:384])[0:320].reshape(8, 40, 128)

    pl.semaphore_wait(barrier, 48)

    def way_copy(k, slot):
        return pltpu.make_async_remote_copy(
            src_ref=way_ref,
            dst_ref=ways.at[slot],
            send_sem=wsend.at[k],
            recv_sem=wrecv.at[k],
            device_id=(first + (turn + k) % 4, rep),
            device_id_type=MESH,
        )

    for k in range(1, 4):
        way_copy(k, turn).start()
    own_way = pltpu.make_async_copy(way_ref, ways.at[turn], own_sem.at[1])
    own_way.start()

    def out_copy(k):
        to = (half + k) % 16
        return pltpu.make_async_remote_copy(
            src_ref=slab.at[to // 2],
            dst_ref=g_ref.at[leaf],
            send_sem=send.at[k],
            recv_sem=recv.at[k],
            device_id=(2 * to + core, rep),
            device_id_type=MESH,
        )

    def in_copy(k):
        return pltpu.make_async_remote_copy(
            src_ref=slab.at[0],
            dst_ref=g_ref.at[2 * ((half + 16 - k) % 16) + core],
            send_sem=send.at[k],
            recv_sem=recv.at[k],
            device_id=(sibling, rep),
            device_id_type=MESH,
        )

    def pass_copy(k, which):
        slot = 2 * ((half + 16 - k) % 16) + which
        return pltpu.make_async_remote_copy(
            src_ref=g_ref.at[slot],
            dst_ref=g_ref.at[slot],
            send_sem=fsend.at[k],
            recv_sem=frecv.at[k],
            device_id=(sibling, rep),
            device_id_type=MESH,
        )

    def begin(k, carry):
        out_copy(k).start()
        return carry

    own = pltpu.make_async_copy(slab.at[group], g_ref.at[leaf], own_sem.at[0])
    own.start()
    lax.fori_loop(1, 16, begin, 0)

    for load in consts[2:4]:
        load.wait()
    v = jnp.concatenate([v0, dot(mid_ref[128:416], u3)], 0)
    gh, gm = split(g1_ref[...])
    gl = (g1_ref[...] - gh.astype(F32) - gm.astype(F32)).astype(BF16)
    gain = dot(gh, ex_ref[...]) + dot(gm, ex_ref[...]) + dot(gl, ex_ref[...])
    w = left_dot(midt_ref[...], v * gain)
    high, low = split(w)
    z = dot_t(high, high_rx) + dot_t(low, high_rx) + dot_t(high, low_rx)
    for by in range(2):
        for bx in range(2):
            r = 2 * bx + by
            last = []
            for s in range(2):
                base = (2 * s + by) * 104
                back[r, :, 256 * s : 256 * s + 256] = z[
                    base : base + 104, 384 * bx : 384 * bx + 256
                ]
                last.append(z[base : base + 104, 384 * bx + 256 : 384 * bx + 384])
            back[r, :, 512:640] = last[0] + pltpu.roll(last[1], 64, 1)

    def home_copy(k, to, slot):
        return pltpu.make_async_remote_copy(
            src_ref=back.at[to],
            dst_ref=back_ref.at[slot],
            send_sem=zsend.at[k],
            recv_sem=zrecv.at[k],
            device_id=(leaf, (rep + k) % 4),
            device_id_type=MESH,
        )

    own.wait()
    pass_copy(0, core).start()

    def relay(k, carry):
        in_copy(k).wait_recv()
        pass_copy(k, core).start()
        return carry

    lax.fori_loop(1, 16, relay, 0)
    for k in range(1, 4):
        home_copy(k, (rep + k) % 4, rep).start()
    own_back = pltpu.make_async_copy(back.at[rep], back_ref.at[rep], own_sem.at[2])
    own_back.start()

    kids[...] = jnp.zeros_like(kids)
    own_way.wait()
    for k in range(1, 4):
        way_copy(k, (turn + 4 - k) % 4).wait_recv()
    code = lax.broadcasted_iota(jnp.int32, (64, 128), 0)
    lane = lax.broadcasted_iota(jnp.int32, (64, 128), 1)
    for t in range(4):
        hit = jnp.broadcast_to(ways[t, 0:1, :], (64, 128)) == code
        found = jnp.max(jnp.where(hit & (lane < 32), lane, -1), axis=1, keepdims=True)
        inv[t] = jnp.broadcast_to(found, (64, 128))
    to_smem = [
        pltpu.make_async_copy(ways, ways_s, own_sem.at[3]),
        pltpu.make_async_copy(inv, inv_s, own_sem.at[4]),
    ]
    for load in to_smem:
        load.start()
    for load in to_smem:
        load.wait()

    def arrive(k, carry):
        pass_copy(k, 1 - core).wait_recv()
        return carry

    lax.fori_loop(0, 16, arrive, 0)

    def gather(n, carry):
        for s in range(2):
            for t in range(4):
                l = inv_s[t, 2 * n + s, 0]
                there = jnp.where(l >= 0, 1.0, 0.0)
                kids[n * 8 + t * 2 + s, 0:10, :] = (
                    g_ref[jnp.clip(l, 0, 31), 10 * t : 10 * t + 10, :] * there
                )
        return carry

    lax.fori_loop(0, 32, gather, 0)
    for load in consts[4:]:
        load.wait()

    def eight(g, carry):
        base = 64 * g
        sets = kids[pl.ds(base, 64)].reshape(8, 2, 4, 16, 128)
        y = jnp.concatenate([sets[:, :, b].reshape(256, 128) for b in range(4)], 1)
        z = right_dot(y, top_ref[...])
        v = left_dot(tx_ref[...], z)
        tops[pl.ds(8 * g, 8)] = v.reshape(8, 2, 16, 512)[:, 0, :, 0:128]
        v = (v.reshape(8, 32, 512) * g2_ref[...][None]).reshape(256, 512)
        z = left_dot(txt_ref[...], v)
        y = right_dot(z, topt_ref[...])
        for l in range(8):
            for b in range(4):
                for bx in range(2):
                    kids[base + 8 * l + 4 * bx + b] = y[
                        32 * l + 16 * bx : 32 * l + 16 * bx + 16, 128 * b : 128 * b + 128
                    ]
        return carry

    lax.fori_loop(0, 4, eight, 0)

    def pick(n, carry):
        for t in range(4):
            c = ways_s[t, 0, 4 * n + turn]
            news[n, 10 * t : 10 * t + 10, :] = kids[jnp.clip((c // 2) * 8 + t * 2 + c % 2, 0, 255), 0:10, :]
        return carry

    lax.fori_loop(0, 8, pick, 0)

    def out_new(k):
        to = (spot + k) % 32
        return pltpu.make_async_remote_copy(
            src_ref=news.at[to // 4],
            dst_ref=out_ref.at[spot],
            send_sem=psend.at[k],
            recv_sem=precv.at[k],
            device_id=(4 * (to // 4) + turn, to % 4),
            device_id_type=MESH,
        )

    def in_new(k):
        return pltpu.make_async_remote_copy(
            src_ref=news.at[0],
            dst_ref=out_ref.at[(spot + 32 - k) % 32],
            send_sem=psend.at[k],
            recv_sem=precv.at[k],
            device_id=(sibling, rep),
            device_id_type=MESH,
        )

    def out_top(k):
        to = 4 * ((group + k) % 8) + turn
        return pltpu.make_async_remote_copy(
            src_ref=tops.at[to],
            dst_ref=coarse_ref.at[group],
            send_sem=tsend.at[k],
            recv_sem=trecv.at[k],
            device_id=(to, rep),
            device_id_type=MESH,
        )

    def in_top(k):
        return pltpu.make_async_remote_copy(
            src_ref=tops.at[0],
            dst_ref=coarse_ref.at[(group + 8 - k) % 8],
            send_sem=tsend.at[k],
            recv_sem=trecv.at[k],
            device_id=(sibling, rep),
            device_id_type=MESH,
        )

    def begin_new(k, carry):
        out_new(k).start()
        return carry

    def begin_top(k, carry):
        out_top(k).start()
        return carry

    lax.fori_loop(1, 32, begin_new, 0)
    lax.fori_loop(1, 8, begin_top, 0)
    own_new = pltpu.make_async_copy(news.at[group], out_ref.at[spot], own_sem.at[5])
    own_new.start()
    own_top = pltpu.make_async_copy(tops.at[leaf], coarse_ref.at[group], own_sem.at[6])
    own_top.start()

    def sent(k, carry):
        out_copy(k).wait_send()
        return carry

    def passed(k, carry):
        pass_copy(k, core).wait_send()
        return carry

    lax.fori_loop(1, 16, sent, 0)
    lax.fori_loop(0, 16, passed, 0)
    for k in range(1, 4):
        way_copy(k, turn).wait_send()
        home_copy(k, (rep + k) % 4, rep).wait_send()
        home_copy(k, (rep + k) % 4, (rep + 4 - k) % 4).wait_recv()

    def finish(k, carry):
        in_new(k).wait_recv()
        out_new(k).wait_send()
        return carry

    def finish_top(k, carry):
        in_top(k).wait_recv()
        out_top(k).wait_send()
        return carry

    lax.fori_loop(1, 32, finish, 0)
    lax.fori_loop(1, 8, finish_top, 0)
    own_back.wait()
    own_new.wait()
    own_top.wait()


def core_call(blocks, way, gain_mid, gain_top):
    T = tables()
    dma = pltpu.SemaphoreType.DMA
    consts = [T[n] for n in ("rx", "mid", "midT", "ex", "top", "tx", "txT", "topT")]
    return pl.pallas_call(
        core_kernel,
        in_specs=[ANY] * 4 + [VMEM] * 3 + [ANY] * 8,
        out_specs=[ANY] * 3,
        out_shape=[
            jax.ShapeDtypeStruct((32, 40, 128), F32),
            jax.ShapeDtypeStruct((8, 16, 128), F32),
            jax.ShapeDtypeStruct((4, 104, 640), F32),
        ],
        scratch_shapes=[pltpu.VMEM(c.shape, BF16) for c in consts]
        + [
            pltpu.VMEM((4, 104, 640), F32),
            pltpu.VMEM((4, 104, 640), F32),
            pltpu.VMEM((8, 40, 128), F32),
            pltpu.VMEM((32, 40, 128), F32),
            pltpu.VMEM((4, 8, 128), jnp.int32),
            pltpu.VMEM((4, 64, 128), jnp.int32),
            pltpu.VMEM((256, 16, 128), F32),
            pltpu.VMEM((32, 16, 128), F32),
            pltpu.VMEM((8, 40, 128), F32),
            pltpu.SMEM((4, 8, 128), jnp.int32),
            pltpu.SMEM((4, 64, 128), jnp.int32),
            dma((8,)), dma((4,)), dma((7,)),
            dma((16,)), dma((16,)), dma((16,)), dma((16,)),
            dma((4,)), dma((4,)), dma((4,)), dma((4,)),
            dma((32,)), dma((32,)), dma((8,)), dma((8,)),
        ],
        compiler_params=pltpu.CompilerParams(
            collective_id=1, has_side_effects=True, vmem_limit_bytes=60 * 1024 * 1024
        ),
        name="core",
    )(*blocks, way, gain_mid, gain_top, *consts)


def final_kernel(
    rep_ref, slab_ref, got, up_ref, rx_ref, tgt_ref, x0t_ref, yzt_ref, z_ref, live_ref,
    o_ref, sums, ypos, pnew, big, ob, sem, osem,
):
    loads = [
        pltpu.make_async_copy(
            z_ref.at[pl.ds(13 * p, 13)], big.at[pl.ds(13 * p, 13)], sem.at[p]
        )
        for p in range(4)
    ]
    for load in loads:
        load.start()
    rep = rep_ref[0]
    by, bx = rep % 2, rep // 2
    mine = slab_ref[...].reshape(8, 4, 40, 128)
    cols = []
    for r in range(4):
        rows = mine[:, r].reshape(320, 128)
        rows = jnp.concatenate([rows, jnp.zeros((64, 128), F32)], 0)
        cols.append(jnp.transpose(rows))
    tall = left_dot(up_ref[by], jnp.concatenate(cols, 1))
    stack = jnp.concatenate(
        [tall[104 * s : 104 * s + 104, 384 * r : 384 * r + 384] for r in range(4) for s in range(2)],
        0,
    )
    high, low = split(stack)
    hi_rx = rx_ref[0, bx][:, 0:384]
    lo_rx = rx_ref[1, bx][:, 0:384]
    f = dot_t(high, hi_rx) + dot_t(low, hi_rx) + dot_t(high, lo_rx)
    for r in range(4):
        for s in range(2):
            base = (2 * r + s) * 104
            sums[r, :, 256 * s : 256 * s + 256] = (
                got[r, :, 256 * s : 256 * s + 256] + f[base : base + 104, 0:256]
            )
        sums[r, :, 512:640] = got[r, :, 512:640] + f[2 * r * 104 : 2 * r * 104 + 104, 256:384] + pltpu.roll(
            f[(2 * r + 1) * 104 : (2 * r + 2) * 104, 256:384], 64, 1
        )
    for i in range(10):
        for pair in range(2):
            pieces = []
            for r in (2 * pair, 2 * pair + 1):
                for s in range(2):
                    if i < 8:
                        tile = 2 * s + i // 4
                        now = i % 4
                    else:
                        tile = 4
                        now = 2 * s + i - 8
                    pieces.append((sums[r, :, 128 * tile : 128 * tile + 128], now))
            ypos[i, :, 128 * pair : 128 * pair + 128] = place(pieces, 104)
    row = lax.broadcasted_iota(jnp.int32, (256, 256), 0)
    code = 2 * ((row % 32) * 4 + row // 64) + (row // 32) % 2
    hot = (tgt_ref[...] == code).astype(F32).astype(BF16)
    pnew[...] = one_hot_dot(ypos[...].reshape(1040, 256), hot).reshape(10, 104, 256)
    loads[0].wait()
    for t in range(13):
        w = pnew[:, 8 * t : 8 * t + 8, :].reshape(80, 256)
        big[t] += left_dot(x0t_ref[...], w).reshape(20, 8, 256)
    for load in loads[1:]:
        load.wait()
    live = jnp.broadcast_to(live_ref[...][None] > 0, (4, 104, 256))
    stores = []
    for n in range(10):
        z = []
        for i2 in range(2):
            w = big[:, 2 * n + i2].reshape(416, 256)
            z.append(jnp.where(live, left_dot(yzt_ref[i2], w).reshape(4, 104, 256), 0.0))
        ob[n, :, 0:96, :] = z[0][:, 0:96]
        ob[n, :, 96:104, :] = z[0][:, 96:104] + z[1][:, 0:8]
        ob[n, :, 104:200, :] = z[1][:, 8:104]
        store = pltpu.make_async_copy(ob.at[n], window(o_ref, n), osem.at[n])
        store.start()
        stores.append(store)
    for store in stores:
        store.wait()


def final_call(rep, slabs, blocks, target, z, live):
    T = tables()
    return pl.pallas_call(
        final_kernel,
        in_specs=[SMEM] + [VMEM] * 7 + [ANY, VMEM],
        out_specs=ANY,
        out_shape=jax.ShapeDtypeStruct((2, 4, 5, 200, 256), F32),
        scratch_shapes=[
            pltpu.VMEM((4, 104, 640), F32),
            pltpu.VMEM((10, 104, 256), F32),
            pltpu.VMEM((10, 104, 256), F32),
            pltpu.VMEM((52, 20, 8, 256), F32),
            pltpu.VMEM((10, 4, 200, 256), F32),
            pltpu.SemaphoreType.DMA((4,)),
            pltpu.SemaphoreType.DMA((10,)),
        ],
        compiler_params=vmem(60),
        name="final",
    )(rep, slabs, blocks, T["up"], T["rx"], target, T["x0T"], T["yzT"], z, live)


def gain_cube(row):
    cube = jnp.concatenate([jnp.zeros((1000,), F32), row]).reshape(2, 4, 10, 100)
    return jnp.pad(cube, ((0, 0), (0, 0), (0, 0), (0, 4)))


def finest_gain(row):
    cube = gain_cube(row).reshape(2, 4, 10, 13, 8).transpose(1, 0, 2, 4, 3).reshape(4, 160, 13)
    return jnp.pad(cube, ((0, 0), (0, 0), (0, 115)))


def middle_gain(row):
    cube = gain_cube(row).transpose(1, 3, 0, 2).reshape(416, 20)
    return jnp.pad(cube, ((0, 0), (0, 108)))


def top_gain(row):
    cube = jnp.concatenate([jnp.ones((1000,), F32), row]).reshape(2, 4, 10, 100)
    cube = jnp.pad(cube, ((0, 0), (0, 0), (0, 6), (0, 28)))
    return cube.transpose(0, 2, 1, 3).reshape(32, 512)


def swap(blocks):
    out = [blocks[0]]
    for o in range(1, 4):
        out.append(lax.ppermute(blocks[o], "rep", [(r, (r + o) % 4) for r in range(4)]))
    return out


def shards(fine_coeffs, set_counts, route_first, route_top, level_gain):
    rep = lax.axis_index("rep").reshape(1).astype(jnp.int32)
    living = lax.iota(jnp.int32, 256) < set_counts[0]
    target = jnp.where(living, route_first, -1)
    live = living.astype(F32).reshape(1, 256)
    way = jnp.pad(route_top.reshape(1, 32), ((0, 7), (0, 96)), constant_values=-1)
    x5 = fine_coeffs.reshape(2, 4, 5, 200, 256)
    blocks = parents_call(x5, rep, target.reshape(256, 1))
    blocks = swap(blocks)
    z = details_call(x5, finest_gain(level_gain[0]))
    z, *blocks = lax.optimization_barrier((z, *blocks))
    new, coarse, back = core_call(
        blocks, way, middle_gain(level_gain[1]), top_gain(level_gain[2])
    )
    out = final_call(rep, new, back, target.reshape(1, 256), z, live)
    coarse = coarse[:, :10, :100].reshape(8, 1000).T
    return (out.reshape(8000, 256), coarse)


def solution(mesh):
    placed = (
        P(None, ("leaf", "rep")),
        P(("leaf", "rep")),
        P(("leaf", "rep")),
        P(("leaf", "rep")),
        P(),
    )
    return jax.shard_map(
        shards,
        mesh=mesh,
        in_specs=placed,
        out_specs=(P(None, ("leaf", "rep")), P(None, ("leaf", "rep"))),
        check_vma=False,
    )
```

```python
import functools
import math

import jax
import jax.numpy as jnp
import ml_dtypes
import numpy as np
from jax import lax
from jax.experimental import pallas as pl
from jax.experimental.pallas import tpu as pltpu
from jax.sharding import PartitionSpec as P

POLY_ORDER = 10
F32 = jnp.float32
BF16 = jnp.bfloat16
MESH = pl.DeviceIdType.MESH


def legendre_pair(count, position):
    before, current = (1.0, position)
    for degree in range(1, count):
        before, current = (
            current,
            ((2 * degree + 1) * position * current - degree * before) / (degree + 1),
        )
    derivative = count * (position * current - before) / (position * position - 1.0)
    return (current, derivative)


def gauss_points(count):
    nodes = []
    weights = []
    for node_index in range(count):
        estimate = math.cos(math.pi * (node_index + 0.75) / (count + 0.5))
        for newton_step in range(100):
            current, derivative = legendre_pair(count, estimate)
            estimate = estimate - current / derivative
        current, derivative = legendre_pair(count, estimate)
        nodes.append(estimate)
        weights.append(2.0 / ((1.0 - estimate * estimate) * derivative * derivative))
    return (np.array(nodes), np.array(weights))


def legendre_rows(degree_count, points):
    values = [points * 0.0 + 1.0, points.copy()]
    for degree in range(1, degree_count - 1):
        values.append(
            ((2 * degree + 1) * points * values[degree] - degree * values[degree - 1])
            / (degree + 1)
        )
    return np.stack(
        [np.sqrt(2.0 * degree + 1.0) * values[degree] for degree in range(degree_count)]
    )


@functools.cache
def two_scale(poly_order):
    points, weights = gauss_points(2 * poly_order)
    lower_half = (points + 1.0) / 4.0
    half_weights = weights / 4.0
    child_rows = legendre_rows(poly_order, 4.0 * lower_half - 1.0)
    parent_low = legendre_rows(poly_order, 2.0 * lower_half - 1.0)
    parent_high = legendre_rows(poly_order, 2.0 * (lower_half + 0.5) - 1.0)
    filter_left = math.sqrt(2.0) * (parent_low * half_weights) @ child_rows.T
    filter_right = math.sqrt(2.0) * (parent_high * half_weights) @ child_rows.T
    basis_rows = list(np.concatenate([filter_left, filter_right], axis=1))
    units = np.eye(2 * poly_order)
    for step_index in range(poly_order):
        residuals = []
        for vector in units:
            for sweep in range(2):
                for previous in basis_rows:
                    vector = vector - np.dot(previous, vector) * previous
            residuals.append(vector)
        lengths = np.array([np.sqrt(np.dot(vector, vector)) for vector in residuals])
        chosen = int(np.argmax(lengths))
        basis_rows.append(residuals[chosen] / lengths[chosen])
    filters = np.array(basis_rows).reshape(2, poly_order, 2, poly_order)
    return filters.astype(np.float32).astype(np.float64)


def halves(matrix):
    high = matrix.astype(ml_dtypes.bfloat16)
    low = (matrix - high.astype(np.float64)).astype(ml_dtypes.bfloat16)
    return high, low


def left3(matrix):
    high, low = halves(matrix)
    return np.concatenate([high, low, high], axis=-1)


def right3(matrix):
    high, low = halves(matrix)
    return np.concatenate([high, low, high], axis=-2)


@functools.cache
def tables():
    H = two_scale(POLY_ORDER)
    out = {}
    yz = np.einsum("rtbj,uwck->rutwbcjk", H, H)
    yz = yz.reshape(4, 100, 4, 100)
    par = np.zeros((2, 104, 4, 2, 100))
    for i2 in range(2):
        par[i2, :100, :, i2, :] = yz[0]
    par = par.reshape(208, 800)
    out["par"] = left3(par)
    out["parT"] = left3(par.T.copy())
    full = np.zeros((2, 4, 104, 4, 104))
    full[0, :, :100, :, :100] = yz
    full[1, :, :100, :, 4:] = yz
    full = full.reshape(2, 416, 416)
    out["yz"] = left3(full)
    out["yzT"] = left3(full.transpose(0, 2, 1))
    hx = H.reshape(20, 20)
    kx = np.kron(hx, np.eye(8))
    out["x"] = left3(kx)
    out["xT"] = left3(kx.T.copy())
    out["x0"] = left3(kx[:80])
    out["x0T"] = left3(kx[:80].T.copy())
    mid = np.zeros((4, 104, 2, 2, 104))
    mid[:, :100, :, :, :100] = yz.reshape(4, 100, 2, 2, 100).transpose(0, 1, 3, 2, 4)
    mid = mid.reshape(416, 416)
    out["mid"] = left3(mid)
    out["midT"] = left3(mid.T.copy())
    rx = np.zeros((2, 3, 4, 32, 2, 32, 10))
    for tile in range(3):
        for quarter in range(4 if tile < 2 else 2):
            i = 4 * tile + quarter
            for s in range(32):
                rx[:, tile, quarter, s, :, s, :] = H[:, :, :, i].transpose(2, 0, 1)
    rx = rx.reshape(2, 384, 640)
    out["rx"] = np.stack(halves(rx), 0)
    ex = np.zeros((128, 2, 32, 10))
    for p in range(2):
        for m in range(10):
            ex[p * 10 + m, p, :, m] = 1.0
    out["ex"] = ex.reshape(128, 640).astype(ml_dtypes.bfloat16)
    up = np.zeros((2, 2, 104, 128))
    up[:, :, :100, :100] = yz[0].reshape(100, 2, 2, 100).transpose(1, 2, 3, 0)
    out["up"] = left3(up.reshape(2, 208, 128))
    top = np.zeros((4, 128, 4, 128))
    top[:, :100, :, :100] = yz.transpose(2, 3, 0, 1)
    top = top.reshape(512, 512)
    out["top"] = right3(top)
    out["topT"] = right3(top.T.copy())
    one = np.zeros((2, 16, 2, 16))
    one[:, :10, :, :10] = H
    kt = np.kron(np.eye(8), one.reshape(32, 32))
    out["tx"] = left3(kt)
    out["txT"] = left3(kt.T.copy())
    return out


def split(x):
    high = x.astype(BF16)
    low = (x - high.astype(F32)).astype(BF16)
    return high, low


def dot(a, b):
    return lax.dot_general(a, b, (((1,), (0,)), ((), ())), preferred_element_type=F32)


def dot_t(a, b):
    return lax.dot_general(a, b, (((1,), (1,)), ((), ())), preferred_element_type=F32)


def left_dot(m3, x):
    high, low = split(x)
    return dot(m3, jnp.concatenate([high, high, low], 0))


def right_dot(x, m3):
    high, low = split(x)
    return dot(jnp.concatenate([high, high, low], 1), m3)


def one_hot_dot(x, hot):
    high, low = split(x)
    return dot(high, hot) + dot(low, hot)


def quarter_of(shape):
    return lax.broadcasted_iota(jnp.int32, shape, len(shape) - 1) // 32


def place(pieces, rows):
    mark = quarter_of((rows, 128))
    out = None
    for n, (tile, now) in enumerate(pieces):
        turn = ((n - now) * 32) % 128
        moved = pltpu.roll(tile, turn, 1) if turn else tile
        out = moved if out is None else jnp.where(mark == n, moved, out)
    return out


def vmem(mib):
    return pltpu.CompilerParams(vmem_limit_bytes=mib * 1024 * 1024)


def whole(shape):
    return pl.BlockSpec(shape, lambda *_: (0,) * len(shape))


SMEM = pl.BlockSpec(memory_space=pltpu.SMEM)


def fill_gain(rows_ref, turned_ref, gain_ref, level):
    rows_ref[...] = jnp.zeros_like(rows_ref)
    for k in range(10, 80):
        px, p, m = k // 40, (k // 10) % 4, k % 10
        at = px * 10 + m
        rows_ref[p, at : at + 1, 0:100] = gain_ref[
            level : level + 1, 100 * (k - 10) : 100 * (k - 10) + 100
        ]
    for p in range(4):
        turned_ref[p] = jnp.transpose(rows_ref[p])


VMEM = pl.BlockSpec(memory_space=pltpu.VMEM)
ANY = pl.BlockSpec(memory_space=pl.ANY)


def window(ref, pair):
    return ref.at[pair // 5, :, pair % 5]


def code_hot(route_ref, count, shift):
    row = lax.broadcasted_iota(jnp.int32, (256, 256), 0)
    column = lax.broadcasted_iota(jnp.int32, (256, 256), 1)
    code = 2 * ((row % 32) * 4 + (row // 64 + shift) % 4) + (row // 32) % 2
    hit = (jnp.broadcast_to(route_ref[...], (256, 256)) == code) & (column < count)
    return hit.astype(F32).astype(BF16)


def finest_kernel(
    count_ref, x_ref, route_ref, g_ref, par_hbm, x0_hbm, yz_hbm, x1_hbm, xt_hbm,
    z_ref, block_ref,
    par_ref, x0_ref, yz_ref, x1_ref, xt_ref, xb, acc0, pm, blocks, acc, acc2, grows, gturn,
    csem, sem, osem, own_sem, send, recv,
):
    leaf = lax.axis_index("leaf")
    rep = lax.axis_index("rep")
    barrier = pltpu.get_barrier_semaphore()
    for k in range(1, 4):
        pl.semaphore_signal(
            barrier, inc=1, device_id=(leaf, (rep + k) % 4), device_id_type=MESH
        )
    consts = [
        pltpu.make_async_copy(src, dst, csem.at[n])
        for n, (src, dst) in enumerate(
            (
                (par_hbm, par_ref), (x0_hbm, x0_ref), (yz_hbm, yz_ref), (x1_hbm, x1_ref),
                (xt_hbm, xt_ref),
            )
        )
    ]
    loads = [pltpu.make_async_copy(window(x_ref, n), xb.at[n], sem.at[n]) for n in range(10)]
    consts[0].start()
    for load in loads[:3]:
        load.start()
    consts[1].start()
    hot = code_hot(route_ref, count_ref[0], rep)
    fill_gain(grows, gturn, g_ref, 0)
    consts[0].wait()
    for n in range(10):
        loads[n].wait()
        if n < 7:
            loads[n + 3].start()
        u = left_dot(par_ref[...], xb[n].reshape(800, 256)).reshape(2, 13, 8, 256)
        acc0[:, 2 * n] = u[0]
        acc0[:, 2 * n + 1] = u[1]
    for load in consts[2:]:
        load.start()
    consts[1].wait()
    for t in range(13):
        v = left_dot(x0_ref[...], acc0[t].reshape(160, 256))
        pm[:, 8 * t : 8 * t + 8, :] = v.reshape(10, 8, 256)
    high, low = split(pm[...].reshape(1040, 256))
    y = (dot_t(high, hot) + dot_t(low, hot)).reshape(10, 104, 256)
    def move(k, slot):
        return pltpu.make_async_remote_copy(
            src_ref=blocks.at[k],
            dst_ref=block_ref.at[slot],
            send_sem=send.at[k],
            recv_sem=recv.at[k],
            device_id=(leaf, (rep + k) % 4),
            device_id_type=MESH,
        )

    pl.semaphore_wait(barrier, 3)
    for o in (2, 1, 3, 0):
        tile = y[:, :, (o // 2) * 128 : (o // 2) * 128 + 128]
        base = (o % 2) * 2
        for s in range(2):
            for q in range(2):
                blocks[o, :, (2 * s + q) * 128 : (2 * s + q + 1) * 128] = place(
                    [(tile[4 * q + n], base + s) for n in range(4)], 104
                )
        blocks[o, :, 512:640] = place(
            [(tile[8], base), (tile[9], base), (tile[8], base + 1), (tile[9], base + 1)], 104
        )
        if o:
            move(o, rep).start()
    own = pltpu.make_async_copy(blocks.at[0], block_ref.at[rep], own_sem)
    own.start()

    for load in consts[2:]:
        load.wait()
    for n in range(10):
        for i2 in range(2):
            w = xb[n, :, 96 * i2 : 96 * i2 + 104, :].reshape(416, 256)
            acc[:, 2 * n + i2] = left_dot(yz_ref[i2], w).reshape(52, 8, 256)

    def store(p):
        part = pl.ds(13 * p, 13)
        return pltpu.make_async_copy(acc2.at[part], z_ref.at[part], osem.at[p])

    def quarter(p, carry):
        for n in range(13):
            t = 13 * p + n
            v = left_dot(x1_ref[...], acc[t].reshape(160, 256))
            g = gturn[p, 8 * n : 8 * n + 8, :]
            g = jnp.concatenate(
                [jnp.broadcast_to(g[:, c : c + 1], (8, 256)) for c in range(20)], 0
            )
            acc2[t] = left_dot(xt_ref[...], v * g).reshape(20, 8, 256)
        store(p).start()
        return carry

    lax.fori_loop(0, 4, quarter, 0)
    own.wait()
    for k in range(1, 4):
        move(k, rep).wait_send()
        move(k, (rep + 4 - k) % 4).wait_recv()
    for p in range(4):
        store(p).wait()


def finest_call(x5, count, route, gain):
    T = tables()
    dma = pltpu.SemaphoreType.DMA
    consts = [T[n] for n in ("par", "x0", "yz", "x", "xT")]
    return pl.pallas_call(
        finest_kernel,
        in_specs=[SMEM, ANY, VMEM, VMEM] + [ANY] * 5,
        out_specs=[ANY] * 2,
        out_shape=[
            jax.ShapeDtypeStruct((52, 20, 8, 256), F32),
            jax.ShapeDtypeStruct((4, 104, 640), F32),
        ],
        scratch_shapes=[pltpu.VMEM(c.shape, BF16) for c in consts]
        + [
            pltpu.VMEM((10, 4, 200, 256), F32),
            pltpu.VMEM((13, 20, 8, 256), F32),
            pltpu.VMEM((10, 104, 256), F32),
            pltpu.VMEM((4, 104, 640), F32),
            pltpu.VMEM((52, 20, 8, 256), F32),
            pltpu.VMEM((52, 20, 8, 256), F32),
            pltpu.VMEM((4, 128, 128), F32),
            pltpu.VMEM((4, 128, 128), F32),
            dma((5,)), dma((10,)), dma((4,)), dma, dma((4,)), dma((4,)),
        ],
        compiler_params=pltpu.CompilerParams(
            collective_id=2, has_side_effects=True, vmem_limit_bytes=60 * 1024 * 1024
        ),
        name="finest",
    )(count, x5, route, gain, *consts)


def core_kernel(
    block_ref, route_ref, gain_ref, rx_hbm, mid_hbm, midt_hbm, ex_hbm, top_hbm, tx_hbm,
    txt_hbm, topt_hbm,
    out_ref, coarse_ref, back_ref,
    rx_ref, mid_ref, midt_ref, ex_ref, top_ref, tx_ref, txt_ref, topt_ref,
    got, back, slab, g_ref, way_ref, ways, inv, kids, grown, grows, gturn, g2_ref, tops, news, ways_s, inv_s,
    csem, bsem, own_sem, send, recv, fsend, frecv, wsend, wrecv, zsend, zrecv,
    psend, precv, tsend, trecv,
):
    leaf = lax.axis_index("leaf")
    rep = lax.axis_index("rep")
    core = leaf % 2
    half = leaf // 2
    sibling = leaf + 1 - 2 * core
    turn = leaf % 4
    group = leaf // 4
    first = 4 * group
    across = first + (sibling + 2) % 4
    spot = group * 4 + rep
    barrier = pltpu.get_barrier_semaphore()

    def greet_core(k, carry):
        other = 2 * ((half + k) % 16) + core
        pl.semaphore_signal(barrier, inc=1, device_id=(other, rep), device_id_type=MESH)
        return carry

    def greet_turn(k, carry):
        to = (spot + k) % 32
        pl.semaphore_signal(
            barrier, inc=1, device_id=(4 * (to // 4) + turn, to % 4), device_id_type=MESH
        )
        return carry

    lax.fori_loop(1, 16, greet_core, 0)
    pl.semaphore_signal(barrier, inc=1, device_id=(sibling, rep), device_id_type=MESH)
    pl.semaphore_signal(barrier, inc=1, device_id=(across, rep), device_id_type=MESH)
    lax.fori_loop(1, 32, greet_turn, 0)

    ins = [pltpu.make_async_copy(block_ref, got, bsem)]
    consts = [
        pltpu.make_async_copy(src, dst, csem.at[n])
        for n, (src, dst) in enumerate(
            (
                (rx_hbm, rx_ref), (mid_hbm, mid_ref), (midt_hbm, midt_ref), (ex_hbm, ex_ref),
                (top_hbm, top_ref), (tx_hbm, tx_ref), (txt_hbm, txt_ref), (topt_hbm, topt_ref),
            )
        )
    ]
    for load in ins:
        load.start()
    for load in consts[:2]:
        load.start()
    fill_gain(grows, gturn, gain_ref, 1)
    g2_ref[...] = jnp.zeros_like(g2_ref)
    g2_ref[0:10, 0:100] = jnp.ones((10, 100), F32)
    for k in range(10, 80):
        px, p, m = k // 40, (k // 10) % 4, k % 10
        at = px * 16 + m
        g2_ref[at : at + 1, 128 * p : 128 * p + 100] = gain_ref[
            2:3, 100 * (k - 10) : 100 * (k - 10) + 100
        ]
    way_ref[...] = jnp.full((8, 128), -1, jnp.int32)
    way_ref[0:1, 0:32] = route_ref[...]
    kids[...] = jnp.zeros_like(kids)

    for load in ins:
        load.wait()
    consts[0].wait()
    for load in consts[2:]:
        load.start()
    high_rx, low_rx = rx_ref[0].reshape(768, 640), rx_ref[1].reshape(768, 640)
    rows = []
    for s in range(2):
        for by in range(2):
            parts = []
            for bx in range(2):
                r = 2 * bx + by
                last = got[r, :, 512:640]
                parts += [
                    got[r, :, 256 * s : 256 * s + 256],
                    pltpu.roll(last, 64, 1) if s else last,
                ]
            rows.append(jnp.concatenate(parts, 1))
    x = jnp.concatenate(rows, 0)
    high, low = split(x)
    u = dot(high, high_rx) + dot(low, high_rx) + dot(high, low_rx)
    high, low = split(u)
    u3 = jnp.concatenate([high, high, low], 0)
    consts[1].wait()
    v0 = dot(mid_ref[0:128], u3)
    slab[...] = jnp.transpose(v0[:, 0:384])[0:320].reshape(8, 40, 128)

    pl.semaphore_wait(barrier, 48)

    def way_copy(k, slot):
        return pltpu.make_async_remote_copy(
            src_ref=way_ref,
            dst_ref=ways.at[slot],
            send_sem=wsend.at[k],
            recv_sem=wrecv.at[k],
            device_id=(first + (turn + k) % 4, rep),
            device_id_type=MESH,
        )

    for k in range(1, 4):
        way_copy(k, turn).start()
    own_way = pltpu.make_async_copy(way_ref, ways.at[turn], own_sem.at[1])
    own_way.start()

    def out_copy(k):
        to = (half + k) % 16
        return pltpu.make_async_remote_copy(
            src_ref=slab.at[to // 2],
            dst_ref=g_ref.at[leaf],
            send_sem=send.at[k],
            recv_sem=recv.at[k],
            device_id=(2 * to + core, rep),
            device_id_type=MESH,
        )

    def in_copy(k):
        return pltpu.make_async_remote_copy(
            src_ref=slab.at[0],
            dst_ref=g_ref.at[2 * ((half + 16 - k) % 16) + core],
            send_sem=send.at[k],
            recv_sem=recv.at[k],
            device_id=(sibling, rep),
            device_id_type=MESH,
        )

    def pass_copy(k, which):
        slot = 2 * ((half + 16 - k) % 16) + which
        return pltpu.make_async_remote_copy(
            src_ref=g_ref.at[slot],
            dst_ref=g_ref.at[slot],
            send_sem=fsend.at[k],
            recv_sem=frecv.at[k],
            device_id=(sibling, rep),
            device_id_type=MESH,
        )

    def begin(k, carry):
        out_copy(k).start()
        return carry

    own = pltpu.make_async_copy(slab.at[group], g_ref.at[leaf], own_sem.at[0])
    own.start()
    lax.fori_loop(1, 16, begin, 0)

    for load in consts[2:4]:
        load.wait()
    v = jnp.concatenate([v0, dot(mid_ref[128:416], u3)], 0)
    g1 = jnp.concatenate([gturn[p, 0:104, :] for p in range(4)], 0)
    gh, gm = split(g1)
    gl = (g1 - gh.astype(F32) - gm.astype(F32)).astype(BF16)
    gain = dot(gh, ex_ref[...]) + dot(gm, ex_ref[...]) + dot(gl, ex_ref[...])
    w = left_dot(midt_ref[...], v * gain)
    high, low = split(w)
    z = dot_t(high, high_rx) + dot_t(low, high_rx) + dot_t(high, low_rx)
    for by in range(2):
        for bx in range(2):
            r = 2 * bx + by
            last = []
            for s in range(2):
                base = (2 * s + by) * 104
                back[r, :, 256 * s : 256 * s + 256] = z[
                    base : base + 104, 384 * bx : 384 * bx + 256
                ]
                last.append(z[base : base + 104, 384 * bx + 256 : 384 * bx + 384])
            back[r, :, 512:640] = last[0] + pltpu.roll(last[1], 64, 1)

    def home_copy(k, to, slot):
        return pltpu.make_async_remote_copy(
            src_ref=back.at[to],
            dst_ref=back_ref.at[slot],
            send_sem=zsend.at[k],
            recv_sem=zrecv.at[k],
            device_id=(leaf, (rep + k) % 4),
            device_id_type=MESH,
        )

    own.wait()
    pass_copy(0, core).start()

    def relay(k, carry):
        in_copy(k).wait_recv()
        pass_copy(k, core).start()
        return carry

    lax.fori_loop(1, 16, relay, 0)
    for k in range(1, 4):
        home_copy(k, (rep + k) % 4, rep).start()
    own_back = pltpu.make_async_copy(back.at[rep], back_ref.at[rep], own_sem.at[2])
    own_back.start()

    own_way.wait()
    for k in range(1, 4):
        way_copy(k, (turn + 4 - k) % 4).wait_recv()
    code = lax.broadcasted_iota(jnp.int32, (64, 128), 0)
    lane = lax.broadcasted_iota(jnp.int32, (64, 128), 1)
    for t in range(4):
        hit = jnp.broadcast_to(ways[t, 0:1, :], (64, 128)) == code
        found = jnp.max(jnp.where(hit & (lane < 32), lane, -1), axis=1, keepdims=True)
        inv[t] = jnp.broadcast_to(found, (64, 128))
    to_smem = [
        pltpu.make_async_copy(ways, ways_s, own_sem.at[3]),
        pltpu.make_async_copy(inv, inv_s, own_sem.at[4]),
    ]
    for load in to_smem:
        load.start()
    for load in to_smem:
        load.wait()

    def arrive(k, carry):
        pass_copy(k, 1 - core).wait_recv()
        return carry

    lax.fori_loop(0, 16, arrive, 0)

    def gather(n, carry):
        for s in range(2):
            for t in range(4):
                l = inv_s[t, 2 * n + s, 0]
                there = jnp.where(l >= 0, 1.0, 0.0)
                kids[n * 8 + t * 2 + s, 0:10, :] = (
                    g_ref[jnp.clip(l, 0, 31), 10 * t : 10 * t + 10, :] * there
                )
        return carry

    lax.fori_loop(0, 32, gather, 0)
    for load in consts[4:]:
        load.wait()

    for g in range(4):
        base = 64 * g
        sets = kids[base : base + 64].reshape(8, 2, 4, 16, 128)
        y = jnp.concatenate([sets[:, :, b].reshape(256, 128) for b in range(4)], 1)
        z = right_dot(y, top_ref[...])
        v = left_dot(tx_ref[...], z)
        tops[8 * g : 8 * g + 8] = v.reshape(8, 2, 16, 512)[:, 0, :, 0:128]
        v = (v.reshape(8, 32, 512) * g2_ref[...][None]).reshape(256, 512)
        z = left_dot(txt_ref[...], v)
        y = right_dot(z, topt_ref[...])
        for l in range(8):
            for b in range(4):
                for bx in range(2):
                    grown[base + 8 * l + 4 * bx + b] = y[
                        32 * l + 16 * bx : 32 * l + 16 * bx + 16, 128 * b : 128 * b + 128
                    ]

    def pick(n, carry):
        for t in range(4):
            c = ways_s[t, 0, 4 * n + turn]
            news[n, 10 * t : 10 * t + 10, :] = grown[jnp.clip((c // 2) * 8 + t * 2 + c % 2, 0, 255), 0:10, :]
        return carry

    lax.fori_loop(0, 8, pick, 0)

    def out_new(k):
        to = (spot + k) % 32
        return pltpu.make_async_remote_copy(
            src_ref=news.at[to // 4],
            dst_ref=out_ref.at[spot],
            send_sem=psend.at[k],
            recv_sem=precv.at[k],
            device_id=(4 * (to // 4) + turn, to % 4),
            device_id_type=MESH,
        )

    def in_new(k):
        return pltpu.make_async_remote_copy(
            src_ref=news.at[0],
            dst_ref=out_ref.at[(spot + 32 - k) % 32],
            send_sem=psend.at[k],
            recv_sem=precv.at[k],
            device_id=(sibling, rep),
            device_id_type=MESH,
        )

    def out_top(k):
        to = 4 * ((group + k) % 8) + turn
        return pltpu.make_async_remote_copy(
            src_ref=tops.at[to],
            dst_ref=coarse_ref.at[group],
            send_sem=tsend.at[k],
            recv_sem=trecv.at[k],
            device_id=(to, rep),
            device_id_type=MESH,
        )

    def in_top(k):
        return pltpu.make_async_remote_copy(
            src_ref=tops.at[0],
            dst_ref=coarse_ref.at[(group + 8 - k) % 8],
            send_sem=tsend.at[k],
            recv_sem=trecv.at[k],
            device_id=(sibling, rep),
            device_id_type=MESH,
        )

    def begin_new(k, carry):
        out_new(k).start()
        return carry

    def begin_top(k, carry):
        out_top(k).start()
        return carry

    lax.fori_loop(1, 32, begin_new, 0)
    lax.fori_loop(1, 8, begin_top, 0)
    own_new = pltpu.make_async_copy(news.at[group], out_ref.at[spot], own_sem.at[5])
    own_new.start()
    own_top = pltpu.make_async_copy(tops.at[leaf], coarse_ref.at[group], own_sem.at[6])
    own_top.start()

    def sent(k, carry):
        out_copy(k).wait_send()
        return carry

    def passed(k, carry):
        pass_copy(k, core).wait_send()
        return carry

    lax.fori_loop(1, 16, sent, 0)
    lax.fori_loop(0, 16, passed, 0)
    for k in range(1, 4):
        way_copy(k, turn).wait_send()
        home_copy(k, (rep + k) % 4, rep).wait_send()
        home_copy(k, (rep + k) % 4, (rep + 4 - k) % 4).wait_recv()

    def finish(k, carry):
        in_new(k).wait_recv()
        out_new(k).wait_send()
        return carry

    def finish_top(k, carry):
        in_top(k).wait_recv()
        out_top(k).wait_send()
        return carry

    lax.fori_loop(1, 32, finish, 0)
    lax.fori_loop(1, 8, finish_top, 0)
    own_back.wait()
    own_new.wait()
    own_top.wait()


def core_call(blocks, route, gain):
    T = tables()
    dma = pltpu.SemaphoreType.DMA
    consts = [T[n] for n in ("rx", "mid", "midT", "ex", "top", "tx", "txT", "topT")]
    return pl.pallas_call(
        core_kernel,
        in_specs=[ANY] + [VMEM] * 2 + [ANY] * 8,
        out_specs=[ANY] * 3,
        out_shape=[
            jax.ShapeDtypeStruct((32, 40, 128), F32),
            jax.ShapeDtypeStruct((8, 16, 128), F32),
            jax.ShapeDtypeStruct((4, 104, 640), F32),
        ],
        scratch_shapes=[pltpu.VMEM(c.shape, BF16) for c in consts]
        + [
            pltpu.VMEM((4, 104, 640), F32),
            pltpu.VMEM((4, 104, 640), F32),
            pltpu.VMEM((8, 40, 128), F32),
            pltpu.VMEM((32, 40, 128), F32),
            pltpu.VMEM((8, 128), jnp.int32),
            pltpu.VMEM((4, 8, 128), jnp.int32),
            pltpu.VMEM((4, 64, 128), jnp.int32),
            pltpu.VMEM((256, 16, 128), F32),
            pltpu.VMEM((256, 16, 128), F32),
            pltpu.VMEM((4, 128, 128), F32),
            pltpu.VMEM((4, 128, 128), F32),
            pltpu.VMEM((32, 512), F32),
            pltpu.VMEM((32, 16, 128), F32),
            pltpu.VMEM((8, 40, 128), F32),
            pltpu.SMEM((4, 8, 128), jnp.int32),
            pltpu.SMEM((4, 64, 128), jnp.int32),
            dma((8,)), dma, dma((7,)),
            dma((16,)), dma((16,)), dma((16,)), dma((16,)),
            dma((4,)), dma((4,)), dma((4,)), dma((4,)),
            dma((32,)), dma((32,)), dma((8,)), dma((8,)),
        ],
        compiler_params=pltpu.CompilerParams(
            collective_id=1, has_side_effects=True, vmem_limit_bytes=60 * 1024 * 1024
        ),
        name="core",
    )(blocks, route, gain, *consts)


def final_kernel(
    count_ref, route_ref, slab_hbm, got_hbm, up_hbm, rx_hbm, x0t_hbm, yzt_hbm, z_ref, top_ref,
    o_ref, coarse_ref, slab_ref, got, up_ref, rx_ref, x0t_ref, yzt_ref, csem, sums, ypos, pnew, big, ob, sem, osem,
):
    loads = [
        pltpu.make_async_copy(
            z_ref.at[pl.ds(13 * p, 13)], big.at[pl.ds(13 * p, 13)], sem.at[p]
        )
        for p in range(4)
    ]
    rep = lax.axis_index("rep")
    by, bx = rep % 2, rep // 2
    firsts = [
        pltpu.make_async_copy(slab_hbm, slab_ref, csem.at[0]),
        pltpu.make_async_copy(up_hbm.at[by], up_ref, csem.at[1]),
        pltpu.make_async_copy(rx_hbm.at[0, bx], rx_ref.at[0], csem.at[2]),
        pltpu.make_async_copy(rx_hbm.at[1, bx], rx_ref.at[1], csem.at[3]),
        pltpu.make_async_copy(got_hbm, got, csem.at[4]),
        pltpu.make_async_copy(x0t_hbm, x0t_ref, csem.at[5]),
    ]
    late = pltpu.make_async_copy(yzt_hbm, yzt_ref, csem.at[6])
    for load in firsts:
        load.start()
    loads[0].start()
    hot = code_hot(route_ref, count_ref[0], 0)
    for m in range(10):
        coarse_ref[:, 100 * m : 100 * m + 100] = top_ref[:, m, 0:100]
    for load in firsts[:2]:
        load.wait()
    late.start()
    for load in loads[1:]:
        load.start()
    mine = slab_ref[...].reshape(8, 4, 40, 128)
    cols = []
    for r in range(4):
        rows = mine[:, r].reshape(320, 128)
        rows = jnp.concatenate([rows, jnp.zeros((64, 128), F32)], 0)
        cols.append(jnp.transpose(rows))
    tall = left_dot(up_ref[...], jnp.concatenate(cols, 1))
    stack = jnp.concatenate(
        [tall[104 * s : 104 * s + 104, 384 * r : 384 * r + 384] for r in range(4) for s in range(2)],
        0,
    )
    high, low = split(stack)
    for load in firsts[2:]:
        load.wait()
    hi_rx = rx_ref[0][:, 0:384]
    lo_rx = rx_ref[1][:, 0:384]
    f = dot_t(high, hi_rx) + dot_t(low, hi_rx) + dot_t(high, lo_rx)
    for r in range(4):
        for s in range(2):
            base = (2 * r + s) * 104
            sums[r, :, 256 * s : 256 * s + 256] = (
                got[r, :, 256 * s : 256 * s + 256] + f[base : base + 104, 0:256]
            )
        sums[r, :, 512:640] = got[r, :, 512:640] + f[2 * r * 104 : 2 * r * 104 + 104, 256:384] + pltpu.roll(
            f[(2 * r + 1) * 104 : (2 * r + 2) * 104, 256:384], 64, 1
        )
    for i in range(10):
        for pair in range(2):
            pieces = []
            for r in (2 * pair, 2 * pair + 1):
                for s in range(2):
                    if i < 8:
                        tile = 2 * s + i // 4
                        now = i % 4
                    else:
                        tile = 4
                        now = 2 * s + i - 8
                    pieces.append((sums[r, :, 128 * tile : 128 * tile + 128], now))
            ypos[i, :, 128 * pair : 128 * pair + 128] = place(pieces, 104)
    pnew[...] = one_hot_dot(ypos[...].reshape(1040, 256), hot).reshape(10, 104, 256)
    loads[0].wait()
    for t in range(13):
        w = pnew[:, 8 * t : 8 * t + 8, :].reshape(80, 256)
        big[t] += left_dot(x0t_ref[...], w).reshape(20, 8, 256)
    late.wait()
    for load in loads[1:]:
        load.wait()
    live = lax.broadcasted_iota(jnp.int32, (4, 104, 256), 2) < count_ref[0]
    stores = []
    for n in range(10):
        z = []
        for i2 in range(2):
            w = big[:, 2 * n + i2].reshape(416, 256)
            z.append(jnp.where(live, left_dot(yzt_ref[i2], w).reshape(4, 104, 256), 0.0))
        ob[n, :, 0:96, :] = z[0][:, 0:96]
        ob[n, :, 96:104, :] = z[0][:, 96:104] + z[1][:, 0:8]
        ob[n, :, 104:200, :] = z[1][:, 8:104]
        store = pltpu.make_async_copy(ob.at[n], window(o_ref, n), osem.at[n])
        store.start()
        stores.append(store)
    for store in stores:
        store.wait()


def final_call(count, slabs, blocks, route, z, tops):
    T = tables()
    return pl.pallas_call(
        final_kernel,
        in_specs=[SMEM, VMEM] + [ANY] * 7 + [VMEM],
        out_specs=[ANY, VMEM],
        out_shape=[
            jax.ShapeDtypeStruct((2, 4, 5, 200, 256), F32),
            jax.ShapeDtypeStruct((8, 1000), F32),
        ],
        scratch_shapes=[
            pltpu.VMEM((32, 40, 128), F32),
            pltpu.VMEM((4, 104, 640), F32),
            pltpu.VMEM((208, 384), BF16),
            pltpu.VMEM((2, 384, 640), BF16),
            pltpu.VMEM((160, 240), BF16),
            pltpu.VMEM((2, 416, 1248), BF16),
            pltpu.SemaphoreType.DMA((7,)),
            pltpu.VMEM((4, 104, 640), F32),
            pltpu.VMEM((10, 104, 256), F32),
            pltpu.VMEM((10, 104, 256), F32),
            pltpu.VMEM((52, 20, 8, 256), F32),
            pltpu.VMEM((10, 4, 200, 256), F32),
            pltpu.SemaphoreType.DMA((4,)),
            pltpu.SemaphoreType.DMA((10,)),
        ],
        compiler_params=vmem(60),
        name="final",
    )(count, route, slabs, blocks, T["up"], T["rx"], T["x0T"], T["yzT"], z, tops)


def shards(fine_coeffs, set_counts, route_first, route_top, level_gain):
    route = route_first.reshape(1, 256)
    x5 = fine_coeffs.reshape(2, 4, 5, 200, 256)
    z, blocks = finest_call(x5, set_counts, route, level_gain)
    new, tops, back = core_call(blocks, route_top.reshape(1, 32), level_gain)
    out, coarse = final_call(set_counts, new, back, route, z, tops)
    return (out.reshape(8000, 256), coarse.T)


def solution(mesh):
    placed = (
        P(None, ("leaf", "rep")),
        P(("leaf", "rep")),
        P(("leaf", "rep")),
        P(("leaf", "rep")),
        P(),
    )
    return jax.shard_map(
        shards,
        mesh=mesh,
        in_specs=placed,
        out_specs=(P(None, ("leaf", "rep")), P(None, ("leaf", "rep"))),
        check_vma=False,
    )
```

```python
import functools
import math

import jax
import jax.numpy as jnp
import ml_dtypes
import numpy as np
from jax import lax
from jax.experimental import pallas as pl
from jax.experimental.pallas import tpu as pltpu
from jax.sharding import PartitionSpec as P

POLY_ORDER = 10
F32 = jnp.float32
BF16 = jnp.bfloat16
MESH = pl.DeviceIdType.MESH


def legendre_pair(count, position):
    before, current = (1.0, position)
    for degree in range(1, count):
        before, current = (
            current,
            ((2 * degree + 1) * position * current - degree * before) / (degree + 1),
        )
    derivative = count * (position * current - before) / (position * position - 1.0)
    return (current, derivative)


def gauss_points(count):
    nodes = []
    weights = []
    for node_index in range(count):
        estimate = math.cos(math.pi * (node_index + 0.75) / (count + 0.5))
        for newton_step in range(100):
            current, derivative = legendre_pair(count, estimate)
            estimate = estimate - current / derivative
        current, derivative = legendre_pair(count, estimate)
        nodes.append(estimate)
        weights.append(2.0 / ((1.0 - estimate * estimate) * derivative * derivative))
    return (np.array(nodes), np.array(weights))


def legendre_rows(degree_count, points):
    values = [points * 0.0 + 1.0, points.copy()]
    for degree in range(1, degree_count - 1):
        values.append(
            ((2 * degree + 1) * points * values[degree] - degree * values[degree - 1])
            / (degree + 1)
        )
    return np.stack(
        [np.sqrt(2.0 * degree + 1.0) * values[degree] for degree in range(degree_count)]
    )


@functools.cache
def two_scale(poly_order):
    points, weights = gauss_points(2 * poly_order)
    lower_half = (points + 1.0) / 4.0
    half_weights = weights / 4.0
    child_rows = legendre_rows(poly_order, 4.0 * lower_half - 1.0)
    parent_low = legendre_rows(poly_order, 2.0 * lower_half - 1.0)
    parent_high = legendre_rows(poly_order, 2.0 * (lower_half + 0.5) - 1.0)
    filter_left = math.sqrt(2.0) * (parent_low * half_weights) @ child_rows.T
    filter_right = math.sqrt(2.0) * (parent_high * half_weights) @ child_rows.T
    basis_rows = list(np.concatenate([filter_left, filter_right], axis=1))
    units = np.eye(2 * poly_order)
    for step_index in range(poly_order):
        residuals = []
        for vector in units:
            for sweep in range(2):
                for previous in basis_rows:
                    vector = vector - np.dot(previous, vector) * previous
            residuals.append(vector)
        lengths = np.array([np.sqrt(np.dot(vector, vector)) for vector in residuals])
        chosen = int(np.argmax(lengths))
        basis_rows.append(residuals[chosen] / lengths[chosen])
    filters = np.array(basis_rows).reshape(2, poly_order, 2, poly_order)
    return filters.astype(np.float32).astype(np.float64)


def halves(matrix):
    high = matrix.astype(ml_dtypes.bfloat16)
    low = (matrix - high.astype(np.float64)).astype(ml_dtypes.bfloat16)
    return high, low


def left3(matrix):
    high, low = halves(matrix)
    return np.concatenate([high, low, high], axis=-1)


def right3(matrix):
    high, low = halves(matrix)
    return np.concatenate([high, low, high], axis=-2)


@functools.cache
def tables():
    H = two_scale(POLY_ORDER)
    out = {}
    yz = np.einsum("rtbj,uwck->rutwbcjk", H, H)
    yz = yz.reshape(4, 100, 4, 100)
    par = np.zeros((2, 104, 4, 2, 100))
    for i2 in range(2):
        par[i2, :100, :, i2, :] = yz[0]
    par = par.reshape(208, 800)
    out["par"] = left3(par)
    out["parT"] = left3(par.T.copy())
    full = np.zeros((2, 4, 104, 4, 104))
    full[0, :, :100, :, :100] = yz
    full[1, :, :100, :, 4:] = yz
    full = full.reshape(2, 416, 416)
    out["yz"] = left3(full)
    out["yzT"] = left3(full.transpose(0, 2, 1))
    hx = H.reshape(20, 20)
    kx = np.kron(hx, np.eye(8))
    out["x"] = left3(kx)
    out["xT"] = left3(kx.T.copy())
    out["x0"] = left3(kx[:80])
    out["x0T"] = left3(kx[:80].T.copy())
    mid = np.zeros((4, 104, 2, 2, 104))
    mid[:, :100, :, :, :100] = yz.reshape(4, 100, 2, 2, 100).transpose(0, 1, 3, 2, 4)
    mid = mid.reshape(416, 416)
    out["mid"] = left3(mid)
    out["midT"] = left3(mid.T.copy())
    rx = np.zeros((2, 3, 4, 32, 2, 32, 10))
    for tile in range(3):
        for quarter in range(4 if tile < 2 else 2):
            i = 4 * tile + quarter
            for s in range(32):
                rx[:, tile, quarter, s, :, s, :] = H[:, :, :, i].transpose(2, 0, 1)
    rx = rx.reshape(2, 384, 640)
    out["rx"] = np.stack(halves(rx), 0)
    ex = np.zeros((128, 2, 32, 10))
    for p in range(2):
        for m in range(10):
            ex[p * 10 + m, p, :, m] = 1.0
    out["ex"] = ex.reshape(128, 640).astype(ml_dtypes.bfloat16)
    up = np.zeros((2, 2, 104, 128))
    up[:, :, :100, :100] = yz[0].reshape(100, 2, 2, 100).transpose(1, 2, 3, 0)
    out["up"] = left3(up.reshape(2, 208, 128))
    top = np.zeros((4, 128, 4, 128))
    top[:, :100, :, :100] = yz.transpose(2, 3, 0, 1)
    top = top.reshape(512, 512)
    out["top"] = right3(top)
    out["topT"] = right3(top.T.copy())
    one = np.zeros((2, 16, 2, 16))
    one[:, :10, :, :10] = H
    kt = np.kron(np.eye(8), one.reshape(32, 32))
    out["tx"] = left3(kt)
    out["txT"] = left3(kt.T.copy())
    return out


def split(x):
    high = x.astype(BF16)
    low = (x - high.astype(F32)).astype(BF16)
    return high, low


def dot(a, b):
    return lax.dot_general(a, b, (((1,), (0,)), ((), ())), preferred_element_type=F32)


def dot_t(a, b):
    return lax.dot_general(a, b, (((1,), (1,)), ((), ())), preferred_element_type=F32)


def two_rows(product, high, low, m):
    rows = high.shape[0]
    both = product(jnp.concatenate([high, low], 0), m)
    return both[:rows] + both[rows:]


def left_dot(m3, x):
    high, low = split(x)
    return dot(m3, jnp.concatenate([high, high, low], 0))


def right_dot(x, m3):
    high, low = split(x)
    return dot(jnp.concatenate([high, high, low], 1), m3)


def one_hot_dot(x, hot):
    high, low = split(x)
    return dot(high, hot) + dot(low, hot)


def quarter_of(shape):
    return lax.broadcasted_iota(jnp.int32, shape, len(shape) - 1) // 32


def place(pieces, rows):
    mark = quarter_of((rows, 128))
    out = None
    for n, (tile, now) in enumerate(pieces):
        turn = ((n - now) * 32) % 128
        moved = pltpu.roll(tile, turn, 1) if turn else tile
        out = moved if out is None else jnp.where(mark == n, moved, out)
    return out


def vmem(mib):
    return pltpu.CompilerParams(vmem_limit_bytes=mib * 1024 * 1024)


def whole(shape):
    return pl.BlockSpec(shape, lambda *_: (0,) * len(shape))


SMEM = pl.BlockSpec(memory_space=pltpu.SMEM)


def fill_gain(rows_ref, turned_ref, gain_ref, level):
    rows_ref[...] = jnp.zeros_like(rows_ref)
    for k in range(10, 80):
        px, p, m = k // 40, (k // 10) % 4, k % 10
        at = px * 10 + m
        rows_ref[p, at : at + 1, 0:100] = gain_ref[
            level : level + 1, 100 * (k - 10) : 100 * (k - 10) + 100
        ]
    for p in range(4):
        turned_ref[p] = jnp.transpose(rows_ref[p])


VMEM = pl.BlockSpec(memory_space=pltpu.VMEM)
ANY = pl.BlockSpec(memory_space=pl.ANY)


def window(ref, pair):
    return ref.at[pair // 5, :, pair % 5]


def code_hot(route_ref, count, shift):
    row = lax.broadcasted_iota(jnp.int32, (256, 256), 0)
    column = lax.broadcasted_iota(jnp.int32, (256, 256), 1)
    code = 2 * ((row % 32) * 4 + (row // 64 + shift) % 4) + (row // 32) % 2
    hit = (jnp.broadcast_to(route_ref[...], (256, 256)) == code) & (column < count)
    return hit.astype(F32).astype(BF16)


def finest_kernel(
    count_ref, x_ref, route_ref, g_ref, par_hbm, x0_hbm, yz_hbm, x1_hbm, xt_hbm,
    z_ref, block_ref,
    par_ref, x0_ref, yz_ref, x1_ref, xt_ref, xb, acc0, pm, blocks, acc, acc2, grows, gturn,
    csem, sem, osem, own_sem, send, recv,
):
    leaf = lax.axis_index("leaf")
    rep = lax.axis_index("rep")
    barrier = pltpu.get_barrier_semaphore()
    for k in range(1, 4):
        pl.semaphore_signal(
            barrier, inc=1, device_id=(leaf, (rep + k) % 4), device_id_type=MESH
        )
    consts = [
        pltpu.make_async_copy(src, dst, csem.at[n])
        for n, (src, dst) in enumerate(
            (
                (par_hbm, par_ref), (x0_hbm, x0_ref), (yz_hbm, yz_ref), (x1_hbm, x1_ref),
                (xt_hbm, xt_ref),
            )
        )
    ]
    loads = [pltpu.make_async_copy(window(x_ref, n), xb.at[n], sem.at[n]) for n in range(10)]
    consts[0].start()
    for load in loads[:3]:
        load.start()
    consts[1].start()
    hot = code_hot(route_ref, count_ref[0], rep)
    fill_gain(grows, gturn, g_ref, 0)
    consts[0].wait()
    for n in range(10):
        loads[n].wait()
        if n < 7:
            loads[n + 3].start()
        u = left_dot(par_ref[...], xb[n].reshape(800, 256)).reshape(2, 13, 8, 256)
        acc0[:, 2 * n] = u[0]
        acc0[:, 2 * n + 1] = u[1]
    for load in consts[2:]:
        load.start()
    consts[1].wait()
    for t in range(13):
        v = left_dot(x0_ref[...], acc0[t].reshape(160, 256))
        pm[:, 8 * t : 8 * t + 8, :] = v.reshape(10, 8, 256)
    high, low = split(pm[...].reshape(1040, 256))
    y = (dot_t(high, hot) + dot_t(low, hot)).reshape(10, 104, 256)
    def move(k, slot):
        return pltpu.make_async_remote_copy(
            src_ref=blocks.at[k],
            dst_ref=block_ref.at[slot],
            send_sem=send.at[k],
            recv_sem=recv.at[k],
            device_id=(leaf, (rep + k) % 4),
            device_id_type=MESH,
        )

    pl.semaphore_wait(barrier, 3)
    for o in (2, 1, 3, 0):
        tile = y[:, :, (o // 2) * 128 : (o // 2) * 128 + 128]
        base = (o % 2) * 2
        for s in range(2):
            for q in range(2):
                blocks[o, :, (2 * s + q) * 128 : (2 * s + q + 1) * 128] = place(
                    [(tile[4 * q + n], base + s) for n in range(4)], 104
                )
        blocks[o, :, 512:640] = place(
            [(tile[8], base), (tile[9], base), (tile[8], base + 1), (tile[9], base + 1)], 104
        )
        if o:
            move(o, rep).start()
    own = pltpu.make_async_copy(blocks.at[0], block_ref.at[rep], own_sem)
    own.start()

    for load in consts[2:]:
        load.wait()
    for n in range(10):
        for i2 in range(2):
            w = xb[n, :, 96 * i2 : 96 * i2 + 104, :].reshape(416, 256)
            acc[:, 2 * n + i2] = left_dot(yz_ref[i2], w).reshape(52, 8, 256)

    def store(p):
        part = pl.ds(13 * p, 13)
        return pltpu.make_async_copy(acc2.at[part], z_ref.at[part], osem.at[p])

    def quarter(p, carry):
        for n in range(13):
            t = 13 * p + n
            v = left_dot(x1_ref[...], acc[t].reshape(160, 256))
            g = gturn[p, 8 * n : 8 * n + 8, :]
            g = jnp.concatenate(
                [jnp.broadcast_to(g[:, c : c + 1], (8, 256)) for c in range(20)], 0
            )
            acc2[t] = left_dot(xt_ref[...], v * g).reshape(20, 8, 256)
        store(p).start()
        return carry

    lax.fori_loop(0, 4, quarter, 0)
    own.wait()
    for k in range(1, 4):
        move(k, rep).wait_send()
        move(k, (rep + 4 - k) % 4).wait_recv()
    for p in range(4):
        store(p).wait()


def finest_call(x5, count, route, gain):
    T = tables()
    dma = pltpu.SemaphoreType.DMA
    consts = [T[n] for n in ("par", "x0", "yz", "x", "xT")]
    return pl.pallas_call(
        finest_kernel,
        in_specs=[SMEM, ANY, VMEM, VMEM] + [ANY] * 5,
        out_specs=[ANY] * 2,
        out_shape=[
            jax.ShapeDtypeStruct((52, 20, 8, 256), F32),
            jax.ShapeDtypeStruct((4, 104, 640), F32),
        ],
        scratch_shapes=[pltpu.VMEM(c.shape, BF16) for c in consts]
        + [
            pltpu.VMEM((10, 4, 200, 256), F32),
            pltpu.VMEM((13, 20, 8, 256), F32),
            pltpu.VMEM((10, 104, 256), F32),
            pltpu.VMEM((4, 104, 640), F32),
            pltpu.VMEM((52, 20, 8, 256), F32),
            pltpu.VMEM((52, 20, 8, 256), F32),
            pltpu.VMEM((4, 128, 128), F32),
            pltpu.VMEM((4, 128, 128), F32),
            dma((5,)), dma((10,)), dma((4,)), dma, dma((4,)), dma((4,)),
        ],
        compiler_params=pltpu.CompilerParams(
            collective_id=2, has_side_effects=True, vmem_limit_bytes=60 * 1024 * 1024
        ),
        name="finest",
    )(count, x5, route, gain, *consts)


def core_kernel(
    block_ref, route_ref, gain_ref, rx_hbm, mid_hbm, midt_hbm, ex_hbm, top_hbm, tx_hbm,
    txt_hbm, topt_hbm,
    out_ref, coarse_ref, back_ref,
    rx_ref, mid_ref, midt_ref, ex_ref, top_ref, tx_ref, txt_ref, topt_ref,
    got, back, slab, g_ref, way_ref, ways, inv, kids, grown, grows, gturn, g2_ref, tops, news, ways_s, inv_s,
    csem, bsem, own_sem, send, recv, fsend, frecv, wsend, wrecv, zsend, zrecv,
    psend, precv, tsend, trecv,
):
    leaf = lax.axis_index("leaf")
    rep = lax.axis_index("rep")
    core = leaf % 2
    half = leaf // 2
    sibling = leaf + 1 - 2 * core
    turn = leaf % 4
    group = leaf // 4
    first = 4 * group
    across = first + (sibling + 2) % 4
    spot = group * 4 + rep
    barrier = pltpu.get_barrier_semaphore()

    def greet_core(k, carry):
        other = 2 * ((half + k) % 16) + core
        pl.semaphore_signal(barrier, inc=1, device_id=(other, rep), device_id_type=MESH)
        return carry

    def greet_turn(k, carry):
        to = (spot + k) % 32
        pl.semaphore_signal(
            barrier, inc=1, device_id=(4 * (to // 4) + turn, to % 4), device_id_type=MESH
        )
        return carry

    lax.fori_loop(1, 16, greet_core, 0)
    pl.semaphore_signal(barrier, inc=1, device_id=(sibling, rep), device_id_type=MESH)
    pl.semaphore_signal(barrier, inc=1, device_id=(across, rep), device_id_type=MESH)
    lax.fori_loop(1, 32, greet_turn, 0)

    ins = [pltpu.make_async_copy(block_ref, got, bsem)]
    consts = [
        pltpu.make_async_copy(src, dst, csem.at[n])
        for n, (src, dst) in enumerate(
            (
                (rx_hbm, rx_ref), (mid_hbm, mid_ref), (midt_hbm, midt_ref), (ex_hbm, ex_ref),
                (top_hbm, top_ref), (tx_hbm, tx_ref), (txt_hbm, txt_ref), (topt_hbm, topt_ref),
            )
        )
    ]
    for load in ins:
        load.start()
    for load in consts[:2]:
        load.start()
    fill_gain(grows, gturn, gain_ref, 1)
    g2_ref[...] = jnp.zeros_like(g2_ref)
    g2_ref[0:10, 0:100] = jnp.ones((10, 100), F32)
    for k in range(10, 80):
        px, p, m = k // 40, (k // 10) % 4, k % 10
        at = px * 16 + m
        g2_ref[at : at + 1, 128 * p : 128 * p + 100] = gain_ref[
            2:3, 100 * (k - 10) : 100 * (k - 10) + 100
        ]
    way_ref[...] = jnp.full((8, 128), -1, jnp.int32)
    way_ref[0:1, 0:32] = route_ref[...]
    kids[...] = jnp.zeros_like(kids)

    for load in ins:
        load.wait()
    consts[0].wait()
    for load in consts[2:]:
        load.start()
    high_rx, low_rx = rx_ref[0].reshape(768, 640), rx_ref[1].reshape(768, 640)
    rows = []
    for s in range(2):
        for by in range(2):
            parts = []
            for bx in range(2):
                r = 2 * bx + by
                last = got[r, :, 512:640]
                parts += [
                    got[r, :, 256 * s : 256 * s + 256],
                    pltpu.roll(last, 64, 1) if s else last,
                ]
            rows.append(jnp.concatenate(parts, 1))
    x = jnp.concatenate(rows, 0)
    high, low = split(x)
    u = two_rows(dot, high, low, high_rx) + dot(high, low_rx)
    high, low = split(u)
    u3 = jnp.concatenate([high, high, low], 0)
    consts[1].wait()
    v0 = dot(mid_ref[0:128], u3)
    slab[...] = jnp.transpose(v0[:, 0:384])[0:320].reshape(8, 40, 128)

    pl.semaphore_wait(barrier, 48)

    def way_copy(k, slot):
        return pltpu.make_async_remote_copy(
            src_ref=way_ref,
            dst_ref=ways.at[slot],
            send_sem=wsend.at[k],
            recv_sem=wrecv.at[k],
            device_id=(first + (turn + k) % 4, rep),
            device_id_type=MESH,
        )

    for k in range(1, 4):
        way_copy(k, turn).start()
    own_way = pltpu.make_async_copy(way_ref, ways.at[turn], own_sem.at[1])
    own_way.start()

    def out_copy(k):
        to = (half + k) % 16
        return pltpu.make_async_remote_copy(
            src_ref=slab.at[to // 2],
            dst_ref=g_ref.at[leaf],
            send_sem=send.at[k],
            recv_sem=recv.at[k],
            device_id=(2 * to + core, rep),
            device_id_type=MESH,
        )

    def in_copy(k):
        return pltpu.make_async_remote_copy(
            src_ref=slab.at[0],
            dst_ref=g_ref.at[2 * ((half + 16 - k) % 16) + core],
            send_sem=send.at[k],
            recv_sem=recv.at[k],
            device_id=(sibling, rep),
            device_id_type=MESH,
        )

    def pass_copy(k, which):
        slot = 2 * ((half + 16 - k) % 16) + which
        return pltpu.make_async_remote_copy(
            src_ref=g_ref.at[slot],
            dst_ref=g_ref.at[slot],
            send_sem=fsend.at[k],
            recv_sem=frecv.at[k],
            device_id=(sibling, rep),
            device_id_type=MESH,
        )

    def begin(k, carry):
        out_copy(k).start()
        return carry

    own = pltpu.make_async_copy(slab.at[group], g_ref.at[leaf], own_sem.at[0])
    own.start()
    lax.fori_loop(1, 16, begin, 0)

    for load in consts[2:4]:
        load.wait()
    v = jnp.concatenate([v0, dot(mid_ref[128:416], u3)], 0)
    g1 = jnp.concatenate([gturn[p, 0:104, :] for p in range(4)], 0)
    gh, gm = split(g1)
    gl = (g1 - gh.astype(F32) - gm.astype(F32)).astype(BF16)
    gain = dot(gh, ex_ref[...]) + dot(gm, ex_ref[...]) + dot(gl, ex_ref[...])
    w = left_dot(midt_ref[...], v * gain)
    high, low = split(w)
    z = two_rows(dot_t, high, low, high_rx) + dot_t(high, low_rx)
    for by in range(2):
        for bx in range(2):
            r = 2 * bx + by
            last = []
            for s in range(2):
                base = (2 * s + by) * 104
                back[r, :, 256 * s : 256 * s + 256] = z[
                    base : base + 104, 384 * bx : 384 * bx + 256
                ]
                last.append(z[base : base + 104, 384 * bx + 256 : 384 * bx + 384])
            back[r, :, 512:640] = last[0] + pltpu.roll(last[1], 64, 1)

    def home_copy(k, to, slot):
        return pltpu.make_async_remote_copy(
            src_ref=back.at[to],
            dst_ref=back_ref.at[slot],
            send_sem=zsend.at[k],
            recv_sem=zrecv.at[k],
            device_id=(leaf, (rep + k) % 4),
            device_id_type=MESH,
        )

    own.wait()
    pass_copy(0, core).start()

    def relay(k, carry):
        in_copy(k).wait_recv()
        pass_copy(k, core).start()
        return carry

    lax.fori_loop(1, 16, relay, 0)
    for k in range(1, 4):
        home_copy(k, (rep + k) % 4, rep).start()
    own_back = pltpu.make_async_copy(back.at[rep], back_ref.at[rep], own_sem.at[2])
    own_back.start()

    own_way.wait()
    for k in range(1, 4):
        way_copy(k, (turn + 4 - k) % 4).wait_recv()
    code = lax.broadcasted_iota(jnp.int32, (64, 128), 0)
    lane = lax.broadcasted_iota(jnp.int32, (64, 128), 1)
    for t in range(4):
        hit = jnp.broadcast_to(ways[t, 0:1, :], (64, 128)) == code
        found = jnp.max(jnp.where(hit & (lane < 32), lane, -1), axis=1, keepdims=True)
        inv[t] = jnp.broadcast_to(found, (64, 128))
    to_smem = [
        pltpu.make_async_copy(ways, ways_s, own_sem.at[3]),
        pltpu.make_async_copy(inv, inv_s, own_sem.at[4]),
    ]
    for load in to_smem:
        load.start()
    for load in to_smem:
        load.wait()

    def arrive(k, carry):
        pass_copy(k, 1 - core).wait_recv()
        return carry

    lax.fori_loop(0, 16, arrive, 0)

    def gather(n, carry):
        for s in range(2):
            for t in range(4):
                l = inv_s[t, 2 * n + s, 0]
                there = jnp.where(l >= 0, 1.0, 0.0)
                kids[n * 8 + t * 2 + s, 0:10, :] = (
                    g_ref[jnp.clip(l, 0, 31), 10 * t : 10 * t + 10, :] * there
                )
        return carry

    lax.fori_loop(0, 32, gather, 0)
    for load in consts[4:]:
        load.wait()

    sets = kids[...].reshape(32, 2, 4, 16, 128)
    y = jnp.concatenate([sets[:, :, b].reshape(1024, 128) for b in range(4)], 1)
    z = right_dot(y, top_ref[...])
    parts = []
    for g in range(4):
        v = left_dot(tx_ref[...], z[256 * g : 256 * g + 256])
        tops[8 * g : 8 * g + 8] = v.reshape(8, 2, 16, 512)[:, 0, :, 0:128]
        v = (v.reshape(8, 32, 512) * g2_ref[...][None]).reshape(256, 512)
        parts.append(left_dot(txt_ref[...], v))
    y = right_dot(jnp.concatenate(parts, 0), topt_ref[...]).reshape(32, 2, 16, 512)
    for b in range(4):
        grown[:, :, b] = y[:, :, :, 128 * b : 128 * b + 128]

    def pick(n, carry):
        for t in range(4):
            c = ways_s[t, 0, 4 * n + turn]
            home = jnp.clip(c // 2, 0, 31)
            news[n, 10 * t : 10 * t + 10, :] = grown[home, t // 2, (t % 2) * 2 + c % 2, 0:10, :]
        return carry

    lax.fori_loop(0, 8, pick, 0)

    def out_new(k):
        to = (spot + k) % 32
        return pltpu.make_async_remote_copy(
            src_ref=news.at[to // 4],
            dst_ref=out_ref.at[spot],
            send_sem=psend.at[k],
            recv_sem=precv.at[k],
            device_id=(4 * (to // 4) + turn, to % 4),
            device_id_type=MESH,
        )

    def in_new(k):
        return pltpu.make_async_remote_copy(
            src_ref=news.at[0],
            dst_ref=out_ref.at[(spot + 32 - k) % 32],
            send_sem=psend.at[k],
            recv_sem=precv.at[k],
            device_id=(sibling, rep),
            device_id_type=MESH,
        )

    def out_top(k):
        to = 4 * ((group + k) % 8) + turn
        return pltpu.make_async_remote_copy(
            src_ref=tops.at[to],
            dst_ref=coarse_ref.at[group],
            send_sem=tsend.at[k],
            recv_sem=trecv.at[k],
            device_id=(to, rep),
            device_id_type=MESH,
        )

    def in_top(k):
        return pltpu.make_async_remote_copy(
            src_ref=tops.at[0],
            dst_ref=coarse_ref.at[(group + 8 - k) % 8],
            send_sem=tsend.at[k],
            recv_sem=trecv.at[k],
            device_id=(sibling, rep),
            device_id_type=MESH,
        )

    def begin_new(k, carry):
        out_new(k).start()
        return carry

    def begin_top(k, carry):
        out_top(k).start()
        return carry

    lax.fori_loop(1, 32, begin_new, 0)
    lax.fori_loop(1, 8, begin_top, 0)
    own_new = pltpu.make_async_copy(news.at[group], out_ref.at[spot], own_sem.at[5])
    own_new.start()
    own_top = pltpu.make_async_copy(tops.at[leaf], coarse_ref.at[group], own_sem.at[6])
    own_top.start()

    def sent(k, carry):
        out_copy(k).wait_send()
        return carry

    def passed(k, carry):
        pass_copy(k, core).wait_send()
        return carry

    lax.fori_loop(1, 16, sent, 0)
    lax.fori_loop(0, 16, passed, 0)
    for k in range(1, 4):
        way_copy(k, turn).wait_send()
        home_copy(k, (rep + k) % 4, rep).wait_send()
        home_copy(k, (rep + k) % 4, (rep + 4 - k) % 4).wait_recv()

    def finish(k, carry):
        in_new(k).wait_recv()
        out_new(k).wait_send()
        return carry

    def finish_top(k, carry):
        in_top(k).wait_recv()
        out_top(k).wait_send()
        return carry

    lax.fori_loop(1, 32, finish, 0)
    lax.fori_loop(1, 8, finish_top, 0)
    own_back.wait()
    own_new.wait()
    own_top.wait()


def core_call(blocks, route, gain):
    T = tables()
    dma = pltpu.SemaphoreType.DMA
    consts = [T[n] for n in ("rx", "mid", "midT", "ex", "top", "tx", "txT", "topT")]
    return pl.pallas_call(
        core_kernel,
        in_specs=[ANY] + [VMEM] * 2 + [ANY] * 8,
        out_specs=[ANY] * 3,
        out_shape=[
            jax.ShapeDtypeStruct((32, 40, 128), F32),
            jax.ShapeDtypeStruct((8, 16, 128), F32),
            jax.ShapeDtypeStruct((4, 104, 640), F32),
        ],
        scratch_shapes=[pltpu.VMEM(c.shape, BF16) for c in consts]
        + [
            pltpu.VMEM((4, 104, 640), F32),
            pltpu.VMEM((4, 104, 640), F32),
            pltpu.VMEM((8, 40, 128), F32),
            pltpu.VMEM((32, 40, 128), F32),
            pltpu.VMEM((8, 128), jnp.int32),
            pltpu.VMEM((4, 8, 128), jnp.int32),
            pltpu.VMEM((4, 64, 128), jnp.int32),
            pltpu.VMEM((256, 16, 128), F32),
            pltpu.VMEM((32, 2, 4, 16, 128), F32),
            pltpu.VMEM((4, 128, 128), F32),
            pltpu.VMEM((4, 128, 128), F32),
            pltpu.VMEM((32, 512), F32),
            pltpu.VMEM((32, 16, 128), F32),
            pltpu.VMEM((8, 40, 128), F32),
            pltpu.SMEM((4, 8, 128), jnp.int32),
            pltpu.SMEM((4, 64, 128), jnp.int32),
            dma((8,)), dma, dma((7,)),
            dma((16,)), dma((16,)), dma((16,)), dma((16,)),
            dma((4,)), dma((4,)), dma((4,)), dma((4,)),
            dma((32,)), dma((32,)), dma((8,)), dma((8,)),
        ],
        compiler_params=pltpu.CompilerParams(
            collective_id=1, has_side_effects=True, vmem_limit_bytes=60 * 1024 * 1024
        ),
        name="core",
    )(blocks, route, gain, *consts)


def final_kernel(
    count_ref, route_ref, slab_hbm, got_hbm, up_hbm, rx_hbm, x0t_hbm, yzt_hbm, z_ref, top_ref,
    o_ref, coarse_ref, slab_ref, got, up_ref, rx_ref, x0t_ref, yzt_ref, csem, sums, ypos, pnew, big, ob, sem, osem,
):
    loads = [
        pltpu.make_async_copy(
            z_ref.at[pl.ds(13 * p, 13)], big.at[pl.ds(13 * p, 13)], sem.at[p]
        )
        for p in range(4)
    ]
    rep = lax.axis_index("rep")
    by, bx = rep % 2, rep // 2
    firsts = [
        pltpu.make_async_copy(slab_hbm, slab_ref, csem.at[0]),
        pltpu.make_async_copy(up_hbm.at[by], up_ref, csem.at[1]),
        pltpu.make_async_copy(rx_hbm.at[0, bx], rx_ref.at[0], csem.at[2]),
        pltpu.make_async_copy(rx_hbm.at[1, bx], rx_ref.at[1], csem.at[3]),
        pltpu.make_async_copy(got_hbm, got, csem.at[4]),
        pltpu.make_async_copy(x0t_hbm, x0t_ref, csem.at[5]),
    ]
    late = pltpu.make_async_copy(yzt_hbm, yzt_ref, csem.at[6])
    for load in firsts:
        load.start()
    loads[0].start()
    hot = code_hot(route_ref, count_ref[0], 0)
    for m in range(10):
        coarse_ref[:, 100 * m : 100 * m + 100] = top_ref[:, m, 0:100]
    for load in firsts[:2]:
        load.wait()
    late.start()
    for load in loads[1:]:
        load.start()
    mine = slab_ref[...].reshape(8, 4, 40, 128)
    cols = []
    for r in range(4):
        rows = mine[:, r].reshape(320, 128)
        rows = jnp.concatenate([rows, jnp.zeros((64, 128), F32)], 0)
        cols.append(jnp.transpose(rows))
    tall = left_dot(up_ref[...], jnp.concatenate(cols, 1))
    stack = jnp.concatenate(
        [tall[104 * s : 104 * s + 104, 384 * r : 384 * r + 384] for r in range(4) for s in range(2)],
        0,
    )
    high, low = split(stack)
    for load in firsts[2:]:
        load.wait()
    hi_rx = rx_ref[0][:, 0:384]
    lo_rx = rx_ref[1][:, 0:384]
    f = two_rows(dot_t, high, low, hi_rx) + dot_t(high, lo_rx)
    for r in range(4):
        for s in range(2):
            base = (2 * r + s) * 104
            sums[r, :, 256 * s : 256 * s + 256] = (
                got[r, :, 256 * s : 256 * s + 256] + f[base : base + 104, 0:256]
            )
        sums[r, :, 512:640] = got[r, :, 512:640] + f[2 * r * 104 : 2 * r * 104 + 104, 256:384] + pltpu.roll(
            f[(2 * r + 1) * 104 : (2 * r + 2) * 104, 256:384], 64, 1
        )
    for i in range(10):
        for pair in range(2):
            pieces = []
            for r in (2 * pair, 2 * pair + 1):
                for s in range(2):
                    if i < 8:
                        tile = 2 * s + i // 4
                        now = i % 4
                    else:
                        tile = 4
                        now = 2 * s + i - 8
                    pieces.append((sums[r, :, 128 * tile : 128 * tile + 128], now))
            ypos[i, :, 128 * pair : 128 * pair + 128] = place(pieces, 104)
    pnew[...] = one_hot_dot(ypos[...].reshape(1040, 256), hot).reshape(10, 104, 256)
    loads[0].wait()
    for t in range(13):
        w = pnew[:, 8 * t : 8 * t + 8, :].reshape(80, 256)
        big[t] += left_dot(x0t_ref[...], w).reshape(20, 8, 256)
    late.wait()
    for load in loads[1:]:
        load.wait()
    live = lax.broadcasted_iota(jnp.int32, (4, 104, 256), 2) < count_ref[0]
    stores = []
    for n in range(10):
        z = []
        for i2 in range(2):
            w = big[:, 2 * n + i2].reshape(416, 256)
            z.append(jnp.where(live, left_dot(yzt_ref[i2], w).reshape(4, 104, 256), 0.0))
        ob[n, :, 0:96, :] = z[0][:, 0:96]
        ob[n, :, 96:104, :] = z[0][:, 96:104] + z[1][:, 0:8]
        ob[n, :, 104:200, :] = z[1][:, 8:104]
        store = pltpu.make_async_copy(ob.at[n], window(o_ref, n), osem.at[n])
        store.start()
        stores.append(store)
    for store in stores:
        store.wait()


def final_call(count, slabs, blocks, route, z, tops):
    T = tables()
    return pl.pallas_call(
        final_kernel,
        in_specs=[SMEM, VMEM] + [ANY] * 7 + [VMEM],
        out_specs=[ANY, VMEM],
        out_shape=[
            jax.ShapeDtypeStruct((2, 4, 5, 200, 256), F32),
            jax.ShapeDtypeStruct((8, 1000), F32),
        ],
        scratch_shapes=[
            pltpu.VMEM((32, 40, 128), F32),
            pltpu.VMEM((4, 104, 640), F32),
            pltpu.VMEM((208, 384), BF16),
            pltpu.VMEM((2, 384, 640), BF16),
            pltpu.VMEM((160, 240), BF16),
            pltpu.VMEM((2, 416, 1248), BF16),
            pltpu.SemaphoreType.DMA((7,)),
            pltpu.VMEM((4, 104, 640), F32),
            pltpu.VMEM((10, 104, 256), F32),
            pltpu.VMEM((10, 104, 256), F32),
            pltpu.VMEM((52, 20, 8, 256), F32),
            pltpu.VMEM((10, 4, 200, 256), F32),
            pltpu.SemaphoreType.DMA((4,)),
            pltpu.SemaphoreType.DMA((10,)),
        ],
        compiler_params=vmem(60),
        name="final",
    )(count, route, slabs, blocks, T["up"], T["rx"], T["x0T"], T["yzT"], z, tops)


def shards(fine_coeffs, set_counts, route_first, route_top, level_gain):
    route = route_first.reshape(1, 256)
    x5 = fine_coeffs.reshape(2, 4, 5, 200, 256)
    z, blocks = finest_call(x5, set_counts, route, level_gain)
    new, tops, back = core_call(blocks, route_top.reshape(1, 32), level_gain)
    out, coarse = final_call(set_counts, new, back, route, z, tops)
    return (out.reshape(8000, 256), coarse.T)


def solution(mesh):
    placed = (
        P(None, ("leaf", "rep")),
        P(("leaf", "rep")),
        P(("leaf", "rep")),
        P(("leaf", "rep")),
        P(),
    )
    return jax.shard_map(
        shards,
        mesh=mesh,
        in_specs=placed,
        out_specs=(P(None, ("leaf", "rep")), P(None, ("leaf", "rep"))),
        check_vma=False,
    )
```

```python
import functools
import math

import jax
import jax.numpy as jnp
import ml_dtypes
import numpy as np
from jax import lax
from jax.experimental import pallas as pl
from jax.experimental.pallas import tpu as pltpu
from jax.sharding import PartitionSpec as P

POLY_ORDER = 10
F32 = jnp.float32
BF16 = jnp.bfloat16
MESH = pl.DeviceIdType.MESH


def legendre_pair(count, position):
    before, current = (1.0, position)
    for degree in range(1, count):
        before, current = (
            current,
            ((2 * degree + 1) * position * current - degree * before) / (degree + 1),
        )
    derivative = count * (position * current - before) / (position * position - 1.0)
    return (current, derivative)


def gauss_points(count):
    nodes = []
    weights = []
    for node_index in range(count):
        estimate = math.cos(math.pi * (node_index + 0.75) / (count + 0.5))
        for newton_step in range(100):
            current, derivative = legendre_pair(count, estimate)
            estimate = estimate - current / derivative
        current, derivative = legendre_pair(count, estimate)
        nodes.append(estimate)
        weights.append(2.0 / ((1.0 - estimate * estimate) * derivative * derivative))
    return (np.array(nodes), np.array(weights))


def legendre_rows(degree_count, points):
    values = [points * 0.0 + 1.0, points.copy()]
    for degree in range(1, degree_count - 1):
        values.append(
            ((2 * degree + 1) * points * values[degree] - degree * values[degree - 1])
            / (degree + 1)
        )
    return np.stack(
        [np.sqrt(2.0 * degree + 1.0) * values[degree] for degree in range(degree_count)]
    )


@functools.cache
def two_scale(poly_order):
    points, weights = gauss_points(2 * poly_order)
    lower_half = (points + 1.0) / 4.0
    half_weights = weights / 4.0
    child_rows = legendre_rows(poly_order, 4.0 * lower_half - 1.0)
    parent_low = legendre_rows(poly_order, 2.0 * lower_half - 1.0)
    parent_high = legendre_rows(poly_order, 2.0 * (lower_half + 0.5) - 1.0)
    filter_left = math.sqrt(2.0) * (parent_low * half_weights) @ child_rows.T
    filter_right = math.sqrt(2.0) * (parent_high * half_weights) @ child_rows.T
    basis_rows = list(np.concatenate([filter_left, filter_right], axis=1))
    units = np.eye(2 * poly_order)
    for step_index in range(poly_order):
        residuals = []
        for vector in units:
            for sweep in range(2):
                for previous in basis_rows:
                    vector = vector - np.dot(previous, vector) * previous
            residuals.append(vector)
        lengths = np.array([np.sqrt(np.dot(vector, vector)) for vector in residuals])
        chosen = int(np.argmax(lengths))
        basis_rows.append(residuals[chosen] / lengths[chosen])
    filters = np.array(basis_rows).reshape(2, poly_order, 2, poly_order)
    return filters.astype(np.float32).astype(np.float64)


def halves(matrix):
    high = matrix.astype(ml_dtypes.bfloat16)
    low = (matrix - high.astype(np.float64)).astype(ml_dtypes.bfloat16)
    return high, low


def left3(matrix):
    high, low = halves(matrix)
    return np.concatenate([high, low, high], axis=-1)


def right3(matrix):
    high, low = halves(matrix)
    return np.concatenate([high, low, high], axis=-2)


@functools.cache
def tables():
    H = two_scale(POLY_ORDER)
    out = {}
    yz = np.einsum("rtbj,uwck->rutwbcjk", H, H)
    yz = yz.reshape(4, 100, 4, 100)
    par = np.zeros((2, 104, 4, 2, 100))
    for i2 in range(2):
        par[i2, :100, :, i2, :] = yz[0]
    par = par.reshape(208, 800)
    out["par"] = left3(par)
    out["parT"] = left3(par.T.copy())
    full = np.zeros((2, 4, 104, 4, 104))
    full[0, :, :100, :, :100] = yz
    full[1, :, :100, :, 4:] = yz
    full = full.reshape(2, 416, 416)
    out["yz"] = left3(full)
    out["yzT"] = left3(full.transpose(0, 2, 1))
    hx = H.reshape(20, 20)
    kx = np.kron(hx, np.eye(8))
    out["x"] = left3(kx)
    out["xT"] = left3(kx.T.copy())
    out["x0"] = left3(kx[:80])
    out["x0T"] = left3(kx[:80].T.copy())
    mid = np.zeros((4, 104, 2, 2, 104))
    mid[:, :100, :, :, :100] = yz.reshape(4, 100, 2, 2, 100).transpose(0, 1, 3, 2, 4)
    mid = mid.reshape(416, 416)
    out["mid"] = left3(mid)
    out["midT"] = left3(mid.T.copy())
    rx = np.zeros((2, 3, 4, 32, 2, 32, 10))
    for tile in range(3):
        for quarter in range(4 if tile < 2 else 2):
            i = 4 * tile + quarter
            for s in range(32):
                rx[:, tile, quarter, s, :, s, :] = H[:, :, :, i].transpose(2, 0, 1)
    rx = rx.reshape(2, 384, 640)
    out["rx"] = np.stack(halves(rx), 0)
    ex = np.zeros((128, 2, 32, 10))
    for p in range(2):
        for m in range(10):
            ex[p * 10 + m, p, :, m] = 1.0
    out["ex"] = ex.reshape(128, 640).astype(ml_dtypes.bfloat16)
    up = np.zeros((2, 2, 104, 128))
    up[:, :, :100, :100] = yz[0].reshape(100, 2, 2, 100).transpose(1, 2, 3, 0)
    out["up"] = left3(up.reshape(2, 208, 128))
    top = np.zeros((4, 128, 4, 128))
    top[:, :100, :, :100] = yz.transpose(2, 3, 0, 1)
    top = top.reshape(512, 512)
    out["top"] = right3(top)
    out["topT"] = right3(top.T.copy())
    one = np.zeros((2, 16, 2, 16))
    one[:, :10, :, :10] = H
    kt = np.kron(np.eye(8), one.reshape(32, 32))
    out["tx"] = left3(kt)
    out["txT"] = left3(kt.T.copy())
    return out


def split(x):
    high = x.astype(BF16)
    low = (x - high.astype(F32)).astype(BF16)
    return high, low


def dot(a, b):
    return lax.dot_general(a, b, (((1,), (0,)), ((), ())), preferred_element_type=F32)


def dot_t(a, b):
    return lax.dot_general(a, b, (((1,), (1,)), ((), ())), preferred_element_type=F32)


def two_rows(product, high, low, m):
    rows = high.shape[0]
    both = product(jnp.concatenate([high, low], 0), m)
    return both[:rows] + both[rows:]


def left_dot(m3, x):
    high, low = split(x)
    return dot(m3, jnp.concatenate([high, high, low], 0))


def right_dot(x, m3):
    high, low = split(x)
    return dot(jnp.concatenate([high, high, low], 1), m3)


def one_hot_dot(x, hot):
    high, low = split(x)
    return dot(high, hot) + dot(low, hot)


def quarter_of(shape):
    return lax.broadcasted_iota(jnp.int32, shape, len(shape) - 1) // 32


def place(pieces, rows):
    mark = quarter_of((rows, 128))
    out = None
    for n, (tile, now) in enumerate(pieces):
        turn = ((n - now) * 32) % 128
        moved = pltpu.roll(tile, turn, 1) if turn else tile
        out = moved if out is None else jnp.where(mark == n, moved, out)
    return out


def vmem(mib):
    return pltpu.CompilerParams(vmem_limit_bytes=mib * 1024 * 1024)


def whole(shape):
    return pl.BlockSpec(shape, lambda *_: (0,) * len(shape))


SMEM = pl.BlockSpec(memory_space=pltpu.SMEM)


def fill_gain(rows_ref, turned_ref, gain_ref, level):
    rows_ref[...] = jnp.zeros_like(rows_ref)
    for k in range(10, 80):
        px, p, m = k // 40, (k // 10) % 4, k % 10
        at = px * 10 + m
        rows_ref[p, at : at + 1, 0:100] = gain_ref[
            level : level + 1, 100 * (k - 10) : 100 * (k - 10) + 100
        ]
    for p in range(4):
        turned_ref[p] = jnp.transpose(rows_ref[p])


VMEM = pl.BlockSpec(memory_space=pltpu.VMEM)
ANY = pl.BlockSpec(memory_space=pl.ANY)


def window(ref, pair):
    return ref.at[pair // 5, :, pair % 5]


def code_hot(route_ref, count, shift):
    row = lax.broadcasted_iota(jnp.int32, (256, 256), 0)
    column = lax.broadcasted_iota(jnp.int32, (256, 256), 1)
    code = 2 * ((row % 32) * 4 + (row // 64 + shift) % 4) + (row // 32) % 2
    hit = (jnp.broadcast_to(route_ref[...], (256, 256)) == code) & (column < count)
    return hit.astype(F32).astype(BF16)


def finest_kernel(
    count_ref, x_ref, route_ref, g_ref, yz_hbm, x0_hbm, x1_hbm, xt_hbm,
    z_ref, block_ref,
    yz_ref, x0_ref, x1_ref, xt_ref, xb, pm, blocks, up_half, down_half, acc, acc2, grows, gturn,
    csem, sem, osem, own_sem, send, recv,
):
    leaf = lax.axis_index("leaf")
    rep = lax.axis_index("rep")
    barrier = pltpu.get_barrier_semaphore()
    for k in (1, 3):
        pl.semaphore_signal(
            barrier, inc=1, device_id=(leaf, (rep + k) % 4), device_id_type=MESH
        )
    consts = [
        pltpu.make_async_copy(src, dst, csem.at[n])
        for n, (src, dst) in enumerate(
            (
                (yz_hbm, yz_ref), (x0_hbm, x0_ref), (x1_hbm, x1_ref), (xt_hbm, xt_ref),
            )
        )
    ]
    loads = [pltpu.make_async_copy(window(x_ref, n), xb.at[n], sem.at[n]) for n in range(10)]
    consts[0].start()
    for load in loads[:3]:
        load.start()
    consts[1].start()
    hot = code_hot(route_ref, count_ref[0], rep)
    fill_gain(grows, gturn, g_ref, 0)
    consts[0].wait()
    for n in range(10):
        loads[n].wait()
        if n < 7:
            loads[n + 3].start()
        for i2 in range(2):
            w = xb[n, :, 96 * i2 : 96 * i2 + 104, :].reshape(416, 256)
            acc[:, 2 * n + i2] = left_dot(yz_ref[i2], w).reshape(52, 8, 256)
    for load in consts[2:]:
        load.start()
    consts[1].wait()
    for t in range(13):
        v = left_dot(x0_ref[...], acc[t].reshape(160, 256))
        pm[:, 8 * t : 8 * t + 8, :] = v.reshape(10, 8, 256)
    high, low = split(pm[...].reshape(1040, 256))
    y = (dot_t(high, hot) + dot_t(low, hot)).reshape(10, 104, 256)
    high_part, low_part = pl.ds(0, 56), pl.ds(56, 48)

    def hop(n, src, dst, step):
        return pltpu.make_async_remote_copy(
            src_ref=src,
            dst_ref=dst,
            send_sem=send.at[n],
            recv_sem=recv.at[n],
            device_id=(leaf, (rep + step) % 4),
            device_id_type=MESH,
        )

    def near(k, slot):
        return hop(k, blocks.at[k], block_ref.at[slot], k)

    def up_first():
        return hop(0, blocks.at[2, high_part], up_half, 1)

    def down_first():
        return hop(2, blocks.at[2, low_part], down_half, 3)

    def up_second(slot):
        return hop(4, up_half, block_ref.at[slot, high_part], 1)

    def down_second(slot):
        return hop(5, down_half, block_ref.at[slot, low_part], 3)

    pl.semaphore_wait(barrier, 2)
    for o in (2, 1, 3, 0):
        tile = y[:, :, (o // 2) * 128 : (o // 2) * 128 + 128]
        base = (o % 2) * 2
        for s in range(2):
            for q in range(2):
                blocks[o, :, (2 * s + q) * 128 : (2 * s + q + 1) * 128] = place(
                    [(tile[4 * q + n], base + s) for n in range(4)], 104
                )
        blocks[o, :, 512:640] = place(
            [(tile[8], base), (tile[9], base), (tile[8], base + 1), (tile[9], base + 1)], 104
        )
        if o == 2:
            up_first().start()
            down_first().start()
        elif o:
            near(o, rep).start()
    own = pltpu.make_async_copy(blocks.at[0], block_ref.at[rep], own_sem)
    own.start()

    for load in consts[2:]:
        load.wait()

    def store(p):
        part = pl.ds(13 * p, 13)
        return pltpu.make_async_copy(acc2.at[part], z_ref.at[part], osem.at[p])

    def quarter(p, carry):
        for n in range(13):
            t = 13 * p + n
            v = left_dot(x1_ref[...], acc[t].reshape(160, 256))
            g = gturn[p, 8 * n : 8 * n + 8, :]
            g = jnp.concatenate(
                [jnp.broadcast_to(g[:, c : c + 1], (8, 256)) for c in range(20)], 0
            )
            acc2[t] = left_dot(xt_ref[...], v * g).reshape(20, 8, 256)
        store(p).start()
        return carry

    lax.fori_loop(0, 2, quarter, 0)
    up_first().wait_recv()
    up_second((rep + 3) % 4).start()
    down_first().wait_recv()
    down_second((rep + 1) % 4).start()
    lax.fori_loop(2, 4, quarter, 0)
    own.wait()
    up_first().wait_send()
    down_first().wait_send()
    for k in (1, 3):
        near(k, rep).wait_send()
        near(k, (rep + 4 - k) % 4).wait_recv()
    up_second((rep + 3) % 4).wait_send()
    down_second((rep + 1) % 4).wait_send()
    up_second((rep + 2) % 4).wait_recv()
    down_second((rep + 2) % 4).wait_recv()
    for p in range(4):
        store(p).wait()


def finest_call(x5, count, route, gain):
    T = tables()
    dma = pltpu.SemaphoreType.DMA
    consts = [T[n] for n in ("yz", "x0", "x", "xT")]
    return pl.pallas_call(
        finest_kernel,
        in_specs=[SMEM, ANY, VMEM, VMEM] + [ANY] * 4,
        out_specs=[ANY] * 2,
        out_shape=[
            jax.ShapeDtypeStruct((52, 20, 8, 256), F32),
            jax.ShapeDtypeStruct((4, 104, 640), F32),
        ],
        scratch_shapes=[pltpu.VMEM(c.shape, BF16) for c in consts]
        + [
            pltpu.VMEM((10, 4, 200, 256), F32),
            pltpu.VMEM((10, 104, 256), F32),
            pltpu.VMEM((4, 104, 640), F32),
            pltpu.VMEM((56, 640), F32),
            pltpu.VMEM((48, 640), F32),
            pltpu.VMEM((52, 20, 8, 256), F32),
            pltpu.VMEM((52, 20, 8, 256), F32),
            pltpu.VMEM((4, 128, 128), F32),
            pltpu.VMEM((4, 128, 128), F32),
            dma((4,)), dma((10,)), dma((4,)), dma, dma((6,)), dma((6,)),
        ],
        compiler_params=pltpu.CompilerParams(
            collective_id=2, has_side_effects=True, vmem_limit_bytes=60 * 1024 * 1024
        ),
        name="finest",
    )(count, x5, route, gain, *consts)


def core_kernel(
    block_ref, route_ref, gain_ref, rx_hbm, mid_hbm, midt_hbm, ex_hbm, top_hbm, tx_hbm,
    txt_hbm, topt_hbm,
    out_ref, coarse_ref, back_ref,
    rx_ref, mid_ref, midt_ref, ex_ref, top_ref, tx_ref, txt_ref, topt_ref,
    got, back, slab, g_ref, way_ref, ways, inv, kids, grown, grows, gturn, g2_ref, tops, news, ways_s, inv_s,
    csem, bsem, own_sem, send, recv, fsend, frecv, wsend, wrecv, zsend, zrecv,
    psend, precv, tsend, trecv,
):
    leaf = lax.axis_index("leaf")
    rep = lax.axis_index("rep")
    core = leaf % 2
    half = leaf // 2
    sibling = leaf + 1 - 2 * core
    turn = leaf % 4
    group = leaf // 4
    first = 4 * group
    across = first + (sibling + 2) % 4
    spot = group * 4 + rep
    barrier = pltpu.get_barrier_semaphore()

    def greet_core(k, carry):
        other = 2 * ((half + k) % 16) + core
        pl.semaphore_signal(barrier, inc=1, device_id=(other, rep), device_id_type=MESH)
        return carry

    def greet_turn(k, carry):
        to = (spot + k) % 32
        pl.semaphore_signal(
            barrier, inc=1, device_id=(4 * (to // 4) + turn, to % 4), device_id_type=MESH
        )
        return carry

    lax.fori_loop(1, 16, greet_core, 0)
    pl.semaphore_signal(barrier, inc=1, device_id=(sibling, rep), device_id_type=MESH)
    pl.semaphore_signal(barrier, inc=1, device_id=(across, rep), device_id_type=MESH)
    lax.fori_loop(1, 32, greet_turn, 0)

    ins = [pltpu.make_async_copy(block_ref, got, bsem)]
    consts = [
        pltpu.make_async_copy(src, dst, csem.at[n])
        for n, (src, dst) in enumerate(
            (
                (rx_hbm, rx_ref), (mid_hbm, mid_ref), (midt_hbm, midt_ref), (ex_hbm, ex_ref),
                (top_hbm, top_ref), (tx_hbm, tx_ref), (txt_hbm, txt_ref), (topt_hbm, topt_ref),
            )
        )
    ]
    for load in ins:
        load.start()
    for load in consts[:2]:
        load.start()
    fill_gain(grows, gturn, gain_ref, 1)
    g2_ref[...] = jnp.zeros_like(g2_ref)
    g2_ref[0:10, 0:100] = jnp.ones((10, 100), F32)
    for k in range(10, 80):
        px, p, m = k // 40, (k // 10) % 4, k % 10
        at = px * 16 + m
        g2_ref[at : at + 1, 128 * p : 128 * p + 100] = gain_ref[
            2:3, 100 * (k - 10) : 100 * (k - 10) + 100
        ]
    way_ref[...] = jnp.full((8, 128), -1, jnp.int32)
    way_ref[0:1, 0:32] = route_ref[...]
    kids[...] = jnp.zeros_like(kids)

    for load in ins:
        load.wait()
    consts[0].wait()
    for load in consts[2:]:
        load.start()
    high_rx, low_rx = rx_ref[0].reshape(768, 640), rx_ref[1].reshape(768, 640)
    rows = []
    for s in range(2):
        for by in range(2):
            parts = []
            for bx in range(2):
                r = 2 * bx + by
                last = got[r, :, 512:640]
                parts += [
                    got[r, :, 256 * s : 256 * s + 256],
                    pltpu.roll(last, 64, 1) if s else last,
                ]
            rows.append(jnp.concatenate(parts, 1))
    x = jnp.concatenate(rows, 0)
    high, low = split(x)
    u = two_rows(dot, high, low, high_rx) + dot(high, low_rx)
    high, low = split(u)
    u3 = jnp.concatenate([high, high, low], 0)
    consts[1].wait()
    v0 = dot(mid_ref[0:128], u3)
    slab[...] = jnp.transpose(v0[:, 0:384])[0:320].reshape(8, 40, 128)

    pl.semaphore_wait(barrier, 48)

    def way_copy(k, slot):
        return pltpu.make_async_remote_copy(
            src_ref=way_ref,
            dst_ref=ways.at[slot],
            send_sem=wsend.at[k],
            recv_sem=wrecv.at[k],
            device_id=(first + (turn + k) % 4, rep),
            device_id_type=MESH,
        )

    for k in range(1, 4):
        way_copy(k, turn).start()
    own_way = pltpu.make_async_copy(way_ref, ways.at[turn], own_sem.at[1])
    own_way.start()

    def out_copy(k):
        to = (half + k) % 16
        return pltpu.make_async_remote_copy(
            src_ref=slab.at[to // 2],
            dst_ref=g_ref.at[leaf],
            send_sem=send.at[k],
            recv_sem=recv.at[k],
            device_id=(2 * to + core, rep),
            device_id_type=MESH,
        )

    def in_copy(k):
        return pltpu.make_async_remote_copy(
            src_ref=slab.at[0],
            dst_ref=g_ref.at[2 * ((half + 16 - k) % 16) + core],
            send_sem=send.at[k],
            recv_sem=recv.at[k],
            device_id=(sibling, rep),
            device_id_type=MESH,
        )

    def pass_copy(k, which):
        slot = 2 * ((half + 16 - k) % 16) + which
        return pltpu.make_async_remote_copy(
            src_ref=g_ref.at[slot],
            dst_ref=g_ref.at[slot],
            send_sem=fsend.at[k],
            recv_sem=frecv.at[k],
            device_id=(sibling, rep),
            device_id_type=MESH,
        )

    def begin(k, carry):
        out_copy(k).start()
        return carry

    own = pltpu.make_async_copy(slab.at[group], g_ref.at[leaf], own_sem.at[0])
    own.start()
    lax.fori_loop(1, 16, begin, 0)

    for load in consts[2:4]:
        load.wait()
    v = jnp.concatenate([v0, dot(mid_ref[128:416], u3)], 0)
    g1 = jnp.concatenate([gturn[p, 0:104, :] for p in range(4)], 0)
    gh, gm = split(g1)
    gl = (g1 - gh.astype(F32) - gm.astype(F32)).astype(BF16)
    gain = dot(gh, ex_ref[...]) + dot(gm, ex_ref[...]) + dot(gl, ex_ref[...])
    w = left_dot(midt_ref[...], v * gain)
    high, low = split(w)
    z = two_rows(dot_t, high, low, high_rx) + dot_t(high, low_rx)
    for by in range(2):
        for bx in range(2):
            r = 2 * bx + by
            last = []
            for s in range(2):
                base = (2 * s + by) * 104
                back[r, :, 256 * s : 256 * s + 256] = z[
                    base : base + 104, 384 * bx : 384 * bx + 256
                ]
                last.append(z[base : base + 104, 384 * bx + 256 : 384 * bx + 384])
            back[r, :, 512:640] = last[0] + pltpu.roll(last[1], 64, 1)

    def home_copy(k, to, slot):
        return pltpu.make_async_remote_copy(
            src_ref=back.at[to],
            dst_ref=back_ref.at[slot],
            send_sem=zsend.at[k],
            recv_sem=zrecv.at[k],
            device_id=(leaf, (rep + k) % 4),
            device_id_type=MESH,
        )

    own.wait()
    pass_copy(0, core).start()

    def relay(k, carry):
        in_copy(k).wait_recv()
        pass_copy(k, core).start()
        return carry

    lax.fori_loop(1, 16, relay, 0)
    for k in range(1, 4):
        home_copy(k, (rep + k) % 4, rep).start()
    own_back = pltpu.make_async_copy(back.at[rep], back_ref.at[rep], own_sem.at[2])
    own_back.start()

    own_way.wait()
    for k in range(1, 4):
        way_copy(k, (turn + 4 - k) % 4).wait_recv()
    code = lax.broadcasted_iota(jnp.int32, (64, 128), 0)
    lane = lax.broadcasted_iota(jnp.int32, (64, 128), 1)
    for t in range(4):
        hit = jnp.broadcast_to(ways[t, 0:1, :], (64, 128)) == code
        found = jnp.max(jnp.where(hit & (lane < 32), lane, -1), axis=1, keepdims=True)
        inv[t] = jnp.broadcast_to(found, (64, 128))
    to_smem = [
        pltpu.make_async_copy(ways, ways_s, own_sem.at[3]),
        pltpu.make_async_copy(inv, inv_s, own_sem.at[4]),
    ]
    for load in to_smem:
        load.start()
    for load in to_smem:
        load.wait()

    def arrive(k, carry):
        pass_copy(k, 1 - core).wait_recv()
        return carry

    lax.fori_loop(0, 16, arrive, 0)

    def gather(n, carry):
        for s in range(2):
            for t in range(4):
                l = inv_s[t, 2 * n + s, 0]
                there = jnp.where(l >= 0, 1.0, 0.0)
                kids[n * 8 + t * 2 + s, 0:10, :] = (
                    g_ref[jnp.clip(l, 0, 31), 10 * t : 10 * t + 10, :] * there
                )
        return carry

    lax.fori_loop(0, 32, gather, 0)
    for load in consts[4:]:
        load.wait()

    sets = kids[...].reshape(32, 2, 4, 16, 128)
    y = jnp.concatenate([sets[:, :, b].reshape(1024, 128) for b in range(4)], 1)
    z = right_dot(y, top_ref[...])
    parts = []
    for g in range(4):
        v = left_dot(tx_ref[...], z[256 * g : 256 * g + 256])
        tops[8 * g : 8 * g + 8] = v.reshape(8, 2, 16, 512)[:, 0, :, 0:128]
        v = (v.reshape(8, 32, 512) * g2_ref[...][None]).reshape(256, 512)
        parts.append(left_dot(txt_ref[...], v))
    y = right_dot(jnp.concatenate(parts, 0), topt_ref[...]).reshape(32, 2, 16, 512)
    for b in range(4):
        grown[:, :, b] = y[:, :, :, 128 * b : 128 * b + 128]

    def pick(n, carry):
        for t in range(4):
            c = ways_s[t, 0, 4 * n + turn]
            home = jnp.clip(c // 2, 0, 31)
            news[n, 10 * t : 10 * t + 10, :] = grown[home, t // 2, (t % 2) * 2 + c % 2, 0:10, :]
        return carry

    lax.fori_loop(0, 8, pick, 0)

    def out_new(k):
        to = (spot + k) % 32
        return pltpu.make_async_remote_copy(
            src_ref=news.at[to // 4],
            dst_ref=out_ref.at[spot],
            send_sem=psend.at[k],
            recv_sem=precv.at[k],
            device_id=(4 * (to // 4) + turn, to % 4),
            device_id_type=MESH,
        )

    def in_new(k):
        return pltpu.make_async_remote_copy(
            src_ref=news.at[0],
            dst_ref=out_ref.at[(spot + 32 - k) % 32],
            send_sem=psend.at[k],
            recv_sem=precv.at[k],
            device_id=(sibling, rep),
            device_id_type=MESH,
        )

    def out_top(k):
        to = 4 * ((group + k) % 8) + turn
        return pltpu.make_async_remote_copy(
            src_ref=tops.at[to],
            dst_ref=coarse_ref.at[group],
            send_sem=tsend.at[k],
            recv_sem=trecv.at[k],
            device_id=(to, rep),
            device_id_type=MESH,
        )

    def in_top(k):
        return pltpu.make_async_remote_copy(
            src_ref=tops.at[0],
            dst_ref=coarse_ref.at[(group + 8 - k) % 8],
            send_sem=tsend.at[k],
            recv_sem=trecv.at[k],
            device_id=(sibling, rep),
            device_id_type=MESH,
        )

    def begin_new(k, carry):
        out_new(k).start()
        return carry

    def begin_top(k, carry):
        out_top(k).start()
        return carry

    lax.fori_loop(1, 32, begin_new, 0)
    lax.fori_loop(1, 8, begin_top, 0)
    own_new = pltpu.make_async_copy(news.at[group], out_ref.at[spot], own_sem.at[5])
    own_new.start()
    own_top = pltpu.make_async_copy(tops.at[leaf], coarse_ref.at[group], own_sem.at[6])
    own_top.start()

    def sent(k, carry):
        out_copy(k).wait_send()
        return carry

    def passed(k, carry):
        pass_copy(k, core).wait_send()
        return carry

    lax.fori_loop(1, 16, sent, 0)
    lax.fori_loop(0, 16, passed, 0)
    for k in range(1, 4):
        way_copy(k, turn).wait_send()
        home_copy(k, (rep + k) % 4, rep).wait_send()
        home_copy(k, (rep + k) % 4, (rep + 4 - k) % 4).wait_recv()

    def finish(k, carry):
        in_new(k).wait_recv()
        out_new(k).wait_send()
        return carry

    def finish_top(k, carry):
        in_top(k).wait_recv()
        out_top(k).wait_send()
        return carry

    lax.fori_loop(1, 32, finish, 0)
    lax.fori_loop(1, 8, finish_top, 0)
    own_back.wait()
    own_new.wait()
    own_top.wait()


def core_call(blocks, route, gain):
    T = tables()
    dma = pltpu.SemaphoreType.DMA
    consts = [T[n] for n in ("rx", "mid", "midT", "ex", "top", "tx", "txT", "topT")]
    return pl.pallas_call(
        core_kernel,
        in_specs=[ANY] + [VMEM] * 2 + [ANY] * 8,
        out_specs=[ANY] * 3,
        out_shape=[
            jax.ShapeDtypeStruct((32, 40, 128), F32),
            jax.ShapeDtypeStruct((8, 16, 128), F32),
            jax.ShapeDtypeStruct((4, 104, 640), F32),
        ],
        scratch_shapes=[pltpu.VMEM(c.shape, BF16) for c in consts]
        + [
            pltpu.VMEM((4, 104, 640), F32),
            pltpu.VMEM((4, 104, 640), F32),
            pltpu.VMEM((8, 40, 128), F32),
            pltpu.VMEM((32, 40, 128), F32),
            pltpu.VMEM((8, 128), jnp.int32),
            pltpu.VMEM((4, 8, 128), jnp.int32),
            pltpu.VMEM((4, 64, 128), jnp.int32),
            pltpu.VMEM((256, 16, 128), F32),
            pltpu.VMEM((32, 2, 4, 16, 128), F32),
            pltpu.VMEM((4, 128, 128), F32),
            pltpu.VMEM((4, 128, 128), F32),
            pltpu.VMEM((32, 512), F32),
            pltpu.VMEM((32, 16, 128), F32),
            pltpu.VMEM((8, 40, 128), F32),
            pltpu.SMEM((4, 8, 128), jnp.int32),
            pltpu.SMEM((4, 64, 128), jnp.int32),
            dma((8,)), dma, dma((7,)),
            dma((16,)), dma((16,)), dma((16,)), dma((16,)),
            dma((4,)), dma((4,)), dma((4,)), dma((4,)),
            dma((32,)), dma((32,)), dma((8,)), dma((8,)),
        ],
        compiler_params=pltpu.CompilerParams(
            collective_id=1, has_side_effects=True, vmem_limit_bytes=60 * 1024 * 1024
        ),
        name="core",
    )(blocks, route, gain, *consts)


def final_kernel(
    count_ref, route_ref, slab_hbm, got_hbm, up_hbm, rx_hbm, x0t_hbm, yzt_hbm, z_ref, top_ref,
    o_ref, coarse_ref, slab_ref, got, up_ref, rx_ref, x0t_ref, yzt_ref, csem, sums, ypos, pnew, big, ob, sem, osem,
):
    loads = [
        pltpu.make_async_copy(
            z_ref.at[pl.ds(13 * p, 13)], big.at[pl.ds(13 * p, 13)], sem.at[p]
        )
        for p in range(4)
    ]
    rep = lax.axis_index("rep")
    by, bx = rep % 2, rep // 2
    firsts = [
        pltpu.make_async_copy(slab_hbm, slab_ref, csem.at[0]),
        pltpu.make_async_copy(up_hbm.at[by], up_ref, csem.at[1]),
        pltpu.make_async_copy(rx_hbm.at[0, bx], rx_ref.at[0], csem.at[2]),
        pltpu.make_async_copy(rx_hbm.at[1, bx], rx_ref.at[1], csem.at[3]),
        pltpu.make_async_copy(got_hbm, got, csem.at[4]),
        pltpu.make_async_copy(x0t_hbm, x0t_ref, csem.at[5]),
    ]
    late = pltpu.make_async_copy(yzt_hbm, yzt_ref, csem.at[6])
    for load in firsts:
        load.start()
    loads[0].start()
    hot = code_hot(route_ref, count_ref[0], 0)
    for m in range(10):
        coarse_ref[:, 100 * m : 100 * m + 100] = top_ref[:, m, 0:100]
    for load in firsts[:2]:
        load.wait()
    late.start()
    for load in loads[1:]:
        load.start()
    mine = slab_ref[...].reshape(8, 4, 40, 128)
    cols = []
    for r in range(4):
        rows = mine[:, r].reshape(320, 128)
        rows = jnp.concatenate([rows, jnp.zeros((64, 128), F32)], 0)
        cols.append(jnp.transpose(rows))
    tall = left_dot(up_ref[...], jnp.concatenate(cols, 1))
    stack = jnp.concatenate(
        [tall[104 * s : 104 * s + 104, 384 * r : 384 * r + 384] for r in range(4) for s in range(2)],
        0,
    )
    high, low = split(stack)
    for load in firsts[2:]:
        load.wait()
    hi_rx = rx_ref[0][:, 0:384]
    lo_rx = rx_ref[1][:, 0:384]
    f = two_rows(dot_t, high, low, hi_rx) + dot_t(high, lo_rx)
    for r in range(4):
        for s in range(2):
            base = (2 * r + s) * 104
            sums[r, :, 256 * s : 256 * s + 256] = (
                got[r, :, 256 * s : 256 * s + 256] + f[base : base + 104, 0:256]
            )
        sums[r, :, 512:640] = got[r, :, 512:640] + f[2 * r * 104 : 2 * r * 104 + 104, 256:384] + pltpu.roll(
            f[(2 * r + 1) * 104 : (2 * r + 2) * 104, 256:384], 64, 1
        )
    for i in range(10):
        for pair in range(2):
            pieces = []
            for r in (2 * pair, 2 * pair + 1):
                for s in range(2):
                    if i < 8:
                        tile = 2 * s + i // 4
                        now = i % 4
                    else:
                        tile = 4
                        now = 2 * s + i - 8
                    pieces.append((sums[r, :, 128 * tile : 128 * tile + 128], now))
            ypos[i, :, 128 * pair : 128 * pair + 128] = place(pieces, 104)
    pnew[...] = one_hot_dot(ypos[...].reshape(1040, 256), hot).reshape(10, 104, 256)
    loads[0].wait()
    for t in range(13):
        w = pnew[:, 8 * t : 8 * t + 8, :].reshape(80, 256)
        big[t] += left_dot(x0t_ref[...], w).reshape(20, 8, 256)
    late.wait()
    for load in loads[1:]:
        load.wait()
    live = lax.broadcasted_iota(jnp.int32, (4, 104, 256), 2) < count_ref[0]
    stores = []
    for n in range(10):
        z = []
        for i2 in range(2):
            w = big[:, 2 * n + i2].reshape(416, 256)
            z.append(jnp.where(live, left_dot(yzt_ref[i2], w).reshape(4, 104, 256), 0.0))
        ob[n, :, 0:96, :] = z[0][:, 0:96]
        ob[n, :, 96:104, :] = z[0][:, 96:104] + z[1][:, 0:8]
        ob[n, :, 104:200, :] = z[1][:, 8:104]
        store = pltpu.make_async_copy(ob.at[n], window(o_ref, n), osem.at[n])
        store.start()
        stores.append(store)
    for store in stores:
        store.wait()


def final_call(count, slabs, blocks, route, z, tops):
    T = tables()
    return pl.pallas_call(
        final_kernel,
        in_specs=[SMEM, VMEM] + [ANY] * 7 + [VMEM],
        out_specs=[ANY, VMEM],
        out_shape=[
            jax.ShapeDtypeStruct((2, 4, 5, 200, 256), F32),
            jax.ShapeDtypeStruct((8, 1000), F32),
        ],
        scratch_shapes=[
            pltpu.VMEM((32, 40, 128), F32),
            pltpu.VMEM((4, 104, 640), F32),
            pltpu.VMEM((208, 384), BF16),
            pltpu.VMEM((2, 384, 640), BF16),
            pltpu.VMEM((160, 240), BF16),
            pltpu.VMEM((2, 416, 1248), BF16),
            pltpu.SemaphoreType.DMA((7,)),
            pltpu.VMEM((4, 104, 640), F32),
            pltpu.VMEM((10, 104, 256), F32),
            pltpu.VMEM((10, 104, 256), F32),
            pltpu.VMEM((52, 20, 8, 256), F32),
            pltpu.VMEM((10, 4, 200, 256), F32),
            pltpu.SemaphoreType.DMA((4,)),
            pltpu.SemaphoreType.DMA((10,)),
        ],
        compiler_params=vmem(60),
        name="final",
    )(count, route, slabs, blocks, T["up"], T["rx"], T["x0T"], T["yzT"], z, tops)


def shards(fine_coeffs, set_counts, route_first, route_top, level_gain):
    route = route_first.reshape(1, 256)
    x5 = fine_coeffs.reshape(2, 4, 5, 200, 256)
    z, blocks = finest_call(x5, set_counts, route, level_gain)
    new, tops, back = core_call(blocks, route_top.reshape(1, 32), level_gain)
    out, coarse = final_call(set_counts, new, back, route, z, tops)
    return (out.reshape(8000, 256), coarse.T)


def solution(mesh):
    placed = (
        P(None, ("leaf", "rep")),
        P(("leaf", "rep")),
        P(("leaf", "rep")),
        P(("leaf", "rep")),
        P(),
    )
    return jax.shard_map(
        shards,
        mesh=mesh,
        in_specs=placed,
        out_specs=(P(None, ("leaf", "rep")), P(None, ("leaf", "rep"))),
        check_vma=False,
    )
```
